32 devices in a mesh: group: 2 (over y), freq: 4 (over z), shot: 2 (over x), half: 2 (over core).
Axes of the slice: x: 2, y: 2, z: 4, core: 2. Of those that a mesh axis runs over, the one named last changes fastest.
Arguments:
- records: bfloat16 [8, 64, 128, 512], P(('group', 'shot'), 'half', 'freq'), parts along dimension 0, may hold values from -6 to 6
- source_pattern: bfloat16 [8, 64, 128], P(('group', 'shot'), 'half'), parts along dimension 0, may hold values from -6 to 6
- wavelet: float32 [256, 2], replicated, may hold values from -6 to 6
- filters: bfloat16 [2, 2, 13, 13, 256], replicated, may hold values from -0.3125 to 0.3125
- vel_table: float32 [64], replicated, may hold values from 0 to 1
- vel_index: int32 [4, 64, 128], P('group', 'half'), parts along dimension 0, may hold values from 0 to 63
- freq_plan: int32 [4, 6], replicated, may hold values from 0 to 255, as said below
- counts: int32 [4], replicated, may hold values from 1 to 6, 12 in all
Outputs:
- image: float32 [2, 32, 4, 128], P('half', 'freq', 'group'), parts along dimension 2
The draws below stay inside these ranges and needn't reach their ends.
There are 2 independent parts, one for each index of `group`. The reference program is written for one: setup_inputs(seed, part) draws one part's arguments, and reference() takes and returns one part's arrays. A program takes and returns all parts, laid end to end along the dimension named above; an argument that names none is the same for every part. Nothing has to cross between parts.
Inputs may be any that keep to these rules, and one draw needn't show every extreme that they name: `freq_plan`: entries are distinct bins; 0 and 255 both appear. `counts`: they sum to 12; the largest is exactly 6.
All inputs are finite; a program needn't handle non-finite values.
Results may differ from the reference program's by a relative error of at most 0.0069.
Values may be sent and summed in bfloat16 or wider, within the bound.
No kernel may reach another device: no remote copies, remote signals or barrier semaphores. Data moves between devices by JAX's collectives and lax.ppermute only.
A program may use at most 64 MiB of HBM per device.

```python
import math
import jax
import jax.numpy as jnp
import numpy as np
from jax import lax

ROWS_DEV = 32
NX = 128
NT = 512
DEPTH = 2
TAPS = 13
NREF = 2
NV = 64
NBIN = 256
FCAP = 6
NF = 12
NY = 64
SHOTS = 4
N_FREQ = 4
N_HALF = 2


def draw_freq_plan(key, part):
    slot_total = N_FREQ * FCAP
    order = jax.random.permutation(key, slot_total)
    bin_ids = order * (NBIN - 1) // (slot_total - 1)
    return bin_ids.reshape(N_FREQ, FCAP).astype(jnp.int32)


def touch_ends(result, rng, low, top_value):
    shape = result.shape
    index_at = [jax.random.randint(jax.random.fold_in(rng, axis), (), 0, shape[axis]) for axis in range(len(shape))]
    result = result.at[tuple(index_at)].set(low)
    longest = shape.index(max(shape))
    index_at[longest] = (index_at[longest] + 1) % shape[longest]
    return result.at[tuple(index_at)].set(top_value)


def shard_levels(stream_key, dims, shards, low, top_value):
    def one(dim, blocks):
        heights = jax.random.uniform(jax.random.fold_in(jax.random.fold_in(stream_key, 6), dim), (blocks,), jnp.float32, low / len(shards), top_value / len(shards))
        return jnp.repeat(jnp.exp(heights), dims[dim] // blocks).reshape((-1,) + (1,) * (len(dims) - dim - 1))

    factor_of = one(*shards[0])
    for cut in shards[1:]:
        factor_of = factor_of * one(*cut)
    return factor_of


def profile(amount, total, bound, slope):
    portions = [(1 << 20) // math.isqrt(standing ** slope) + 1 for standing in range(2, amount + 1)]
    surplus, given = total - bound - (amount - 1), [1] * (amount - 1)
    while surplus > 0:
        candidates = [i for i in range(amount - 1) if given[i] < bound]
        pool, left = sum([portions[i] for i in candidates]), surplus
        for i in candidates:
            more = min(bound - given[i], max(1, left * portions[i] // pool), surplus)
            given[i] = given[i] + more
            surplus = surplus - more
    return np.array([bound] + given)


def ragged(key, amount, total, most, skew):
    if amount == 2:
        one = jax.random.randint(key, (), max(1, total - most), min(most, total - 1) + 1)
        return jnp.stack([one, total - one])
    lengths = jnp.asarray(profile(amount, total, most, skew), jnp.int32)
    pairs = (amount - 1) // 2
    donor, taker = lengths[1:1 + 2 * pairs:2], lengths[2:2 + 2 * pairs:2]
    slack = jnp.minimum(donor - 1, most - taker)
    shifted = jax.random.randint(jax.random.fold_in(key, 1), (pairs,), 0, 1 << 20) % (slack + 1)
    lengths = lengths.at[1:1 + 2 * pairs:2].set(donor - shifted).at[2:2 + 2 * pairs:2].set(taker + shifted)
    return lengths[jax.random.permutation(jax.random.fold_in(key, 2), amount)]


def normal_values(stream_key, dims, deviation, most, split=(), kind=jnp.bfloat16):
    result = deviation * jax.random.normal(stream_key, dims, jnp.float32)
    if split:
        result = result * shard_levels(stream_key, dims, split, -0.22, 0.18)
    return jnp.clip(result, -most, most).astype(kind)


def setup_inputs(seed: int = 0, part: int = 0) -> dict:
    arg_keys = jax.random.split(jax.random.key(seed), 9)
    own_keys = jax.random.split(jax.random.fold_in(arg_keys[8], part), 9)
    return {
        "records": normal_values(own_keys[0], (SHOTS, NY, NX, NT), 1.0, 6.0, ((0, 2), (1, 2), (2, 4))),
        "source_pattern": normal_values(own_keys[1], (SHOTS, NY, NX), 1.0, 6.0, ((0, 2), (1, 2))),
        "wavelet": normal_values(arg_keys[2], (NBIN, 2), 1.0, 6.0, (), jnp.float32),
        "filters": normal_values(arg_keys[3], (NREF, 2, TAPS, TAPS, NBIN), (2 * TAPS * TAPS) ** -0.5, 0.3125),
        "vel_table": jnp.clip(jax.random.uniform(arg_keys[4], (NV,), jnp.float32, 0.0, 1.0), 0.0, 1.0),
        "vel_index": touch_ends(jax.random.randint(own_keys[5], (DEPTH, NY, NX), 0, NV), jax.random.fold_in(own_keys[5], 1), 0, NV - 1).astype(jnp.int32),
        "freq_plan": draw_freq_plan(jax.random.fold_in(arg_keys[8], 71), part),
        "counts": ragged(arg_keys[7], N_FREQ, NF, FCAP, 2).astype(jnp.int32),
    }


def live_bins(freq_plan, counts):
    run_ends = jnp.cumsum(counts).astype(jnp.int32)
    starts = run_ends - counts
    global_slot = jnp.arange(NF, dtype=jnp.int32)
    holder = lax.optimization_barrier(jnp.sum((run_ends[None, :] <= global_slot[:, None]).astype(jnp.int32), axis=1))
    offset = global_slot - starts[holder]
    return freq_plan[holder, offset]

def dft_columns(bin_ids):
    sample = jnp.arange(NT, dtype=jnp.int32)
    phases = bin_ids[None, :] * sample[:, None] % NT
    angles = phases.astype(jnp.float32) * (2.0 * math.pi / NT)
    dft_scale = 1.0 / math.sqrt(NT)
    return jnp.stack([jnp.cos(angles) * dft_scale, -jnp.sin(angles) * dft_scale], axis=-1).astype(jnp.bfloat16)

def extrapolate(fields, filter_taps, blends):
    half_taps = TAPS // 2
    row_count = fields.shape[-2]
    col_count = fields.shape[-1]
    padded = jnp.pad(fields.astype(jnp.float32), ((0, 0), (0, 0), (0, 0), (half_taps, half_taps), (half_taps, half_taps)))
    real_acc = jnp.zeros((NREF,) + fields.shape[:2] + (row_count, col_count), jnp.float32)
    imag_acc = jnp.zeros((NREF,) + fields.shape[:2] + (row_count, col_count), jnp.float32)
    for row_shift in range(TAPS):
        for col_shift in range(TAPS):
            window = padded[:, :, :, row_shift:row_shift + row_count, col_shift:col_shift + col_count]
            tap_real = filter_taps[:, 0, row_shift, col_shift][:, None, None, None, None]
            tap_imag = filter_taps[:, 1, row_shift, col_shift][:, None, None, None, None]
            real_acc = real_acc + tap_real * window[None, :, :, 0] - tap_imag * window[None, :, :, 1]
            imag_acc = imag_acc + tap_real * window[None, :, :, 1] + tap_imag * window[None, :, :, 0]
    out_real = real_acc[0] + blends * (real_acc[1] - real_acc[0])
    out_imag = imag_acc[0] + blends * (imag_acc[1] - imag_acc[0])
    return jnp.stack([out_real, out_imag], axis=2).astype(jnp.bfloat16)

def reference(records, source_pattern, wavelet, filters, vel_table, vel_index, freq_plan, counts):
    bin_ids = live_bins(freq_plan, counts)
    dft_table = dft_columns(bin_ids)
    spectra = jnp.dot(records.reshape(-1, NT), dft_table.reshape(NT, NF * 2), preferred_element_type=jnp.float32)
    spectra = spectra.reshape(SHOTS, NY, NX, NF, 2).transpose(3, 0, 4, 1, 2)
    blends = vel_table[vel_index]
    pattern = source_pattern.astype(jnp.float32)

    def migrate(inputs):
        own_spectra, bin_id = inputs
        filter_taps = filters[..., bin_id].astype(jnp.float32)
        wavelet_bin = wavelet[bin_id]
        source = (pattern[:, None] * wavelet_bin[None, :, None, None]).astype(jnp.bfloat16)
        receiver = own_spectra.astype(jnp.bfloat16)
        fields = jnp.stack([source, receiver])
        images = []
        for depth_step in range(DEPTH):
            fields = extrapolate(fields, filter_taps, blends[depth_step])
            as_float = fields.astype(jnp.float32)
            images.append(lax.optimization_barrier(jnp.sum(as_float[0, :, 0] * as_float[1, :, 0] + as_float[0, :, 1] * as_float[1, :, 1], axis=0)))
        return jnp.stack(images)
    per_bin = lax.map(migrate, (spectra, bin_ids))
    image_scale = 1.0 / math.sqrt(NF * SHOTS)
    summed = lax.optimization_barrier(jnp.sum(per_bin, axis=0)) * image_scale
    return summed.transpose(1, 0, 2).reshape(N_HALF, ROWS_DEV, DEPTH, NX)
```

```python
import functools
import math

import jax
import jax.numpy as jnp
from jax import lax
from jax.experimental import pallas as pl
from jax.experimental.pallas import tpu as pltpu
from jax.sharding import PartitionSpec as P

FPD = 3
LANES = 128
SUB = 8
ROW_PAD = 8
VMEM_BYTES = 40 * 1024 * 1024
BF16 = jnp.bfloat16
F32 = jnp.float32


def list_bins(plan_ref, counts_ref, bins_ref):
    groups, cap = plan_ref.shape
    start = jnp.int32(0)
    for holder in range(groups):
        for slot in range(cap):
            bins_ref[start + slot] = plan_ref[holder, slot]
        start = start + counts_ref[holder]


def lane_iota(shape):
    return lax.broadcasted_iota(jnp.int32, shape, len(shape) - 1)


def row_iota(shape):
    return lax.broadcasted_iota(jnp.int32, shape, 0)


def dft_rows(bins_ref, group, nt):
    shape = (SUB, nt)
    row = row_iota(shape)
    bin_id = jnp.zeros(shape, jnp.int32)
    for slot in range(FPD):
        bin_id = jnp.where(row // 2 == slot, bins_ref[group * FPD + slot], bin_id)
    phase = lax.rem(bin_id * lane_iota(shape), jnp.int32(nt)) if nt & (nt - 1) else (bin_id * lane_iota(shape)) & (nt - 1)
    quarter = nt // 4
    turn = (phase + quarter // 2) // quarter
    angle = (phase - turn * quarter).astype(F32) * (2.0 * math.pi / nt)
    turn = (turn + (row & 1)) & 3
    sq = angle * angle
    cos = 1.0 + sq * (-1.0 / 2 + sq * (1.0 / 24 + sq * (-1.0 / 720 + sq * (1.0 / 40320))))
    sin = angle * (1.0 + sq * (-1.0 / 6 + sq * (1.0 / 120 + sq * (-1.0 / 5040 + sq * (1.0 / 362880)))))
    value = jnp.where((turn & 1) == 1, sin, cos)
    value = jnp.where(((turn + 1) & 2) == 2, -value, value)
    return (value * (1.0 / math.sqrt(nt))).astype(BF16)


def spectra_kernel(groups, plan_ref, counts_ref, rec_ref, out_ref, bins_ref, dft_ref):
    @pl.when(pl.program_id(0) == 0)
    def _():
        list_bins(plan_ref, counts_ref, bins_ref)
        for group in range(groups):
            dft_ref[group * SUB : (group + 1) * SUB] = dft_rows(bins_ref, group, rec_ref.shape[-1]).astype(F32)

    out = lax.dot_general(
        dft_ref[...].astype(BF16), rec_ref[0], (((1,), (1,)), ((), ())), preferred_element_type=F32
    )
    out_ref[0] = out.astype(BF16)


def send_kernel(
    groups, xw, plan_ref, counts_ref, vi_ref, sp_ref, rec_ref, out_ref, bins_ref, dft_ref, extra_ref, block_ref, tmp_ref
):
    shot = pl.program_id(0)
    depth, rows, _ = vi_ref.shape
    shots = sp_ref.shape[0]
    folds = LANES // xw
    block = out_ref.shape[2]

    @pl.when(shot == 0)
    def _():
        list_bins(plan_ref, counts_ref, bins_ref)
        for group in range(groups):
            dft_ref[group * SUB : (group + 1) * SUB] = dft_rows(bins_ref, group, rec_ref.shape[-1]).astype(F32)
        me = lax.axis_index("freq")
        lane = lane_iota((SUB, LANES))
        for item in range(depth + shots):
            if item < depth:
                block_ref[...] = vi_ref[item].astype(F32)
            else:
                block_ref[...] = sp_ref[item - depth].astype(F32)
            kept = jnp.zeros((SUB, LANES), F32)
            for low in range(folds):
                piece = block_ref[pl.ds(low, SUB, stride=folds), :]
                shift = lax.rem((low + folds - me) * xw, jnp.int32(LANES))
                kept = jnp.where(lane // xw == low, pltpu.roll(piece, shift, 1), kept)
            extra_ref[item * SUB : (item + 1) * SUB] = kept

    out = lax.dot_general(
        dft_ref[...].astype(BF16), rec_ref[0], (((1,), (1,)), ((), ())), preferred_element_type=F32
    )
    first = 2 * FPD * SUB
    for group in range(groups):
        base = group * block
        for high in range(SUB):
            tmp_ref[pl.ds(base + high, SUB, stride=SUB), :] = out[
                group * SUB : (group + 1) * SUB, high * LANES : (high + 1) * LANES
            ]
        tmp_ref[base + first : base + first + depth * SUB] = extra_ref[: depth * SUB]
        source = extra_ref[pl.ds(pl.multiple_of((depth + shot) * SUB, SUB), SUB), :]
        tmp_ref[base + first + depth * SUB : base + first + (depth + 1) * SUB] = source
        used = first + (depth + 1) * SUB
        if used < block:
            tmp_ref[base + used : base + block] = jnp.zeros((block - used, LANES), F32)
        out_ref[group, 0] = tmp_ref[base : base + block].astype(BF16)


def band_kernel(taps, ny, plan_ref, counts_ref, filt_ref, out_ref, bins_ref, picked_ref):
    plane = pl.program_id(0)

    @pl.when(plane == 0)
    def _():
        list_bins(plan_ref, counts_ref, bins_ref)

    nbin = filt_ref.shape[1]
    reach = taps // 2
    nref = filt_ref.shape[0] // (2 * taps * taps)
    bin_id = bins_ref[lax.axis_index("freq") * FPD + plane]
    hot = jnp.where(row_iota((nbin, LANES)) == bin_id, 1.0, 0.0).astype(BF16)
    picked_ref[...] = jnp.dot(filt_ref[...], hot, preferred_element_type=F32)
    width = 2 * ny
    lane = lane_iota((taps, LANES))
    full_lane = lane_iota((ny, LANES))
    keep = jnp.abs((full_lane & (ny - 1)) - row_iota((ny, LANES))) <= reach
    sign = jnp.where((lane < ny // 2) | (lane >= ny + ny // 2), -1.0, 1.0)
    for ref in range(nref):
        base = jnp.zeros((taps, LANES), F32)
        for part in range(2):
            for tap in range(taps):
                value = picked_ref[pl.ds((ref * taps + tap) * taps * 2 + part, taps, stride=2), :]
                base = jnp.where(lane == (part * ny + reach - tap) % width, value, base)
        turned = pltpu.roll(base, ny, 1) * sign
        for col_tap in range(taps):
            for part, rows in enumerate((base, turned)):
                spread = jnp.broadcast_to(rows[col_tap : col_tap + 1], (ny, LANES))
                band = pltpu.roll(spread, 0, 1, stride=1, stride_axis=0)
                band = jnp.where(keep, band, 0.0).astype(BF16)
                at = col_tap * width + part * ny
                out_ref[0, at : at + ny, ref * width : (ref + 1) * width] = band


def migrate_kernel(
    dims, plan_ref, counts_ref, wav_ref, table_ref, recv_ref, band_hbm, out_ref,
    bins_ref, grid_ref, field_ref, lhs_ref, band_ref, tab_ref, blend_ref, image_ref, sems,
):
    groups, halves, copies, xw, taps, depth, scale, folded = dims
    for plane in range(FPD):
        pltpu.make_async_copy(band_hbm.at[plane], band_ref.at[plane], sems.at[plane]).start()
    list_bins(plan_ref, counts_ref, bins_ref)
    nx = LANES
    ny = grid_ref.shape[0] // (2 * FPD + depth + 1)
    width = 2 * ny
    reach = taps // 2
    lane = lane_iota((SUB, LANES))
    if folded:
        folds = LANES // xw
        half_rows = ny // halves
        for half in range(halves):
            blocks = [recv_ref[group * halves + half].astype(F32) for group in range(groups)]
            for item in range(2 * FPD + depth + 1):
                for low in range(folds):
                    kept = None
                    for group in range(groups):
                        piece = blocks[group][item * SUB : (item + 1) * SUB]
                        shift = ((group - low) * xw) % LANES
                        if shift:
                            piece = pltpu.roll(piece, shift, 1)
                        kept = piece if kept is None else jnp.where(lane // xw == group, piece, kept)
                    grid_ref[pl.ds(item * ny + half * half_rows + low, SUB, stride=folds), :] = kept
    else:
        grid_ref[...] = recv_ref[...].astype(F32)
    tab_ref[:, : table_ref.shape[1]] = jnp.broadcast_to(table_ref[...], (SUB, table_ref.shape[1]))
    at = 2 * FPD * ny
    for step in range(depth):
        for part in range(2):
            for row in range(0, ny, SUB):
                index = grid_ref[at + row : at + row + SUB].astype(jnp.int32)
                blend_ref[step, part * ny + row : part * ny + row + SUB] = jnp.take_along_axis(
                    tab_ref[...], index, axis=1
                )
        at += ny
        blend_ref[step] = blend_ref[step].T
    pattern = grid_ref[at : at + ny]
    pattern = jnp.concatenate([pattern, pattern], axis=0).T
    full_lane = lane_iota((nx, width))
    first = lax.axis_index("freq") * FPD
    for plane in range(FPD):
        bin_id = bins_ref[first + plane]
        wave = jnp.where(full_lane < ny, wav_ref[0, bin_id], wav_ref[1, bin_id])
        field_ref[plane, 0, ROW_PAD : ROW_PAD + nx] = (pattern * wave).astype(BF16).astype(F32)
        field_ref[plane, 1, ROW_PAD : ROW_PAD + nx] = grid_ref[plane * width : (plane + 1) * width].T
        for field in range(2):
            field_ref[plane, field, :ROW_PAD] = jnp.zeros((ROW_PAD, width), F32)
            field_ref[plane, field, ROW_PAD + nx :] = jnp.zeros((ROW_PAD, width), F32)
    for step in range(depth):
        blend = blend_ref[step]
        total = None
        for plane in range(FPD):
            for field in range(2):
                for tap in range(taps):
                    rows = field_ref[plane, field, pl.ds(ROW_PAD - reach + tap, nx), :]
                    lhs_ref[plane, field * nx : (field + 1) * nx, tap * width : (tap + 1) * width] = rows.astype(BF16)
            if step == 0:
                pltpu.make_async_copy(band_hbm.at[plane], band_ref.at[plane], sems.at[plane]).wait()
            both = jnp.dot(lhs_ref[plane], band_ref[plane], preferred_element_type=F32)
            term = None
            for field in range(2):
                low = both[field * nx : (field + 1) * nx, :width]
                high = both[field * nx : (field + 1) * nx, width:]
                new = (low + blend * (high - low)).astype(BF16).astype(F32)
                if step + 1 < depth:
                    field_ref[plane, field, ROW_PAD : ROW_PAD + nx] = new
                term = new if term is None else term * new
            total = term if total is None else total + term
        turned = total.T
        image_ref[pl.ds(step, ny, stride=depth), :] = (turned[:ny] + turned[ny:]) * scale
    share = ny // (groups * halves) * depth
    for group in range(groups):
        for half in range(halves):
            start = (half * groups + group) * share
            piece = image_ref[start : start + share]
            for copy in range(copies):
                out_ref[(group * halves + half) * copies + copy] = piece


def smem():
    return pl.BlockSpec(memory_space=pltpu.SMEM)


def vmem():
    return pl.BlockSpec(memory_space=pltpu.VMEM)


def body(records, source_pattern, wavelet, filters, vel_table, vel_index, freq_plan, counts):
    groups = lax.axis_size("freq")
    halves = lax.axis_size("half")
    copies = lax.axis_size("shot")
    shots, rows, xw, nt = records.shape
    depth = vel_index.shape[0]
    nref, _, taps, _, nbin = filters.shape
    nx = xw * groups
    ny = rows * halves
    items = 2 * FPD + depth + 1
    cap = freq_plan.shape[1]
    folded = LANES % xw == 0 and rows * xw == SUB * LANES
    bins = pltpu.SMEM((groups * FPD + cap,), jnp.int32)
    params = functools.partial(pltpu.CompilerParams, vmem_limit_bytes=VMEM_BYTES)
    flat = records.reshape(shots, rows * xw, nt)

    if folded:
        block = (items * SUB + 15) // 16 * 16
        send = pl.pallas_call(
            functools.partial(send_kernel, groups, xw),
            out_shape=jax.ShapeDtypeStruct((groups, shots, block, LANES), BF16),
            grid=(shots,),
            in_specs=[
                smem(), smem(),
                pl.BlockSpec(vel_index.shape, lambda s: (0, 0, 0)),
                pl.BlockSpec(source_pattern.shape, lambda s: (0, 0, 0)),
                pl.BlockSpec((1, rows * xw, nt), lambda s: (s, 0, 0)),
            ],
            out_specs=pl.BlockSpec((groups, 1, block, LANES), lambda s: (0, s, 0, 0)),
            scratch_shapes=[
                bins,
                pltpu.VMEM((groups * SUB, nt), F32),
                pltpu.VMEM(((depth + shots) * SUB, LANES), F32),
                pltpu.VMEM((rows, LANES), F32),
                pltpu.VMEM((groups * block, LANES), F32),
            ],
            compiler_params=params(),
            name="send_blocks",
        )(freq_plan, counts, vel_index, source_pattern, flat)
        send = send.reshape(groups * halves, block, LANES)
        recv = lax.all_to_all(send, ("freq", "half"), 0, 0, tiled=True)
    else:
        spectra = pl.pallas_call(
            functools.partial(spectra_kernel, groups),
            out_shape=jax.ShapeDtypeStruct((shots, groups * SUB, rows * xw), BF16),
            grid=(shots,),
            in_specs=[smem(), smem(), pl.BlockSpec((1, rows * xw, nt), lambda s: (s, 0, 0))],
            out_specs=pl.BlockSpec((1, groups * SUB, rows * xw), lambda s: (s, 0, 0)),
            scratch_shapes=[bins, pltpu.VMEM((groups * SUB, nt), F32)],
            compiler_params=params(),
            name="spectra",
        )(freq_plan, counts, flat)
        spectra = spectra.reshape(shots, groups, SUB, rows, xw)[:, :, : 2 * FPD].swapaxes(0, 1)
        start = lax.axis_index("freq") * xw
        classes = lax.dynamic_slice_in_dim(vel_index, start, xw, 2).astype(BF16)
        classes = jnp.broadcast_to(classes, (groups, shots) + classes.shape)
        pattern = lax.dynamic_slice_in_dim(source_pattern, start, xw, 2)[:, None]
        pattern = jnp.broadcast_to(pattern, (groups,) + pattern.shape)
        send = jnp.concatenate([spectra, classes, pattern], axis=2).reshape(groups * halves, items, rows * xw)
        recv = lax.all_to_all(send, ("freq", "half"), 0, 0, tiled=True)
        recv = recv.reshape(groups, halves, items, rows, xw).transpose(2, 1, 3, 0, 4).reshape(items * ny, nx)

    table = filters.transpose(0, 2, 3, 1, 4).reshape(nref * taps * taps * 2, nbin)
    band_shape = (taps * 2 * ny, nref * 2 * ny)
    band = pl.pallas_call(
        functools.partial(band_kernel, taps, ny),
        out_shape=jax.ShapeDtypeStruct((FPD,) + band_shape, BF16),
        grid=(FPD,),
        in_specs=[smem(), smem(), pl.BlockSpec(table.shape, lambda s: (0, 0))],
        out_specs=pl.BlockSpec((1,) + band_shape, lambda s: (s, 0, 0)),
        scratch_shapes=[bins, pltpu.VMEM((table.shape[0], LANES), F32)],
        compiler_params=params(),
        name="bands",
    )(freq_plan, counts, table)

    scale = 1.0 / math.sqrt(FPD * groups * shots * copies)
    dims = (groups, halves, copies, xw, taps, depth, scale, folded)
    share = ny // (groups * halves)
    terms = pl.pallas_call(
        functools.partial(migrate_kernel, dims),
        out_shape=jax.ShapeDtypeStruct((groups * halves * copies, share * depth, nx), F32),
        in_specs=[smem(), smem(), smem(), vmem(), vmem(), pl.BlockSpec(memory_space=pl.ANY)],
        out_specs=vmem(),
        scratch_shapes=[
            bins,
            pltpu.VMEM((items * ny, nx), F32),
            pltpu.VMEM((FPD, 2, nx + 2 * ROW_PAD, 2 * ny), F32),
            pltpu.VMEM((FPD, 2 * nx, taps * 2 * ny), BF16),
            pltpu.VMEM((FPD,) + band_shape, BF16),
            pltpu.VMEM((SUB, LANES), F32),
            pltpu.VMEM((depth, 2 * ny, nx), F32),
            pltpu.VMEM((ny * depth, nx), F32),
            pltpu.SemaphoreType.DMA((FPD,)),
        ],
        compiler_params=params(),
        name="migrate",
    )(freq_plan, counts, wavelet.T, vel_table[None], recv, band)
    terms = lax.all_to_all(terms, ("freq", "half", "shot"), 0, 0, tiled=True)
    return jnp.sum(terms, axis=0).reshape(1, share, depth, nx)


def solution(mesh):
    return jax.shard_map(
        body,
        mesh=mesh,
        in_specs=(
            P(("group", "shot"), "half", "freq", None),
            P(("group", "shot"), "half", None),
            P(),
            P(),
            P(),
            P("group", "half", None),
            P(),
            P(),
        ),
        out_specs=P("half", "freq", "group", None),
        check_vma=False,
    )
```

```python
import functools
import math

import jax
import jax.numpy as jnp
from jax import lax
from jax.experimental import pallas as pl
from jax.experimental.pallas import tpu as pltpu
from jax.sharding import PartitionSpec as P

FPD = 3
LANES = 128
SUB = 8
ROW_PAD = 8
CHUNKS = 2
VMEM_BYTES = 40 * 1024 * 1024
BF16 = jnp.bfloat16
F32 = jnp.float32


def list_bins(plan_ref, counts_ref, bins_ref):
    groups, cap = plan_ref.shape
    start = jnp.int32(0)
    for holder in range(groups):
        for slot in range(cap):
            bins_ref[start + slot] = plan_ref[holder, slot]
        start = start + counts_ref[holder]


def lane_iota(shape):
    return lax.broadcasted_iota(jnp.int32, shape, len(shape) - 1)


def row_iota(shape):
    return lax.broadcasted_iota(jnp.int32, shape, 0)


def dft_rows(bins_ref, group, nt):
    shape = (SUB, nt)
    row = row_iota(shape)
    bin_id = jnp.zeros(shape, jnp.int32)
    for slot in range(FPD):
        bin_id = jnp.where(row // 2 == slot, bins_ref[group * FPD + slot], bin_id)
    phase = bin_id * lane_iota(shape)
    phase = lax.rem(phase, jnp.int32(nt)) if nt & (nt - 1) else phase & (nt - 1)
    quarter = nt // 4
    turn = (phase + quarter // 2) // quarter
    angle = (phase - turn * quarter).astype(F32) * (2.0 * math.pi / nt)
    turn = (turn + (row & 1)) & 3
    sq = angle * angle
    cos = 1.0 + sq * (-1.0 / 2 + sq * (1.0 / 24 + sq * (-1.0 / 720 + sq * (1.0 / 40320))))
    sin = angle * (1.0 + sq * (-1.0 / 6 + sq * (1.0 / 120 + sq * (-1.0 / 5040 + sq * (1.0 / 362880)))))
    value = jnp.where((turn & 1) == 1, sin, cos)
    value = jnp.where(((turn + 1) & 2) == 2, -value, value)
    return value * (1.0 / math.sqrt(nt))


def transform(dft, block):
    return lax.dot_general(dft, block, (((1,), (1,)), ((), ())), preferred_element_type=F32)


def send_kernel(
    groups, folded, plan_hbm, counts_hbm, wav_hbm, filt_hbm, rec_hbm, out_ref, own_ref, wave_ref, filt_ref,
    plan_ref, counts_ref, wav_ref, bins_ref, dft_ref, rec_ref, tmp_ref, small_sems, sems,
):
    shots, cells, nt = rec_hbm.shape
    part = cells // CHUNKS
    small = [
        pltpu.make_async_copy(plan_hbm, plan_ref, small_sems.at[0]),
        pltpu.make_async_copy(counts_hbm, counts_ref, small_sems.at[1]),
        pltpu.make_async_copy(wav_hbm, wav_ref, small_sems.at[2]),
    ]
    for copy in small:
        copy.start()
    copies = []
    for shot in range(shots):
        for chunk in range(CHUNKS):
            rows = pl.ds(chunk * part, part)
            copy = pltpu.make_async_copy(
                rec_hbm.at[shot, rows], rec_ref.at[shot, rows], sems.at[shot * CHUNKS + chunk]
            )
            copy.start()
            copies.append(copy)
    filters = pltpu.make_async_copy(filt_hbm, filt_ref, small_sems.at[3])
    filters.start()
    for copy in small:
        copy.wait()
    list_bins(plan_ref, counts_ref, bins_ref)
    for group in range(groups):
        dft_ref[group * SUB : (group + 1) * SUB] = dft_rows(bins_ref, group, nt)
    dft = dft_ref[...].astype(BF16)
    first = lax.axis_index("freq") * FPD
    lane = lane_iota((1, LANES))
    for plane in range(FPD):
        bin_id = bins_ref[first + plane]
        own_ref[plane : plane + 1] = jnp.full((1, LANES), bin_id, jnp.int32)
        wave_ref[plane : plane + 1] = jnp.where(lane < LANES // 2, wav_ref[0, bin_id], wav_ref[1, bin_id])
    for shot in range(shots):
        for chunk in range(CHUNKS):
            copies[shot * CHUNKS + chunk].wait()
            out = transform(dft, rec_ref[shot, chunk * part : (chunk + 1) * part])
            if not folded:
                out_ref[shot, :, chunk * part : (chunk + 1) * part] = out.astype(BF16)
                continue
            highs = part // LANES
            for group in range(groups):
                base = (group * shots + shot) * SUB * SUB + chunk * highs
                for high in range(highs):
                    tmp_ref[pl.ds(base + high, SUB, stride=SUB), :] = out[
                        group * SUB : (group + 1) * SUB, high * LANES : (high + 1) * LANES
                    ]
        if folded:
            for group in range(groups):
                base = (group * shots + shot) * SUB * SUB
                out_ref[group, shot] = tmp_ref[base : base + 2 * FPD * SUB].astype(BF16)
    filters.wait()


def make_bands(taps, nref, ny, picked_ref, band_ref):
    reach = taps // 2
    width = 2 * ny
    lane = lane_iota((taps, width))
    full_lane = lane_iota((ny, width))
    keep = jnp.abs((full_lane & (ny - 1)) - row_iota((ny, width))) <= reach
    sign = jnp.where((lane < ny // 2) | (lane >= ny + ny // 2), -1.0, 1.0)
    for ref in range(nref):
        base = jnp.zeros((taps, width), F32)
        for part in range(2):
            for tap in range(taps):
                value = picked_ref[pl.ds((ref * taps + tap) * taps * 2 + part, taps, stride=2), :]
                base = jnp.where(lane == (part * ny + reach - tap) % width, value, base)
        turned = pltpu.roll(base, ny, 1) * sign
        for col_tap in range(taps):
            for part, rows in enumerate((base, turned)):
                spread = jnp.broadcast_to(rows[col_tap : col_tap + 1], (ny, width))
                band = pltpu.roll(spread, 0, 1, stride=1, stride_axis=0)
                band = jnp.where(keep, band, 0.0).astype(BF16)
                at = col_tap * width + part * ny
                band_ref[at : at + ny, ref * width : (ref + 1) * width] = band


def set_field(field_ref, value):
    rows, width = value.shape
    field_ref[:ROW_PAD] = jnp.zeros((ROW_PAD, width), F32)
    field_ref[ROW_PAD : ROW_PAD + rows] = value
    field_ref[ROW_PAD + rows :] = jnp.zeros((ROW_PAD, width), F32)


def advance(taps, field_ref, lhs_ref, band_ref, blend):
    rows, width = blend.shape
    for tap in range(taps):
        piece = field_ref[pl.ds(ROW_PAD - taps // 2 + tap, rows), :]
        lhs_ref[:, tap * width : (tap + 1) * width] = piece.astype(BF16)
    both = jnp.dot(lhs_ref[...], band_ref[...], preferred_element_type=F32)
    low, high = both[:, :width], both[:, width:]
    return (low + blend * (high - low)).astype(BF16).astype(F32)


def source_kernel(taps, nref, depth, halves, own_ref, wave_ref, filt_ref, table_hbm, *refs):
    class_hbm, refs = refs[:halves], refs[halves:]
    pattern_hbm, refs = refs[:halves], refs[halves:]
    band_ref, blend_ref, source_ref, class_refs, pattern_refs, table_ref, picked_ref, grid_ref, tab_ref, field_ref, lhs_ref, sems = refs
    copies = [pltpu.make_async_copy(table_hbm, table_ref, sems.at[0])]
    for turn in range(halves):
        copies.append(pltpu.make_async_copy(class_hbm[turn], class_refs.at[turn], sems.at[1 + 2 * turn]))
        copies.append(pltpu.make_async_copy(pattern_hbm[turn], pattern_refs.at[turn], sems.at[2 + 2 * turn]))
    for copy in copies:
        copy.start()
    mine = lax.axis_index("half")
    rows = class_hbm[0].shape[1]
    ny, nx = grid_ref.shape[1:]
    nbin = filt_ref.shape[1]
    for plane in range(FPD):
        hot = jnp.where(row_iota((nbin, LANES)) == own_ref[plane : plane + 1], 1.0, 0.0).astype(BF16)
        picked_ref[plane] = jnp.dot(filt_ref[...], hot, preferred_element_type=F32)
    for plane in range(FPD - 1):
        make_bands(taps, nref, ny, picked_ref.at[plane], band_ref.at[plane])
    for copy in copies:
        copy.wait()
    for turn in range(halves):
        at = pl.ds(pl.multiple_of(lax.rem(mine + turn, halves) * rows, rows), rows)
        for step in range(depth):
            grid_ref[step, at, :] = class_refs[turn, step].astype(F32)
        grid_ref[depth, at, :] = pattern_refs[turn, mine].astype(F32)
    tab_ref[:, : table_ref.shape[1]] = jnp.broadcast_to(table_ref[...], (SUB, table_ref.shape[1]))
    for step in range(depth):
        pieces = []
        for row in range(0, ny, SUB):
            index = grid_ref[step, row : row + SUB].astype(jnp.int32)
            pieces.append(jnp.take_along_axis(tab_ref[...], index, axis=1))
        blend_ref[step] = jnp.concatenate(pieces + pieces, axis=0).T
    pattern = grid_ref[depth]
    pattern = jnp.concatenate([pattern, pattern], axis=0).T
    for plane in range(FPD):
        set_field(field_ref.at[plane], (pattern * wave_ref[plane : plane + 1]).astype(BF16).astype(F32))
    make_bands(taps, nref, ny, picked_ref.at[FPD - 1], band_ref.at[FPD - 1])
    for step in range(depth):
        for plane in range(FPD):
            new = advance(taps, field_ref.at[plane], lhs_ref.at[plane], band_ref.at[plane], blend_ref[step])
            source_ref[step, plane] = new
            if step + 1 < depth:
                field_ref[plane, ROW_PAD : ROW_PAD + nx] = new


def migrate_kernel(dims, recv_ref, band_ref, blend_ref, source_ref, out_ref, grid_ref, field_ref, lhs_ref, image_ref):
    groups, halves, copies, xw, taps, scale, folded = dims
    depth, nx, width = blend_ref.shape
    ny = width // 2
    if folded:
        folds = LANES // xw
        half_rows = ny // halves
        lane = lane_iota((SUB, LANES))
        for half in range(halves):
            blocks = [recv_ref[group * halves + half].astype(F32) for group in range(groups)]
            for item in range(2 * FPD):
                for low in range(folds):
                    kept = None
                    for group in range(groups):
                        piece = blocks[group][item * SUB : (item + 1) * SUB]
                        shift = ((group - low) * xw) % LANES
                        if shift:
                            piece = pltpu.roll(piece, shift, 1)
                        kept = piece if kept is None else jnp.where(lane // xw == group, piece, kept)
                    grid_ref[pl.ds(item * ny + half * half_rows + low, SUB, stride=folds), :] = kept
    else:
        grid_ref[...] = recv_ref[...].astype(F32)
    for plane in range(FPD):
        set_field(field_ref.at[plane], grid_ref[plane * width : (plane + 1) * width].T)
    for step in range(depth):
        total = None
        for plane in range(FPD):
            new = advance(taps, field_ref.at[plane], lhs_ref.at[plane], band_ref.at[plane], blend_ref[step])
            if step + 1 < depth:
                field_ref[plane, ROW_PAD : ROW_PAD + nx] = new
            term = source_ref[step, plane] * new
            total = term if total is None else total + term
        turned = total.T
        image_ref[pl.ds(step, ny, stride=depth), :] = (turned[:ny] + turned[ny:]) * scale
    share = ny // (groups * halves) * depth
    for group in range(groups):
        for half in range(halves):
            start = (half * groups + group) * share
            piece = image_ref[start : start + share].astype(BF16)
            for copy in range(copies):
                out_ref[(group * halves + half) * copies + copy] = piece


def vmem():
    return pl.BlockSpec(memory_space=pltpu.VMEM)


def hbm():
    return pl.BlockSpec(memory_space=pltpu.HBM)


def pinned(*arrays):
    return [pltpu.with_memory_space_constraint(array, pltpu.HBM) for array in arrays]


def from_halves(block, halves):
    blocks = [block]
    for turn in range(1, halves):
        blocks.append(lax.ppermute(block, "half", [((to + turn) % halves, to) for to in range(halves)]))
    return blocks


def body(records, source_pattern, wavelet, filters, vel_table, vel_index, freq_plan, counts):
    groups = lax.axis_size("freq")
    halves = lax.axis_size("half")
    copies = lax.axis_size("shot")
    shots, rows, xw, nt = records.shape
    depth = vel_index.shape[0]
    nref, _, taps, _, nbin = filters.shape
    nx = xw * groups
    ny = rows * halves
    items = 2 * FPD
    cap = freq_plan.shape[1]
    cells = rows * xw
    folded = LANES % xw == 0 and cells == SUB * LANES
    bins = pltpu.SMEM((groups * FPD + cap,), jnp.int32)
    params = pltpu.CompilerParams(vmem_limit_bytes=VMEM_BYTES)

    classes = from_halves(vel_index, halves)
    patterns = from_halves(source_pattern, halves)

    if folded:
        send_shape = (groups, shots, items * SUB, LANES)
    else:
        send_shape = (shots, groups * SUB, cells)
    table = filters.transpose(0, 2, 3, 1, 4)
    send, own, wave, table = pl.pallas_call(
        functools.partial(send_kernel, groups, folded),
        out_shape=[
            jax.ShapeDtypeStruct(send_shape, BF16),
            jax.ShapeDtypeStruct((SUB, LANES), jnp.int32),
            jax.ShapeDtypeStruct((SUB, LANES), F32),
            jax.ShapeDtypeStruct(table.shape, BF16),
        ],
        in_specs=[hbm()] * 5,
        out_specs=[vmem()] * 4,
        scratch_shapes=[
            pltpu.SMEM(freq_plan.shape, jnp.int32),
            pltpu.SMEM(counts.shape, jnp.int32),
            pltpu.SMEM((2, nbin), F32),
            bins,
            pltpu.VMEM((groups * SUB, nt), F32),
            pltpu.VMEM((shots, cells, nt), BF16),
            pltpu.VMEM((groups * shots * SUB * SUB, LANES), F32),
            pltpu.SemaphoreType.DMA((4,)),
            pltpu.SemaphoreType.DMA((shots * CHUNKS,)),
        ],
        compiler_params=params,
        cost_estimate=pl.CostEstimate(flops=2 * groups * SUB * records.size, bytes_accessed=4 * records.size, transcendentals=0),
        name="send_blocks",
    )(*pinned(freq_plan, counts, wavelet.T, table, records.reshape(shots, cells, nt)))
    send, classes, patterns, table = lax.optimization_barrier((send, classes, patterns, table))
    if folded:
        send = send.reshape(groups * halves, items * SUB, LANES)
        recv = lax.all_to_all(send, ("freq", "half"), 0, 0, tiled=True)
    else:
        send = send.reshape(shots, groups, SUB, cells)[:, :, :items].swapaxes(0, 1)
        send = send.reshape(groups * halves, items, cells)
        recv = lax.all_to_all(send, ("freq", "half"), 0, 0, tiled=True)
        recv = recv.reshape(groups, halves, items, rows, xw).transpose(2, 1, 3, 0, 4).reshape(items * ny, nx)

    table = table.reshape(nref * taps * taps * 2, nbin)
    band_shape = (FPD, taps * 2 * ny, nref * 2 * ny)
    lhs = pltpu.VMEM((FPD, nx, taps * 2 * ny), BF16)
    field = pltpu.VMEM((FPD, nx + 2 * ROW_PAD, 2 * ny), F32)
    band, blend, source = pl.pallas_call(
        functools.partial(source_kernel, taps, nref, depth, halves),
        out_shape=[
            jax.ShapeDtypeStruct(band_shape, BF16),
            jax.ShapeDtypeStruct((depth, nx, 2 * ny), F32),
            jax.ShapeDtypeStruct((depth, FPD, nx, 2 * ny), F32),
        ],
        in_specs=[vmem()] * 3 + [hbm()] * (1 + 2 * halves),
        out_specs=[vmem()] * 3,
        scratch_shapes=[
            pltpu.VMEM((halves,) + vel_index.shape, jnp.int32),
            pltpu.VMEM((halves,) + source_pattern.shape, BF16),
            pltpu.VMEM((1,) + vel_table.shape, F32),
            pltpu.VMEM((FPD, table.shape[0], LANES), F32),
            pltpu.VMEM((depth + 1, ny, nx), F32),
            pltpu.VMEM((SUB, LANES), F32),
            field,
            lhs,
            pltpu.SemaphoreType.DMA((1 + 2 * halves,)),
        ],
        compiler_params=params,
        cost_estimate=pl.CostEstimate(flops=4 * 10**9, bytes_accessed=10**7, transcendentals=0),
        name="source_fields",
    )(own, wave, table, *pinned(vel_table[None], *classes, *patterns))

    scale = 1.0 / math.sqrt(FPD * groups * shots * copies)
    share = ny // (groups * halves)
    terms = pl.pallas_call(
        functools.partial(migrate_kernel, (groups, halves, copies, xw, taps, scale, folded)),
        out_shape=jax.ShapeDtypeStruct((groups * halves * copies, share * depth, nx), BF16),
        in_specs=[vmem()] * 4,
        out_specs=vmem(),
        scratch_shapes=[
            pltpu.VMEM((items * ny, nx), F32),
            field,
            lhs,
            pltpu.VMEM((ny * depth, nx), F32),
        ],
        compiler_params=params,
        name="migrate",
    )(recv, band, blend, source)
    terms = lax.all_to_all(terms, ("freq", "half", "shot"), 0, 0, tiled=True)
    return jnp.sum(terms.astype(F32), axis=0).reshape(1, share, depth, nx)


def solution(mesh):
    return jax.shard_map(
        body,
        mesh=mesh,
        in_specs=(
            P(("group", "shot"), "half", "freq", None),
            P(("group", "shot"), "half", None),
            P(),
            P(),
            P(),
            P("group", "half", None),
            P(),
            P(),
        ),
        out_specs=P("half", "freq", "group", None),
        check_vma=False,
    )
```

```python
import functools
import math

import jax
import jax.numpy as jnp
from jax import lax
from jax.experimental import pallas as pl
from jax.experimental.pallas import tpu as pltpu
from jax.sharding import PartitionSpec as P

FPD = 3
LANES = 128
SUB = 8
ROW_PAD = 8
CHUNKS = 2
VMEM_BYTES = 40 * 1024 * 1024
BF16 = jnp.bfloat16
F32 = jnp.float32


def list_bins(plan_ref, counts_ref, bins_ref):
    groups, cap = plan_ref.shape
    start = jnp.int32(0)
    for holder in range(groups):
        for slot in range(cap):
            bins_ref[start + slot] = plan_ref[holder, slot]
        start = start + counts_ref[holder]


def lane_iota(shape):
    return lax.broadcasted_iota(jnp.int32, shape, len(shape) - 1)


def row_iota(shape):
    return lax.broadcasted_iota(jnp.int32, shape, 0)


def dft_rows(bins_ref, group, nt):
    shape = (SUB, nt)
    row = row_iota(shape)
    bin_id = jnp.zeros(shape, jnp.int32)
    for slot in range(FPD):
        bin_id = jnp.where(row // 2 == slot, bins_ref[group * FPD + slot], bin_id)
    phase = bin_id * lane_iota(shape)
    phase = lax.rem(phase, jnp.int32(nt)) if nt & (nt - 1) else phase & (nt - 1)
    quarter = nt // 4
    turn = (phase + quarter // 2) // quarter
    angle = (phase - turn * quarter).astype(F32) * (2.0 * math.pi / nt)
    turn = (turn + (row & 1)) & 3
    sq = angle * angle
    cos = 1.0 + sq * (-1.0 / 2 + sq * (1.0 / 24 + sq * (-1.0 / 720 + sq * (1.0 / 40320))))
    sin = angle * (1.0 + sq * (-1.0 / 6 + sq * (1.0 / 120 + sq * (-1.0 / 5040 + sq * (1.0 / 362880)))))
    value = jnp.where((turn & 1) == 1, sin, cos)
    value = jnp.where(((turn + 1) & 2) == 2, -value, value)
    return value * (1.0 / math.sqrt(nt))


def transform(dft, block):
    return lax.dot_general(dft, block, (((1,), (1,)), ((), ())), preferred_element_type=F32)


def send_kernel(
    groups, folded, plan_hbm, counts_hbm, wav_hbm, filt_hbm, rec_hbm, out_ref, own_ref, wave_ref, filt_ref,
    plan_ref, counts_ref, wav_ref, bins_ref, dft_ref, rec_ref, tmp_ref, small_sems, sems,
):
    shots, cells, nt = rec_hbm.shape
    part = cells // CHUNKS
    small = [
        pltpu.make_async_copy(plan_hbm, plan_ref, small_sems.at[0]),
        pltpu.make_async_copy(counts_hbm, counts_ref, small_sems.at[1]),
        pltpu.make_async_copy(wav_hbm, wav_ref, small_sems.at[2]),
    ]
    for copy in small:
        copy.start()
    copies = []
    for shot in range(shots):
        for chunk in range(CHUNKS):
            rows = pl.ds(chunk * part, part)
            copy = pltpu.make_async_copy(
                rec_hbm.at[shot, rows], rec_ref.at[shot, rows], sems.at[shot * CHUNKS + chunk]
            )
            copy.start()
            copies.append(copy)
    filters = pltpu.make_async_copy(filt_hbm, filt_ref, small_sems.at[3])
    filters.start()
    for copy in small:
        copy.wait()
    list_bins(plan_ref, counts_ref, bins_ref)
    for group in range(groups):
        dft_ref[group * SUB : (group + 1) * SUB] = dft_rows(bins_ref, group, nt)
    dft = dft_ref[...].astype(BF16)
    first = lax.axis_index("freq") * FPD
    lane = lane_iota((1, LANES))
    for plane in range(FPD):
        bin_id = bins_ref[first + plane]
        own_ref[plane : plane + 1] = jnp.full((1, LANES), bin_id, jnp.int32)
        wave_ref[plane : plane + 1] = jnp.where(lane < LANES // 2, wav_ref[0, bin_id], wav_ref[1, bin_id])
    for shot in range(shots):
        for chunk in range(CHUNKS):
            copies[shot * CHUNKS + chunk].wait()
            out = transform(dft, rec_ref[shot, chunk * part : (chunk + 1) * part])
            if not folded:
                out_ref[shot, :, chunk * part : (chunk + 1) * part] = out.astype(BF16)
                continue
            highs = part // LANES
            for group in range(groups):
                base = (group * shots + shot) * SUB * SUB + chunk * highs
                for high in range(highs):
                    tmp_ref[pl.ds(base + high, SUB, stride=SUB), :] = out[
                        group * SUB : (group + 1) * SUB, high * LANES : (high + 1) * LANES
                    ]
        if folded:
            for group in range(groups):
                base = (group * shots + shot) * SUB * SUB
                out_ref[group, shot] = tmp_ref[base : base + 2 * FPD * SUB].astype(BF16)
    filters.wait()


def make_bands(taps, nref, ny, picked_ref, band_ref):
    reach = taps // 2
    width = 2 * ny
    lane = lane_iota((taps, width))
    full_lane = lane_iota((ny, width))
    keep = jnp.abs((full_lane & (ny - 1)) - row_iota((ny, width))) <= reach
    sign = jnp.where((lane < ny // 2) | (lane >= ny + ny // 2), -1.0, 1.0)
    for ref in range(nref):
        base = jnp.zeros((taps, width), F32)
        for part in range(2):
            for tap in range(taps):
                value = picked_ref[pl.ds((ref * taps + tap) * taps * 2 + part, taps, stride=2), :]
                base = jnp.where(lane == (part * ny + reach - tap) % width, value, base)
        turned = pltpu.roll(base, ny, 1) * sign
        for col_tap in range(taps):
            for part, rows in enumerate((base, turned)):
                spread = jnp.broadcast_to(rows[col_tap : col_tap + 1], (ny, width))
                band = pltpu.roll(spread, 0, 1, stride=1, stride_axis=0)
                band = jnp.where(keep, band, 0.0).astype(BF16)
                at = col_tap * width + part * ny
                band_ref[at : at + ny, ref * width : (ref + 1) * width] = band


def set_field(field_ref, value):
    rows, width = value.shape
    field_ref[:ROW_PAD] = jnp.zeros((ROW_PAD, width), F32)
    field_ref[ROW_PAD : ROW_PAD + rows] = value
    field_ref[ROW_PAD + rows :] = jnp.zeros((ROW_PAD, width), F32)


def advance(taps, field_ref, band_ref, blend):
    rows, width = blend.shape
    first = ROW_PAD - taps // 2
    pieces = [field_ref[pl.ds(first + tap, rows), :].astype(BF16) for tap in range(taps)]
    both = jnp.dot(jnp.concatenate(pieces, axis=1), band_ref[...], preferred_element_type=F32)
    low, high = both[:, :width], both[:, width:]
    return (low + blend * (high - low)).astype(BF16).astype(F32)


def source_kernel(taps, nref, depth, halves, own_ref, wave_ref, filt_ref, table_hbm, *refs):
    class_hbm, refs = refs[:halves], refs[halves:]
    pattern_hbm, refs = refs[:halves], refs[halves:]
    band_ref, blend_ref, source_ref, class_refs, pattern_refs, table_ref, picked_ref, grid_ref, tab_ref, field_ref, sems = refs
    copies = [pltpu.make_async_copy(table_hbm, table_ref, sems.at[0])]
    for turn in range(halves):
        copies.append(pltpu.make_async_copy(class_hbm[turn], class_refs.at[turn], sems.at[1 + 2 * turn]))
        copies.append(pltpu.make_async_copy(pattern_hbm[turn], pattern_refs.at[turn], sems.at[2 + 2 * turn]))
    for copy in copies:
        copy.start()
    mine = lax.axis_index("half")
    rows = class_hbm[0].shape[1]
    ny, nx = grid_ref.shape[1:]
    nbin = filt_ref.shape[1]
    for plane in range(FPD):
        hot = jnp.where(row_iota((nbin, LANES)) == own_ref[plane : plane + 1], 1.0, 0.0).astype(BF16)
        picked_ref[plane] = jnp.dot(filt_ref[...], hot, preferred_element_type=F32)
    for plane in range(FPD - 1):
        make_bands(taps, nref, ny, picked_ref.at[plane], band_ref.at[plane])
    for copy in copies:
        copy.wait()
    for turn in range(halves):
        at = pl.ds(pl.multiple_of(lax.rem(mine + turn, halves) * rows, rows), rows)
        for step in range(depth):
            grid_ref[step, at, :] = class_refs[turn, step].astype(F32)
        grid_ref[depth, at, :] = pattern_refs[turn, mine].astype(F32)
    tab_ref[:, : table_ref.shape[1]] = jnp.broadcast_to(table_ref[...], (SUB, table_ref.shape[1]))
    for step in range(depth):
        pieces = []
        for row in range(0, ny, SUB):
            index = grid_ref[step, row : row + SUB].astype(jnp.int32)
            pieces.append(jnp.take_along_axis(tab_ref[...], index, axis=1))
        blend_ref[step] = jnp.concatenate(pieces + pieces, axis=0).T
    pattern = grid_ref[depth]
    pattern = jnp.concatenate([pattern, pattern], axis=0).T
    for plane in range(FPD):
        set_field(field_ref.at[plane], (pattern * wave_ref[plane : plane + 1]).astype(BF16).astype(F32))
    make_bands(taps, nref, ny, picked_ref.at[FPD - 1], band_ref.at[FPD - 1])
    for step in range(depth):
        for plane in range(FPD):
            new = advance(taps, field_ref.at[plane], band_ref.at[plane], blend_ref[step])
            source_ref[step, plane] = new
            if step + 1 < depth:
                field_ref[plane, ROW_PAD : ROW_PAD + nx] = new


def migrate_kernel(dims, recv_ref, band_ref, blend_ref, source_ref, out_ref, grid_ref, field_ref, image_ref):
    groups, halves, copies, xw, taps, scale, folded = dims
    depth, nx, width = blend_ref.shape
    ny = width // 2
    if folded:
        folds = LANES // xw
        half_rows = ny // halves
        lane = lane_iota((SUB, LANES))
        blocks = [recv_ref[block].astype(F32) for block in range(groups * halves)]
    else:
        grid_ref[...] = recv_ref[...].astype(F32)
    steps = [None] * depth

    def gather(plane):
        if folded:
            for half in range(halves):
                for item in range(2 * plane, 2 * plane + 2):
                    for low in range(folds):
                        kept = None
                        for group in range(groups):
                            piece = blocks[group * halves + half][item * SUB : (item + 1) * SUB]
                            shift = ((group - low) * xw) % LANES
                            if shift:
                                piece = pltpu.roll(piece, shift, 1)
                            kept = piece if kept is None else jnp.where(lane // xw == group, piece, kept)
                        grid_ref[pl.ds(item * ny + half * half_rows + low, SUB, stride=folds), :] = kept
        set_field(field_ref.at[plane], grid_ref[plane * width : (plane + 1) * width].T)

    def move(step, plane):
        new = advance(taps, field_ref.at[plane], band_ref.at[plane], blend_ref[step])
        if step + 1 < depth:
            field_ref[plane, ROW_PAD : ROW_PAD + nx] = new
        term = source_ref[step, plane] * new
        steps[step] = term if steps[step] is None else steps[step] + term

    gather(0)
    for plane in range(FPD):
        if plane + 1 < FPD:
            gather(plane + 1)
        move(0, plane)
    for step in range(depth):
        for plane in range(FPD if step else 0):
            move(step, plane)
        turned = steps[step].T
        image_ref[pl.ds(step, ny, stride=depth), :] = (turned[:ny] + turned[ny:]) * scale
    share = ny // (groups * halves) * depth
    for group in range(groups):
        for half in range(halves):
            start = (half * groups + group) * share
            piece = image_ref[start : start + share].astype(BF16)
            for copy in range(copies):
                out_ref[(group * halves + half) * copies + copy] = piece


def vmem():
    return pl.BlockSpec(memory_space=pltpu.VMEM)


def hbm():
    return pl.BlockSpec(memory_space=pltpu.HBM)


def pinned(*arrays):
    return [pltpu.with_memory_space_constraint(array, pltpu.HBM) for array in arrays]


def from_halves(block, halves):
    blocks = [block]
    for turn in range(1, halves):
        blocks.append(lax.ppermute(block, "half", [((to + turn) % halves, to) for to in range(halves)]))
    return blocks


def body(records, source_pattern, wavelet, filters, vel_table, vel_index, freq_plan, counts):
    groups = lax.axis_size("freq")
    halves = lax.axis_size("half")
    copies = lax.axis_size("shot")
    shots, rows, xw, nt = records.shape
    depth = vel_index.shape[0]
    nref, _, taps, _, nbin = filters.shape
    nx = xw * groups
    ny = rows * halves
    items = 2 * FPD
    cap = freq_plan.shape[1]
    cells = rows * xw
    folded = LANES % xw == 0 and cells == SUB * LANES
    bins = pltpu.SMEM((groups * FPD + cap,), jnp.int32)
    params = pltpu.CompilerParams(vmem_limit_bytes=VMEM_BYTES)

    classes = from_halves(vel_index, halves)
    patterns = from_halves(source_pattern, halves)

    if folded:
        send_shape = (groups, shots, items * SUB, LANES)
    else:
        send_shape = (shots, groups * SUB, cells)
    table = filters.transpose(0, 2, 3, 1, 4)
    send, own, wave, table = pl.pallas_call(
        functools.partial(send_kernel, groups, folded),
        out_shape=[
            jax.ShapeDtypeStruct(send_shape, BF16),
            jax.ShapeDtypeStruct((SUB, LANES), jnp.int32),
            jax.ShapeDtypeStruct((SUB, LANES), F32),
            jax.ShapeDtypeStruct(table.shape, BF16),
        ],
        in_specs=[hbm()] * 5,
        out_specs=[vmem()] * 4,
        scratch_shapes=[
            pltpu.SMEM(freq_plan.shape, jnp.int32),
            pltpu.SMEM(counts.shape, jnp.int32),
            pltpu.SMEM((2, nbin), F32),
            bins,
            pltpu.VMEM((groups * SUB, nt), F32),
            pltpu.VMEM((shots, cells, nt), BF16),
            pltpu.VMEM((groups * shots * SUB * SUB, LANES), F32),
            pltpu.SemaphoreType.DMA((4,)),
            pltpu.SemaphoreType.DMA((shots * CHUNKS,)),
        ],
        compiler_params=params,
        cost_estimate=pl.CostEstimate(flops=2 * groups * SUB * records.size, bytes_accessed=4 * records.size, transcendentals=0),
        name="send_blocks",
    )(*pinned(freq_plan, counts, wavelet.T, table, records.reshape(shots, cells, nt)))
    send, classes, patterns, table = lax.optimization_barrier((send, classes, patterns, table))
    if folded:
        send = send.reshape(groups * halves, items * SUB, LANES)
        recv = lax.all_to_all(send, ("freq", "half"), 0, 0, tiled=True)
    else:
        send = send.reshape(shots, groups, SUB, cells)[:, :, :items].swapaxes(0, 1)
        send = send.reshape(groups * halves, items, cells)
        recv = lax.all_to_all(send, ("freq", "half"), 0, 0, tiled=True)
        recv = recv.reshape(groups, halves, items, rows, xw).transpose(2, 1, 3, 0, 4).reshape(items * ny, nx)

    table = table.reshape(nref * taps * taps * 2, nbin)
    band_shape = (FPD, taps * 2 * ny, nref * 2 * ny)
    field = pltpu.VMEM((FPD, nx + 2 * ROW_PAD, 2 * ny), F32)
    band, blend, source = pl.pallas_call(
        functools.partial(source_kernel, taps, nref, depth, halves),
        out_shape=[
            jax.ShapeDtypeStruct(band_shape, BF16),
            jax.ShapeDtypeStruct((depth, nx, 2 * ny), F32),
            jax.ShapeDtypeStruct((depth, FPD, nx, 2 * ny), F32),
        ],
        in_specs=[vmem()] * 3 + [hbm()] * (1 + 2 * halves),
        out_specs=[vmem()] * 3,
        scratch_shapes=[
            pltpu.VMEM((halves,) + vel_index.shape, jnp.int32),
            pltpu.VMEM((halves,) + source_pattern.shape, BF16),
            pltpu.VMEM((1,) + vel_table.shape, F32),
            pltpu.VMEM((FPD, table.shape[0], LANES), F32),
            pltpu.VMEM((depth + 1, ny, nx), F32),
            pltpu.VMEM((SUB, LANES), F32),
            field,
            pltpu.SemaphoreType.DMA((1 + 2 * halves,)),
        ],
        compiler_params=params,
        cost_estimate=pl.CostEstimate(flops=4 * 10**9, bytes_accessed=10**7, transcendentals=0),
        name="source_fields",
    )(own, wave, table, *pinned(vel_table[None], *classes, *patterns))

    scale = 1.0 / math.sqrt(FPD * groups * shots * copies)
    share = ny // (groups * halves)
    terms = pl.pallas_call(
        functools.partial(migrate_kernel, (groups, halves, copies, xw, taps, scale, folded)),
        out_shape=jax.ShapeDtypeStruct((groups * halves * copies, share * depth, nx), BF16),
        in_specs=[vmem()] * 4,
        out_specs=vmem(),
        scratch_shapes=[
            pltpu.VMEM((items * ny, nx), F32),
            field,
            pltpu.VMEM((ny * depth, nx), F32),
        ],
        compiler_params=params,
        name="migrate",
    )(recv, band, blend, source)
    terms = lax.all_to_all(terms, ("freq", "half", "shot"), 0, 0, tiled=True)
    return jnp.sum(terms.astype(F32), axis=0).reshape(1, share, depth, nx)


def solution(mesh):
    return jax.shard_map(
        body,
        mesh=mesh,
        in_specs=(
            P(("group", "shot"), "half", "freq", None),
            P(("group", "shot"), "half", None),
            P(),
            P(),
            P(),
            P("group", "half", None),
            P(),
            P(),
        ),
        out_specs=P("half", "freq", "group", None),
        check_vma=False,
    )
```

```python
import functools
import math

import jax
import jax.numpy as jnp
from jax import lax
from jax.experimental import pallas as pl
from jax.experimental.pallas import tpu as pltpu
from jax.sharding import PartitionSpec as P

FPD = 3
LANES = 128
SUB = 8
ROW_PAD = 8
VMEM_BYTES = 40 * 1024 * 1024
BF16 = jnp.bfloat16
F32 = jnp.float32


def list_bins(plan_ref, counts_ref, bins_ref):
    groups, cap = plan_ref.shape
    start = jnp.int32(0)
    for holder in range(groups):
        for slot in range(cap):
            bins_ref[start + slot] = plan_ref[holder, slot]
        start = start + counts_ref[holder]


def lane_iota(shape):
    return lax.broadcasted_iota(jnp.int32, shape, len(shape) - 1)


def row_iota(shape):
    return lax.broadcasted_iota(jnp.int32, shape, 0)


def dft_rows(bins_ref, group, nt):
    shape = (SUB, nt)
    row = row_iota(shape)
    bin_id = jnp.zeros(shape, jnp.int32)
    for slot in range(FPD):
        bin_id = jnp.where(row // 2 == slot, bins_ref[group * FPD + slot], bin_id)
    phase = bin_id * lane_iota(shape)
    phase = lax.rem(phase, jnp.int32(nt)) if nt & (nt - 1) else phase & (nt - 1)
    quarter = nt // 4
    turn = (phase + quarter // 2) // quarter
    angle = (phase - turn * quarter).astype(F32) * (2.0 * math.pi / nt)
    turn = (turn + (row & 1)) & 3
    sq = angle * angle
    cos = 1.0 + sq * (-1.0 / 2 + sq * (1.0 / 24 + sq * (-1.0 / 720 + sq * (1.0 / 40320))))
    sin = angle * (1.0 + sq * (-1.0 / 6 + sq * (1.0 / 120 + sq * (-1.0 / 5040 + sq * (1.0 / 362880)))))
    value = jnp.where((turn & 1) == 1, sin, cos)
    value = jnp.where(((turn + 1) & 2) == 2, -value, value)
    return value * (1.0 / math.sqrt(nt))


def transform(dft, block):
    return lax.dot_general(dft, block, (((1,), (1,)), ((), ())), preferred_element_type=F32)


def prepare_kernel(
    groups, plan_hbm, counts_hbm, wav_hbm, filt_hbm, dft_ref, own_ref, wave_ref, filt_ref,
    plan_ref, counts_ref, wav_ref, bins_ref, sems,
):
    nt = dft_ref.shape[1]
    filters = pltpu.make_async_copy(filt_hbm, filt_ref, sems.at[3])
    small = [
        pltpu.make_async_copy(plan_hbm, plan_ref, sems.at[0]),
        pltpu.make_async_copy(counts_hbm, counts_ref, sems.at[1]),
        pltpu.make_async_copy(wav_hbm, wav_ref, sems.at[2]),
    ]
    for copy in small + [filters]:
        copy.start()
    for copy in small:
        copy.wait()
    list_bins(plan_ref, counts_ref, bins_ref)
    for pair in range(0, groups, 2):
        both = [dft_rows(bins_ref, group, nt) for group in range(pair, min(pair + 2, groups))]
        dft_ref[pair * SUB : (pair + len(both)) * SUB] = jnp.concatenate(both, axis=0).astype(BF16)
    first = lax.axis_index("freq") * FPD
    lane = lane_iota((1, LANES))
    for plane in range(FPD):
        bin_id = bins_ref[first + plane]
        own_ref[plane : plane + 1] = jnp.full((1, LANES), bin_id, jnp.int32)
        wave_ref[plane : plane + 1] = jnp.where(lane < LANES // 2, wav_ref[0, bin_id], wav_ref[1, bin_id])
    filters.wait()


def send_kernel(groups, folded, dft_ref, rec_ref, out_ref, tmp_ref):
    shots, cells, _ = rec_ref.shape
    dft = dft_ref[...]
    for shot in range(shots):
        out = transform(dft, rec_ref[shot])
        if not folded:
            out_ref[shot] = out.astype(BF16)
            continue
        for group in range(groups):
            base = (group * shots + shot) * SUB * SUB
            for high in range(SUB):
                tmp_ref[pl.ds(base + high, SUB, stride=SUB), :] = out[
                    group * SUB : (group + 1) * SUB, high * LANES : (high + 1) * LANES
                ]
            out_ref[group, shot] = tmp_ref[base : base + 2 * FPD * SUB].astype(BF16)


def make_bands(taps, nref, ny, picked_ref, band_ref):
    reach = taps // 2
    width = 2 * ny
    lane = lane_iota((taps, width))
    full_lane = lane_iota((ny, width))
    keep = jnp.abs((full_lane & (ny - 1)) - row_iota((ny, width))) <= reach
    sign = jnp.where((lane < ny // 2) | (lane >= ny + ny // 2), -1.0, 1.0)
    for ref in range(nref):
        base = jnp.zeros((taps, width), F32)
        for part in range(2):
            for tap in range(taps):
                value = picked_ref[pl.ds((ref * taps + tap) * taps * 2 + part, taps, stride=2), :]
                base = jnp.where(lane == (part * ny + reach - tap) % width, value, base)
        turned = pltpu.roll(base, ny, 1) * sign
        for col_tap in range(taps):
            for part, rows in enumerate((base, turned)):
                spread = jnp.broadcast_to(rows[col_tap : col_tap + 1], (ny, width))
                band = pltpu.roll(spread, 0, 1, stride=1, stride_axis=0)
                band = jnp.where(keep, band, 0.0).astype(BF16)
                at = col_tap * width + part * ny
                band_ref[at : at + ny, ref * width : (ref + 1) * width] = band


def set_field(field_ref, value):
    rows, width = value.shape
    field_ref[:ROW_PAD] = jnp.zeros((ROW_PAD, width), F32)
    field_ref[ROW_PAD : ROW_PAD + rows] = value
    field_ref[ROW_PAD + rows :] = jnp.zeros((ROW_PAD, width), F32)


def shifted(taps, field_ref):
    first = ROW_PAD - taps // 2
    rows = field_ref.shape[0] - 2 * ROW_PAD
    pieces = [field_ref[pl.ds(first + tap, rows), :].astype(BF16) for tap in range(taps)]
    return jnp.concatenate(pieces, axis=1)


def advance(left, band_ref, blend):
    width = blend.shape[1]
    both = jnp.dot(left, band_ref[...], preferred_element_type=F32)
    low, high = both[:, :width], both[:, width:]
    return (low + blend * (high - low)).astype(BF16).astype(F32)


def run_steps(taps, depth, field_ref, band_ref, blend_ref, prepare, use):
    rows = field_ref.shape[1] - 2 * ROW_PAD
    order = [(step, plane) for step in range(depth) for plane in range(FPD)]
    prepare(0)
    left = shifted(taps, field_ref.at[0])
    for at, (step, plane) in enumerate(order):
        follow = None
        if at + 1 < len(order):
            after = order[at + 1][1]
            if order[at + 1][0] == 0:
                prepare(after)
            follow = shifted(taps, field_ref.at[after])
        new = advance(left, band_ref.at[plane], blend_ref[step])
        if step + 1 < depth:
            field_ref[plane, ROW_PAD : ROW_PAD + rows] = new
        use(step, plane, new)
        left = follow


def source_kernel(taps, nref, depth, halves, own_ref, wave_ref, filt_ref, table_hbm, *refs):
    class_hbm, refs = refs[:halves], refs[halves:]
    pattern_hbm, refs = refs[:halves], refs[halves:]
    band_ref, blend_ref, source_ref, class_refs, pattern_refs, table_ref, picked_ref, grid_ref, tab_ref, field_ref, sems = refs
    copies = [pltpu.make_async_copy(table_hbm, table_ref, sems.at[0])]
    for turn in range(halves):
        copies.append(pltpu.make_async_copy(class_hbm[turn], class_refs.at[turn], sems.at[1 + 2 * turn]))
        copies.append(pltpu.make_async_copy(pattern_hbm[turn], pattern_refs.at[turn], sems.at[2 + 2 * turn]))
    for copy in copies:
        copy.start()
    mine = lax.axis_index("half")
    rows = class_hbm[0].shape[1]
    ny, nx = grid_ref.shape[1:]
    nbin = filt_ref.shape[1]
    for plane in range(FPD):
        hot = jnp.where(row_iota((nbin, LANES)) == own_ref[plane : plane + 1], 1.0, 0.0).astype(BF16)
        picked_ref[plane, : filt_ref.shape[0]] = jnp.dot(filt_ref[...], hot, preferred_element_type=F32)
    for plane in range(FPD - 1):
        make_bands(taps, nref, ny, picked_ref.at[plane], band_ref.at[plane])
    for copy in copies:
        copy.wait()
    for turn in range(halves):
        at = pl.ds(pl.multiple_of(lax.rem(mine + turn, halves) * rows, rows), rows)
        for step in range(depth):
            grid_ref[step, at, :] = class_refs[turn, step].astype(F32)
        grid_ref[depth, at, :] = pattern_refs[turn, mine].astype(F32)
    tab_ref[:, : table_ref.shape[1]] = jnp.broadcast_to(table_ref[...], (SUB, table_ref.shape[1]))
    for step in range(depth):
        pieces = []
        for row in range(0, ny, SUB):
            index = grid_ref[step, row : row + SUB].astype(jnp.int32)
            pieces.append(jnp.take_along_axis(tab_ref[...], index, axis=1))
        blend_ref[step] = jnp.concatenate(pieces + pieces, axis=0).T
    pattern = grid_ref[depth]
    pattern = jnp.concatenate([pattern, pattern], axis=0).T
    make_bands(taps, nref, ny, picked_ref.at[FPD - 1], band_ref.at[FPD - 1])

    def start(plane):
        set_field(field_ref.at[plane], (pattern * wave_ref[plane : plane + 1]).astype(BF16).astype(F32))

    def keep(step, plane, new):
        source_ref[step, plane] = new

    run_steps(taps, depth, field_ref, band_ref, blend_ref, start, keep)


def migrate_kernel(dims, recv_ref, band_ref, blend_ref, source_ref, out_ref, grid_ref, field_ref, image_ref):
    groups, halves, copies, xw, taps, scale, folded = dims
    depth, nx, width = blend_ref.shape
    ny = width // 2
    if folded:
        folds = LANES // xw
        half_rows = ny // halves
        lane = lane_iota((SUB, LANES))
        blocks = [recv_ref[block].astype(F32) for block in range(groups * halves)]
    else:
        grid_ref[: recv_ref.shape[0]] = recv_ref[...].astype(F32)
    steps = [None] * depth

    def gather(plane):
        if folded:
            for half in range(halves):
                for item in range(2 * plane, 2 * plane + 2):
                    for low in range(folds):
                        kept = None
                        for group in range(groups):
                            piece = blocks[group * halves + half][item * SUB : (item + 1) * SUB]
                            shift = ((group - low) * xw) % LANES
                            if shift:
                                piece = pltpu.roll(piece, shift, 1)
                            kept = piece if kept is None else jnp.where(lane // xw == group, piece, kept)
                        grid_ref[pl.ds(item * ny + half * half_rows + low, SUB, stride=folds), :] = kept
        set_field(field_ref.at[plane], grid_ref[plane * width : (plane + 1) * width].T)

    def correlate(step, plane, new):
        term = source_ref[step, plane] * new
        steps[step] = term if steps[step] is None else steps[step] + term
        if plane == FPD - 1:
            turned = steps[step].T
            image_ref[pl.ds(step, ny, stride=depth), :] = (turned[:ny] + turned[ny:]) * scale

    run_steps(taps, depth, field_ref, band_ref, blend_ref, gather, correlate)
    share = ny // (groups * halves) * depth
    for group in range(groups):
        for half in range(halves):
            start = (half * groups + group) * share
            piece = image_ref[start : start + share].astype(BF16)
            for copy in range(copies):
                out_ref[(group * halves + half) * copies + copy] = piece


def vmem():
    return pl.BlockSpec(memory_space=pltpu.VMEM)


def hbm():
    return pl.BlockSpec(memory_space=pltpu.HBM)


def pinned(*arrays):
    return [pltpu.with_memory_space_constraint(array, pltpu.HBM) for array in arrays]


def from_halves(block, halves):
    blocks = [block]
    for turn in range(1, halves):
        blocks.append(lax.ppermute(block, "half", [((to + turn) % halves, to) for to in range(halves)]))
    return blocks


def body(records, source_pattern, wavelet, filters, vel_table, vel_index, freq_plan, counts):
    groups = lax.axis_size("freq")
    halves = lax.axis_size("half")
    copies = lax.axis_size("shot")
    shots, rows, xw, nt = records.shape
    depth = vel_index.shape[0]
    nref, _, taps, _, nbin = filters.shape
    nx = xw * groups
    ny = rows * halves
    items = 2 * FPD
    cap = freq_plan.shape[1]
    cells = rows * xw
    folded = LANES % xw == 0 and cells == SUB * LANES
    bins = pltpu.SMEM((groups * FPD + cap,), jnp.int32)
    params = pltpu.CompilerParams(vmem_limit_bytes=VMEM_BYTES)


    if folded:
        send_shape = (groups, shots, items * SUB, LANES)
    else:
        send_shape = (shots, groups * SUB, cells)
    table = filters.transpose(0, 2, 3, 1, 4)
    dft, own, wave, table = pl.pallas_call(
        functools.partial(prepare_kernel, groups),
        out_shape=[
            jax.ShapeDtypeStruct((groups * SUB, nt), BF16),
            jax.ShapeDtypeStruct((SUB, LANES), jnp.int32),
            jax.ShapeDtypeStruct((SUB, LANES), F32),
            jax.ShapeDtypeStruct(table.shape, BF16),
        ],
        in_specs=[hbm()] * 4,
        out_specs=[vmem()] * 4,
        scratch_shapes=[
            pltpu.SMEM(freq_plan.shape, jnp.int32),
            pltpu.SMEM(counts.shape, jnp.int32),
            pltpu.SMEM((2, nbin), F32),
            bins,
            pltpu.SemaphoreType.DMA((4,)),
        ],
        compiler_params=params,
        cost_estimate=pl.CostEstimate(flops=3 * 10**9, bytes_accessed=4 * 10**6, transcendentals=0),
        name="prepare",
    )(*pinned(freq_plan, counts, wavelet.T, table))
    own, vel_index, source_pattern = lax.optimization_barrier((own, vel_index, source_pattern))
    classes = from_halves(vel_index, halves)
    patterns = from_halves(source_pattern, halves)
    send = pl.pallas_call(
        functools.partial(send_kernel, groups, folded),
        out_shape=jax.ShapeDtypeStruct(send_shape, BF16),
        in_specs=[vmem()] * 2,
        out_specs=vmem(),
        scratch_shapes=[pltpu.VMEM((groups * shots * SUB * SUB + SUB, LANES), F32)],
        compiler_params=params,
        name="send_blocks",
    )(dft, records.reshape(shots, cells, nt))
    if folded:
        send = send.reshape(groups * halves, items * SUB, LANES)
        recv = lax.all_to_all(send, ("freq", "half"), 0, 0, tiled=True)
    else:
        send = send.reshape(shots, groups, SUB, cells)[:, :, :items].swapaxes(0, 1)
        send = send.reshape(groups * halves, items, cells)
        recv = lax.all_to_all(send, ("freq", "half"), 0, 0, tiled=True)
        recv = recv.reshape(groups, halves, items, rows, xw).transpose(2, 1, 3, 0, 4).reshape(items * ny, nx)

    table = table.reshape(nref * taps * taps * 2, nbin)
    band_shape = (FPD, taps * 2 * ny, nref * 2 * ny)
    field = pltpu.VMEM((FPD, nx + 2 * ROW_PAD, 2 * ny), F32)
    band, blend, source = pl.pallas_call(
        functools.partial(source_kernel, taps, nref, depth, halves),
        out_shape=[
            jax.ShapeDtypeStruct(band_shape, BF16),
            jax.ShapeDtypeStruct((depth, nx, 2 * ny), F32),
            jax.ShapeDtypeStruct((depth, FPD, nx, 2 * ny), F32),
        ],
        in_specs=[vmem()] * 3 + [hbm()] * (2 + halves) + [pl.BlockSpec(memory_space=pl.ANY)] * (halves - 1),
        out_specs=[vmem()] * 3,
        scratch_shapes=[
            pltpu.VMEM((halves,) + vel_index.shape, jnp.int32),
            pltpu.VMEM((halves,) + source_pattern.shape, BF16),
            pltpu.VMEM((1,) + vel_table.shape, F32),
            pltpu.VMEM((FPD, (table.shape[0] + 2 * taps + SUB) // SUB * SUB + 2 * SUB, LANES), F32),
            pltpu.VMEM((depth + 1, ny, nx), F32),
            pltpu.VMEM((SUB, LANES), F32),
            field,
            pltpu.SemaphoreType.DMA((1 + 2 * halves,)),
        ],
        compiler_params=params,
        cost_estimate=pl.CostEstimate(flops=4 * 10**9, bytes_accessed=10**7, transcendentals=0),
        name="source_fields",
    )(own, wave, table, *pinned(vel_table[None], *classes, patterns[0]), *patterns[1:])

    scale = 1.0 / math.sqrt(FPD * groups * shots * copies)
    share = ny // (groups * halves)
    terms = pl.pallas_call(
        functools.partial(migrate_kernel, (groups, halves, copies, xw, taps, scale, folded)),
        out_shape=jax.ShapeDtypeStruct((groups * halves * copies, share * depth, nx), BF16),
        in_specs=[vmem()] * 4,
        out_specs=vmem(),
        scratch_shapes=[
            pltpu.VMEM((items * ny + SUB, nx), F32),
            field,
            pltpu.VMEM((ny * depth + SUB, nx), F32),
        ],
        compiler_params=params,
        name="migrate",
    )(recv, band, blend, source)
    terms = lax.all_to_all(terms, ("freq", "half", "shot"), 0, 0, tiled=True)
    return jnp.sum(terms.astype(F32), axis=0).reshape(1, share, depth, nx)


def solution(mesh):
    return jax.shard_map(
        body,
        mesh=mesh,
        in_specs=(
            P(("group", "shot"), "half", "freq", None),
            P(("group", "shot"), "half", None),
            P(),
            P(),
            P(),
            P("group", "half", None),
            P(),
            P(),
        ),
        out_specs=P("half", "freq", "group", None),
        check_vma=False,
    )
```

```python
import functools
import math

import jax
import jax.numpy as jnp
from jax import lax
from jax.experimental import pallas as pl
from jax.experimental.pallas import tpu as pltpu
from jax.sharding import PartitionSpec as P

FPD = 3
LANES = 128
SUB = 8
ROW_PAD = 8
VMEM_BYTES = 40 * 1024 * 1024
BF16 = jnp.bfloat16
F32 = jnp.float32


def list_bins(plan_ref, counts_ref, bins_ref):
    groups, cap = plan_ref.shape
    start = jnp.int32(0)
    for holder in range(groups):
        for slot in range(cap):
            bins_ref[start + slot] = plan_ref[holder, slot]
        start = start + counts_ref[holder]


def lane_iota(shape):
    return lax.broadcasted_iota(jnp.int32, shape, len(shape) - 1)


def row_iota(shape):
    return lax.broadcasted_iota(jnp.int32, shape, 0)


def dft_rows(bins_ref, group, nt):
    shape = (SUB, nt)
    row = row_iota(shape)
    bin_id = jnp.zeros(shape, jnp.int32)
    for slot in range(FPD):
        bin_id = jnp.where(row // 2 == slot, bins_ref[group * FPD + slot], bin_id)
    phase = bin_id * lane_iota(shape)
    phase = lax.rem(phase, jnp.int32(nt)) if nt & (nt - 1) else phase & (nt - 1)
    quarter = nt // 4
    turn = (phase + quarter // 2) // quarter
    angle = (phase - turn * quarter).astype(F32) * (2.0 * math.pi / nt)
    turn = (turn + (row & 1)) & 3
    sq = angle * angle
    cos = 1.0 + sq * (-1.0 / 2 + sq * (1.0 / 24 + sq * (-1.0 / 720 + sq * (1.0 / 40320))))
    sin = angle * (1.0 + sq * (-1.0 / 6 + sq * (1.0 / 120 + sq * (-1.0 / 5040 + sq * (1.0 / 362880)))))
    value = jnp.where((turn & 1) == 1, sin, cos)
    value = jnp.where(((turn + 1) & 2) == 2, -value, value)
    return value * (1.0 / math.sqrt(nt))


def transform(dft, block):
    return lax.dot_general(dft, block, (((1,), (1,)), ((), ())), preferred_element_type=F32)


def prepare_kernel(
    groups, plan_hbm, counts_hbm, wav_hbm, filt_hbm, dft_ref, own_ref, wave_ref, filt_ref,
    plan_ref, counts_ref, wav_ref, bins_ref, sems,
):
    nt = dft_ref.shape[1]
    filters = pltpu.make_async_copy(filt_hbm, filt_ref, sems.at[3])
    small = [
        pltpu.make_async_copy(plan_hbm, plan_ref, sems.at[0]),
        pltpu.make_async_copy(counts_hbm, counts_ref, sems.at[1]),
        pltpu.make_async_copy(wav_hbm, wav_ref, sems.at[2]),
    ]
    for copy in small + [filters]:
        copy.start()
    for copy in small:
        copy.wait()
    list_bins(plan_ref, counts_ref, bins_ref)
    for pair in range(0, groups, 2):
        both = [dft_rows(bins_ref, group, nt) for group in range(pair, min(pair + 2, groups))]
        dft_ref[pair * SUB : (pair + len(both)) * SUB] = jnp.concatenate(both, axis=0).astype(BF16)
    first = lax.axis_index("freq") * FPD
    lane = lane_iota((1, LANES))
    for plane in range(FPD):
        bin_id = bins_ref[first + plane]
        own_ref[plane : plane + 1] = jnp.full((1, LANES), bin_id, jnp.int32)
        wave_ref[plane : plane + 1] = jnp.where(lane < LANES // 2, wav_ref[0, bin_id], wav_ref[1, bin_id])
    filters.wait()


def send_kernel(groups, folded, dft_ref, rec_ref, out_ref, tmp_ref):
    shots, cells, _ = rec_ref.shape
    dft = dft_ref[...]
    for shot in range(shots):
        out = transform(dft, rec_ref[shot])
        if not folded:
            out_ref[shot] = out.astype(BF16)
            continue
        for group in range(groups):
            base = (group * shots + shot) * SUB * SUB
            for high in range(SUB):
                tmp_ref[pl.ds(base + high, SUB, stride=SUB), :] = out[
                    group * SUB : (group + 1) * SUB, high * LANES : (high + 1) * LANES
                ]
            out_ref[shot, group] = tmp_ref[base : base + 2 * FPD * SUB].astype(BF16)


def make_bands(taps, nref, ny, picked_ref, band_ref):
    reach = taps // 2
    width = 2 * ny
    lane = lane_iota((taps, width))
    full_lane = lane_iota((ny, width))
    keep = jnp.abs((full_lane & (ny - 1)) - row_iota((ny, width))) <= reach
    sign = jnp.where((lane < ny // 2) | (lane >= ny + ny // 2), -1.0, 1.0)
    for ref in range(nref):
        base = jnp.zeros((taps, width), F32)
        for part in range(2):
            for tap in range(taps):
                value = picked_ref[pl.ds((ref * taps + tap) * taps * 2 + part, taps, stride=2), :]
                base = jnp.where(lane == (part * ny + reach - tap) % width, value, base)
        turned = pltpu.roll(base, ny, 1) * sign
        for col_tap in range(taps):
            for part, rows in enumerate((base, turned)):
                spread = jnp.broadcast_to(rows[col_tap : col_tap + 1], (ny, width))
                band = pltpu.roll(spread, 0, 1, stride=1, stride_axis=0)
                band = jnp.where(keep, band, 0.0).astype(BF16)
                at = col_tap * width + part * ny
                band_ref[at : at + ny, ref * width : (ref + 1) * width] = band


def set_field(field_ref, value):
    rows, width = value.shape
    field_ref[:ROW_PAD] = jnp.zeros((ROW_PAD, width), F32)
    field_ref[ROW_PAD : ROW_PAD + rows] = value
    field_ref[ROW_PAD + rows :] = jnp.zeros((ROW_PAD, width), F32)


def shifted(taps, field_ref):
    first = ROW_PAD - taps // 2
    rows = field_ref.shape[0] - 2 * ROW_PAD
    pieces = [field_ref[pl.ds(first + tap, rows), :].astype(BF16) for tap in range(taps)]
    return jnp.concatenate(pieces, axis=1)


def advance(left, band_ref, blend):
    width = blend.shape[1]
    both = jnp.dot(left, band_ref[...], preferred_element_type=F32)
    low, high = both[:, :width], both[:, width:]
    return (low + blend * (high - low)).astype(BF16).astype(F32)


def run_steps(taps, depth, field_ref, band_ref, blend_ref, prepare, use):
    rows = field_ref.shape[1] - 2 * ROW_PAD
    order = [(step, plane) for step in range(depth) for plane in range(FPD)]
    prepare(0)
    left = shifted(taps, field_ref.at[0])
    for at, (step, plane) in enumerate(order):
        follow = None
        if at + 1 < len(order):
            after = order[at + 1][1]
            if order[at + 1][0] == 0:
                prepare(after)
            follow = shifted(taps, field_ref.at[after])
        new = advance(left, band_ref.at[plane], blend_ref[step])
        if step + 1 < depth:
            field_ref[plane, ROW_PAD : ROW_PAD + rows] = new
        use(step, plane, new)
        left = follow


def source_kernel(taps, nref, depth, halves, own_ref, wave_ref, filt_ref, table_hbm, *refs):
    class_hbm, refs = refs[:halves], refs[halves:]
    pattern_hbm, refs = refs[:halves], refs[halves:]
    band_ref, blend_ref, source_ref, class_refs, pattern_refs, table_ref, picked_ref, grid_ref, tab_ref, field_ref, sems = refs
    copies = [pltpu.make_async_copy(table_hbm, table_ref, sems.at[0])]
    for turn in range(halves):
        copies.append(pltpu.make_async_copy(class_hbm[turn], class_refs.at[turn], sems.at[1 + 2 * turn]))
        copies.append(pltpu.make_async_copy(pattern_hbm[turn], pattern_refs.at[turn], sems.at[2 + 2 * turn]))
    for copy in copies:
        copy.start()
    mine = lax.axis_index("half")
    rows = class_hbm[0].shape[1]
    ny, nx = grid_ref.shape[1:]
    nbin = filt_ref.shape[1]
    for plane in range(FPD):
        hot = jnp.where(row_iota((nbin, LANES)) == own_ref[plane : plane + 1], 1.0, 0.0).astype(BF16)
        picked_ref[plane, : filt_ref.shape[0]] = jnp.dot(filt_ref[...], hot, preferred_element_type=F32)
    for plane in range(FPD - 1):
        make_bands(taps, nref, ny, picked_ref.at[plane], band_ref.at[plane])
    for copy in copies:
        copy.wait()
    for turn in range(halves):
        at = pl.ds(pl.multiple_of(lax.rem(mine + turn, halves) * rows, rows), rows)
        for step in range(depth):
            grid_ref[step, at, :] = class_refs[turn, step].astype(F32)
        grid_ref[depth, at, :] = pattern_refs[turn, mine].astype(F32)
    tab_ref[:, : table_ref.shape[1]] = jnp.broadcast_to(table_ref[...], (SUB, table_ref.shape[1]))
    for step in range(depth):
        pieces = []
        for row in range(0, ny, SUB):
            index = grid_ref[step, row : row + SUB].astype(jnp.int32)
            pieces.append(jnp.take_along_axis(tab_ref[...], index, axis=1))
        blend_ref[step] = jnp.concatenate(pieces + pieces, axis=0).T
    pattern = grid_ref[depth]
    pattern = jnp.concatenate([pattern, pattern], axis=0).T
    make_bands(taps, nref, ny, picked_ref.at[FPD - 1], band_ref.at[FPD - 1])

    def start(plane):
        set_field(field_ref.at[plane], (pattern * wave_ref[plane : plane + 1]).astype(BF16).astype(F32))

    def keep(step, plane, new):
        source_ref[step, plane] = new

    run_steps(taps, depth, field_ref, band_ref, blend_ref, start, keep)


def migrate_kernel(dims, recv_ref, band_ref, blend_ref, source_ref, out_ref, grid_ref, field_ref, image_ref):
    groups, halves, copies, xw, taps, scale, folded = dims
    depth, nx, width = blend_ref.shape
    ny = width // 2
    if folded:
        folds = LANES // xw
        half_rows = ny // halves
        lane = lane_iota((SUB, LANES))
        blocks = [recv_ref[block].astype(F32) for block in range(groups * halves)]
    else:
        grid_ref[: recv_ref.shape[0]] = recv_ref[...].astype(F32)
    steps = [None] * depth

    def gather(plane):
        if folded:
            for half in range(halves):
                for item in range(2 * plane, 2 * plane + 2):
                    for low in range(folds):
                        kept = None
                        for group in range(groups):
                            piece = blocks[half * groups + group][item * SUB : (item + 1) * SUB]
                            shift = ((group - low) * xw) % LANES
                            if shift:
                                piece = pltpu.roll(piece, shift, 1)
                            kept = piece if kept is None else jnp.where(lane // xw == group, piece, kept)
                        grid_ref[pl.ds(item * ny + half * half_rows + low, SUB, stride=folds), :] = kept
        set_field(field_ref.at[plane], grid_ref[plane * width : (plane + 1) * width].T)

    def correlate(step, plane, new):
        term = source_ref[step, plane] * new
        steps[step] = term if steps[step] is None else steps[step] + term
        if plane == FPD - 1:
            turned = steps[step].T
            image_ref[pl.ds(step, ny, stride=depth), :] = (turned[:ny] + turned[ny:]) * scale

    run_steps(taps, depth, field_ref, band_ref, blend_ref, gather, correlate)
    share = ny // (groups * halves) * depth
    for group in range(groups):
        for half in range(halves):
            start = (half * groups + group) * share
            piece = image_ref[start : start + share].astype(BF16)
            for copy in range(copies):
                out_ref[(group * halves + half) * copies + copy] = piece


def vmem():
    return pl.BlockSpec(memory_space=pltpu.VMEM)


def hbm():
    return pl.BlockSpec(memory_space=pltpu.HBM)


def pinned(*arrays):
    return [pltpu.with_memory_space_constraint(array, pltpu.HBM) for array in arrays]


def from_halves(block, halves):
    blocks = [block]
    for turn in range(1, halves):
        blocks.append(lax.ppermute(block, "half", [((to + turn) % halves, to) for to in range(halves)]))
    return blocks


def body(records, source_pattern, wavelet, filters, vel_table, vel_index, freq_plan, counts):
    groups = lax.axis_size("freq")
    halves = lax.axis_size("half")
    copies = lax.axis_size("shot")
    shots, rows, xw, nt = records.shape
    depth = vel_index.shape[0]
    nref, _, taps, _, nbin = filters.shape
    nx = xw * groups
    ny = rows * halves
    items = 2 * FPD
    cap = freq_plan.shape[1]
    cells = rows * xw
    folded = LANES % xw == 0 and cells == SUB * LANES
    bins = pltpu.SMEM((groups * FPD + cap,), jnp.int32)
    params = pltpu.CompilerParams(vmem_limit_bytes=VMEM_BYTES)


    if folded:
        send_shape = (shots, groups, items * SUB, LANES)
    else:
        send_shape = (shots, groups * SUB, cells)
    table = filters.transpose(0, 2, 3, 1, 4)
    dft, own, wave, table = pl.pallas_call(
        functools.partial(prepare_kernel, groups),
        out_shape=[
            jax.ShapeDtypeStruct((groups * SUB, nt), BF16),
            jax.ShapeDtypeStruct((SUB, LANES), jnp.int32),
            jax.ShapeDtypeStruct((SUB, LANES), F32),
            jax.ShapeDtypeStruct(table.shape, BF16),
        ],
        in_specs=[hbm()] * 4,
        out_specs=[vmem()] * 4,
        scratch_shapes=[
            pltpu.SMEM(freq_plan.shape, jnp.int32),
            pltpu.SMEM(counts.shape, jnp.int32),
            pltpu.SMEM((2, nbin), F32),
            bins,
            pltpu.SemaphoreType.DMA((4,)),
        ],
        compiler_params=params,
        cost_estimate=pl.CostEstimate(flops=3 * 10**9, bytes_accessed=4 * 10**6, transcendentals=0),
        name="prepare",
    )(*pinned(freq_plan, counts, wavelet.T, table))
    own, vel_index, source_pattern = lax.optimization_barrier((own, vel_index, source_pattern))
    classes = from_halves(vel_index, halves)
    patterns = from_halves(source_pattern, halves)
    send = pl.pallas_call(
        functools.partial(send_kernel, groups, folded),
        out_shape=jax.ShapeDtypeStruct(send_shape, BF16),
        in_specs=[vmem()] * 2,
        out_specs=vmem(),
        scratch_shapes=[pltpu.VMEM((groups * shots * SUB * SUB + SUB, LANES), F32)],
        compiler_params=params,
        name="send_blocks",
    )(dft, records.reshape(shots, cells, nt))
    if folded:
        send = send.reshape(groups * halves, items * SUB, LANES)
        recv = lax.all_to_all(send, ("half", "freq"), 0, 0, tiled=True)
    else:
        send = send.reshape(shots, groups, SUB, cells)[:, :, :items].swapaxes(0, 1)
        send = send.reshape(groups * halves, items, cells)
        recv = lax.all_to_all(send, ("freq", "half"), 0, 0, tiled=True)
        recv = recv.reshape(groups, halves, items, rows, xw).transpose(2, 1, 3, 0, 4).reshape(items * ny, nx)

    table = table.reshape(nref * taps * taps * 2, nbin)
    band_shape = (FPD, taps * 2 * ny, nref * 2 * ny)
    field = pltpu.VMEM((FPD, nx + 2 * ROW_PAD, 2 * ny), F32)
    band, blend, source = pl.pallas_call(
        functools.partial(source_kernel, taps, nref, depth, halves),
        out_shape=[
            jax.ShapeDtypeStruct(band_shape, BF16),
            jax.ShapeDtypeStruct((depth, nx, 2 * ny), F32),
            jax.ShapeDtypeStruct((depth, FPD, nx, 2 * ny), F32),
        ],
        in_specs=[vmem()] * 3 + [hbm()] * (2 + halves) + [pl.BlockSpec(memory_space=pl.ANY)] * (halves - 1),
        out_specs=[vmem()] * 3,
        scratch_shapes=[
            pltpu.VMEM((halves,) + vel_index.shape, jnp.int32),
            pltpu.VMEM((halves,) + source_pattern.shape, BF16),
            pltpu.VMEM((1,) + vel_table.shape, F32),
            pltpu.VMEM((FPD, (table.shape[0] + 2 * taps + SUB) // SUB * SUB + 2 * SUB, LANES), F32),
            pltpu.VMEM((depth + 1, ny, nx), F32),
            pltpu.VMEM((SUB, LANES), F32),
            field,
            pltpu.SemaphoreType.DMA((1 + 2 * halves,)),
        ],
        compiler_params=params,
        cost_estimate=pl.CostEstimate(flops=4 * 10**9, bytes_accessed=10**7, transcendentals=0),
        name="source_fields",
    )(own, wave, table, *pinned(vel_table[None], *classes, patterns[0]), *patterns[1:])

    scale = 1.0 / math.sqrt(FPD * groups * shots * copies)
    share = ny // (groups * halves)
    terms = pl.pallas_call(
        functools.partial(migrate_kernel, (groups, halves, copies, xw, taps, scale, folded)),
        out_shape=jax.ShapeDtypeStruct((groups * halves * copies, share * depth, nx), BF16),
        in_specs=[vmem()] * 4,
        out_specs=vmem(),
        scratch_shapes=[
            pltpu.VMEM((items * ny + SUB, nx), F32),
            field,
            pltpu.VMEM((ny * depth + SUB, nx), F32),
        ],
        compiler_params=params,
        name="migrate",
    )(recv, band, blend, source)
    terms = lax.all_to_all(terms, ("freq", "half", "shot"), 0, 0, tiled=True)
    return jnp.sum(terms.astype(F32), axis=0).reshape(1, share, depth, nx)


def solution(mesh):
    return jax.shard_map(
        body,
        mesh=mesh,
        in_specs=(
            P(("group", "shot"), "half", "freq", None),
            P(("group", "shot"), "half", None),
            P(),
            P(),
            P(),
            P("group", "half", None),
            P(),
            P(),
        ),
        out_specs=P("half", "freq", "group", None),
        check_vma=False,
    )
```

```python
import functools
import math

import jax
import jax.numpy as jnp
from jax import lax
from jax.experimental import pallas as pl
from jax.experimental.pallas import tpu as pltpu
from jax.sharding import PartitionSpec as P

FPD = 3
LANES = 128
SUB = 8
ROW_PAD = 8
VMEM_BYTES = 40 * 1024 * 1024
BF16 = jnp.bfloat16
F32 = jnp.float32


def list_bins(plan_ref, counts_ref, bins_ref):
    groups, cap = plan_ref.shape
    start = jnp.int32(0)
    for holder in range(groups):
        for slot in range(cap):
            bins_ref[start + slot] = plan_ref[holder, slot]
        start = start + counts_ref[holder]


def lane_iota(shape):
    return lax.broadcasted_iota(jnp.int32, shape, len(shape) - 1)


def row_iota(shape):
    return lax.broadcasted_iota(jnp.int32, shape, 0)


def dft_rows(bins_ref, group, nt):
    shape = (SUB, nt)
    row = row_iota(shape)
    bin_id = jnp.zeros(shape, jnp.int32)
    for slot in range(FPD):
        bin_id = jnp.where(row // 2 == slot, bins_ref[group * FPD + slot], bin_id)
    phase = bin_id * lane_iota(shape)
    phase = lax.rem(phase, jnp.int32(nt)) if nt & (nt - 1) else phase & (nt - 1)
    quarter = nt // 4
    turn = (phase + quarter // 2) // quarter
    angle = (phase - turn * quarter).astype(F32) * (2.0 * math.pi / nt)
    turn = (turn + (row & 1)) & 3
    sq = angle * angle
    cos = 1.0 + sq * (-1.0 / 2 + sq * (1.0 / 24 + sq * (-1.0 / 720 + sq * (1.0 / 40320))))
    sin = angle * (1.0 + sq * (-1.0 / 6 + sq * (1.0 / 120 + sq * (-1.0 / 5040 + sq * (1.0 / 362880)))))
    value = jnp.where((turn & 1) == 1, sin, cos)
    value = jnp.where(((turn + 1) & 2) == 2, -value, value)
    return value * (1.0 / math.sqrt(nt))


def transform(dft, block):
    return lax.dot_general(dft, block, (((1,), (1,)), ((), ())), preferred_element_type=F32)


def prepare_kernel(
    groups, plan_hbm, counts_hbm, wav_hbm, dft_ref, own_ref, wave_ref,
    plan_ref, counts_ref, wav_ref, bins_ref, sems,
):
    nt = dft_ref.shape[1]
    small = [
        pltpu.make_async_copy(plan_hbm, plan_ref, sems.at[0]),
        pltpu.make_async_copy(counts_hbm, counts_ref, sems.at[1]),
        pltpu.make_async_copy(wav_hbm, wav_ref, sems.at[2]),
    ]
    for copy in small:
        copy.start()
    for copy in small:
        copy.wait()
    list_bins(plan_ref, counts_ref, bins_ref)
    for pair in range(0, groups, 2):
        both = [dft_rows(bins_ref, group, nt) for group in range(pair, min(pair + 2, groups))]
        dft_ref[pair * SUB : (pair + len(both)) * SUB] = jnp.concatenate(both, axis=0).astype(BF16)
    first = lax.axis_index("freq") * FPD
    lane = lane_iota((1, LANES))
    for plane in range(FPD):
        bin_id = bins_ref[first + plane]
        own_ref[plane : plane + 1] = jnp.full((1, LANES), bin_id, jnp.int32)
        wave_ref[plane : plane + 1] = jnp.where(lane < LANES // 2, wav_ref[0, bin_id], wav_ref[1, bin_id])


def send_kernel(groups, folded, dft_ref, rec_ref, out_ref, tmp_ref):
    shots, cells, _ = rec_ref.shape
    dft = dft_ref[...]
    for shot in range(shots):
        out = transform(dft, rec_ref[shot])
        if not folded:
            out_ref[shot] = out.astype(BF16)
            continue
        for group in range(groups):
            base = (group * shots + shot) * SUB * SUB
            for high in range(SUB):
                tmp_ref[pl.ds(base + high, SUB, stride=SUB), :] = out[
                    group * SUB : (group + 1) * SUB, high * LANES : (high + 1) * LANES
                ]
            out_ref[shot, group] = tmp_ref[base : base + 2 * FPD * SUB].astype(BF16)


def make_bands(taps, nref, ny, picked_ref, band_ref):
    reach = taps // 2
    width = 2 * ny
    lane = lane_iota((taps, width))
    full_lane = lane_iota((ny, width))
    keep = jnp.abs((full_lane & (ny - 1)) - row_iota((ny, width))) <= reach
    sign = jnp.where((lane < ny // 2) | (lane >= ny + ny // 2), -1.0, 1.0)
    for ref in range(nref):
        base = jnp.zeros((taps, width), F32)
        for part in range(2):
            for tap in range(taps):
                value = picked_ref[pl.ds((ref * taps + tap) * taps * 2 + part, taps, stride=2), :]
                base = jnp.where(lane == (part * ny + reach - tap) % width, value, base)
        turned = pltpu.roll(base, ny, 1) * sign
        for col_tap in range(taps):
            for part, rows in enumerate((base, turned)):
                spread = jnp.broadcast_to(rows[col_tap : col_tap + 1], (ny, width))
                band = pltpu.roll(spread, 0, 1, stride=1, stride_axis=0)
                band = jnp.where(keep, band, 0.0).astype(BF16)
                at = col_tap * width + part * ny
                band_ref[at : at + ny, ref * width : (ref + 1) * width] = band


def set_field(field_ref, value):
    rows, width = value.shape
    field_ref[:ROW_PAD] = jnp.zeros((ROW_PAD, width), F32)
    field_ref[ROW_PAD : ROW_PAD + rows] = value
    field_ref[ROW_PAD + rows :] = jnp.zeros((ROW_PAD, width), F32)


def shifted(taps, field_ref):
    first = ROW_PAD - taps // 2
    rows = field_ref.shape[0] - 2 * ROW_PAD
    pieces = [field_ref[pl.ds(first + tap, rows), :].astype(BF16) for tap in range(taps)]
    return jnp.concatenate(pieces, axis=1)


def advance(left, band_ref, blend):
    width = blend.shape[1]
    both = jnp.dot(left, band_ref[...], preferred_element_type=F32)
    low, high = both[:, :width], both[:, width:]
    return (low + blend * (high - low)).astype(BF16).astype(F32)


def run_steps(taps, depth, field_ref, band_ref, blend_ref, prepare, use):
    rows = field_ref.shape[1] - 2 * ROW_PAD
    order = [(step, plane) for step in range(depth) for plane in range(FPD)]
    prepare(0)
    left = shifted(taps, field_ref.at[0])
    for at, (step, plane) in enumerate(order):
        follow = None
        if at + 1 < len(order):
            after = order[at + 1][1]
            if order[at + 1][0] == 0:
                prepare(after)
            follow = shifted(taps, field_ref.at[after])
        new = advance(left, band_ref.at[plane], blend_ref[step])
        if step + 1 < depth:
            field_ref[plane, ROW_PAD : ROW_PAD + rows] = new
        use(step, plane, new)
        left = follow


def source_kernel(taps, nref, depth, halves, own_ref, wave_ref, filt_ref, table_hbm, *refs):
    class_hbm, refs = refs[:halves], refs[halves:]
    pattern_hbm, refs = refs[:halves], refs[halves:]
    band_ref, blend_ref, source_ref, class_refs, pattern_refs, table_ref, picked_ref, grid_ref, tab_ref, field_ref, sems = refs
    copies = [pltpu.make_async_copy(table_hbm, table_ref, sems.at[0])]
    for turn in range(halves):
        copies.append(pltpu.make_async_copy(class_hbm[turn], class_refs.at[turn], sems.at[1 + 2 * turn]))
        copies.append(pltpu.make_async_copy(pattern_hbm[turn], pattern_refs.at[turn], sems.at[2 + 2 * turn]))
    for copy in copies:
        copy.start()
    mine = lax.axis_index("half")
    rows = class_hbm[0].shape[1]
    ny, nx = grid_ref.shape[1:]
    nbin = filt_ref.shape[1]
    for plane in range(FPD):
        hot = jnp.where(row_iota((nbin, LANES)) == own_ref[plane : plane + 1], 1.0, 0.0).astype(BF16)
        picked_ref[plane, : filt_ref.shape[0]] = jnp.dot(filt_ref[...], hot, preferred_element_type=F32)
    for plane in range(FPD - 1):
        make_bands(taps, nref, ny, picked_ref.at[plane], band_ref.at[plane])
    for copy in copies:
        copy.wait()
    for turn in range(halves):
        at = pl.ds(pl.multiple_of(lax.rem(mine + turn, halves) * rows, rows), rows)
        for step in range(depth):
            grid_ref[step, at, :] = class_refs[turn, step].astype(F32)
        grid_ref[depth, at, :] = pattern_refs[turn, mine].astype(F32)
    tab_ref[:, : table_ref.shape[1]] = jnp.broadcast_to(table_ref[...], (SUB, table_ref.shape[1]))
    for step in range(depth):
        pieces = []
        for row in range(0, ny, SUB):
            index = grid_ref[step, row : row + SUB].astype(jnp.int32)
            pieces.append(jnp.take_along_axis(tab_ref[...], index, axis=1))
        blend_ref[step] = jnp.concatenate(pieces + pieces, axis=0).T
    pattern = grid_ref[depth]
    pattern = jnp.concatenate([pattern, pattern], axis=0).T
    make_bands(taps, nref, ny, picked_ref.at[FPD - 1], band_ref.at[FPD - 1])

    def start(plane):
        set_field(field_ref.at[plane], (pattern * wave_ref[plane : plane + 1]).astype(BF16).astype(F32))

    def keep(step, plane, new):
        source_ref[step, plane] = new

    run_steps(taps, depth, field_ref, band_ref, blend_ref, start, keep)


def migrate_kernel(dims, recv_ref, band_ref, blend_ref, source_ref, out_ref, grid_ref, field_ref, image_ref):
    groups, halves, copies, xw, taps, scale, folded = dims
    depth, nx, width = blend_ref.shape
    ny = width // 2
    if folded:
        folds = LANES // xw
        half_rows = ny // halves
        lane = lane_iota((SUB, LANES))
        blocks = [recv_ref[block].astype(F32) for block in range(groups * halves)]
    else:
        grid_ref[: recv_ref.shape[0]] = recv_ref[...].astype(F32)
    steps = [None] * depth

    def gather(plane):
        if folded:
            for half in range(halves):
                for item in range(2 * plane, 2 * plane + 2):
                    for low in range(folds):
                        kept = None
                        for group in range(groups):
                            piece = blocks[half * groups + group][item * SUB : (item + 1) * SUB]
                            shift = ((group - low) * xw) % LANES
                            if shift:
                                piece = pltpu.roll(piece, shift, 1)
                            kept = piece if kept is None else jnp.where(lane // xw == group, piece, kept)
                        grid_ref[pl.ds(item * ny + half * half_rows + low, SUB, stride=folds), :] = kept
        set_field(field_ref.at[plane], grid_ref[plane * width : (plane + 1) * width].T)

    def correlate(step, plane, new):
        term = source_ref[step, plane] * new
        steps[step] = term if steps[step] is None else steps[step] + term
        if plane == FPD - 1:
            turned = steps[step].T
            image_ref[pl.ds(step, ny, stride=depth), :] = (turned[:ny] + turned[ny:]) * scale

    run_steps(taps, depth, field_ref, band_ref, blend_ref, gather, correlate)
    share = ny // (groups * halves) * depth
    for group in range(groups):
        for half in range(halves):
            start = (half * groups + group) * share
            piece = image_ref[start : start + share].astype(BF16)
            for copy in range(copies):
                out_ref[(group * halves + half) * copies + copy] = piece


def vmem():
    return pl.BlockSpec(memory_space=pltpu.VMEM)


def hbm():
    return pl.BlockSpec(memory_space=pltpu.HBM)


def pinned(*arrays):
    return [pltpu.with_memory_space_constraint(array, pltpu.HBM) for array in arrays]


def from_halves(block, halves):
    blocks = [block]
    for turn in range(1, halves):
        blocks.append(lax.ppermute(block, "half", [((to + turn) % halves, to) for to in range(halves)]))
    return blocks


def body(records, source_pattern, wavelet, filters, vel_table, vel_index, freq_plan, counts):
    groups = lax.axis_size("freq")
    halves = lax.axis_size("half")
    copies = lax.axis_size("shot")
    shots, rows, xw, nt = records.shape
    depth = vel_index.shape[0]
    nref, _, taps, _, nbin = filters.shape
    nx = xw * groups
    ny = rows * halves
    items = 2 * FPD
    cap = freq_plan.shape[1]
    cells = rows * xw
    folded = LANES % xw == 0 and cells == SUB * LANES
    bins = pltpu.SMEM((groups * FPD + cap,), jnp.int32)
    params = pltpu.CompilerParams(vmem_limit_bytes=VMEM_BYTES)


    if folded:
        send_shape = (shots, groups, items * SUB, LANES)
    else:
        send_shape = (shots, groups * SUB, cells)
    table = filters.transpose(0, 2, 3, 1, 4)
    dft, own, wave = pl.pallas_call(
        functools.partial(prepare_kernel, groups),
        out_shape=[
            jax.ShapeDtypeStruct((groups * SUB, nt), BF16),
            jax.ShapeDtypeStruct((SUB, LANES), jnp.int32),
            jax.ShapeDtypeStruct((SUB, LANES), F32),
        ],
        in_specs=[hbm()] * 3,
        out_specs=[vmem()] * 3,
        scratch_shapes=[
            pltpu.SMEM(freq_plan.shape, jnp.int32),
            pltpu.SMEM(counts.shape, jnp.int32),
            pltpu.SMEM((2, nbin), F32),
            bins,
            pltpu.SemaphoreType.DMA((3,)),
        ],
        compiler_params=params,
        cost_estimate=pl.CostEstimate(flops=3 * 10**9, bytes_accessed=4 * 10**6, transcendentals=0),
        name="prepare",
    )(*pinned(freq_plan, counts, wavelet.T))
    own, vel_index, source_pattern = lax.optimization_barrier((own, vel_index, source_pattern))
    classes = from_halves(vel_index, halves)
    patterns = from_halves(source_pattern, halves)
    send = pl.pallas_call(
        functools.partial(send_kernel, groups, folded),
        out_shape=jax.ShapeDtypeStruct(send_shape, BF16),
        in_specs=[vmem()] * 2,
        out_specs=vmem(),
        scratch_shapes=[pltpu.VMEM((groups * shots * SUB * SUB + SUB, LANES), F32)],
        compiler_params=params,
        name="send_blocks",
    )(dft, records.reshape(shots, cells, nt))
    if folded:
        send = send.reshape(groups * halves, items * SUB, LANES)
        recv = lax.all_to_all(send, ("half", "freq"), 0, 0, tiled=True)
    else:
        send = send.reshape(shots, groups, SUB, cells)[:, :, :items].swapaxes(0, 1)
        send = send.reshape(groups * halves, items, cells)
        recv = lax.all_to_all(send, ("freq", "half"), 0, 0, tiled=True)
        recv = recv.reshape(groups, halves, items, rows, xw).transpose(2, 1, 3, 0, 4).reshape(items * ny, nx)

    table = table.reshape(nref * taps * taps * 2, nbin)
    band_shape = (FPD, taps * 2 * ny, nref * 2 * ny)
    field = pltpu.VMEM((FPD, nx + 2 * ROW_PAD, 2 * ny), F32)
    band, blend, source = pl.pallas_call(
        functools.partial(source_kernel, taps, nref, depth, halves),
        out_shape=[
            jax.ShapeDtypeStruct(band_shape, BF16),
            jax.ShapeDtypeStruct((depth, nx, 2 * ny), F32),
            jax.ShapeDtypeStruct((depth, FPD, nx, 2 * ny), F32),
        ],
        in_specs=[vmem()] * 3 + [hbm()] * (2 + halves) + [pl.BlockSpec(memory_space=pl.ANY)] * (halves - 1),
        out_specs=[vmem()] * 3,
        scratch_shapes=[
            pltpu.VMEM((halves,) + vel_index.shape, jnp.int32),
            pltpu.VMEM((halves,) + source_pattern.shape, BF16),
            pltpu.VMEM((1,) + vel_table.shape, F32),
            pltpu.VMEM((FPD, (table.shape[0] + 2 * taps + SUB) // SUB * SUB + 2 * SUB, LANES), F32),
            pltpu.VMEM((depth + 1, ny, nx), F32),
            pltpu.VMEM((SUB, LANES), F32),
            field,
            pltpu.SemaphoreType.DMA((1 + 2 * halves,)),
        ],
        compiler_params=params,
        cost_estimate=pl.CostEstimate(flops=4 * 10**9, bytes_accessed=10**7, transcendentals=0),
        name="source_fields",
    )(own, wave, table, *pinned(vel_table[None], *classes, patterns[0]), *patterns[1:])

    scale = 1.0 / math.sqrt(FPD * groups * shots * copies)
    share = ny // (groups * halves)
    terms = pl.pallas_call(
        functools.partial(migrate_kernel, (groups, halves, copies, xw, taps, scale, folded)),
        out_shape=jax.ShapeDtypeStruct((groups * halves * copies, share * depth, nx), BF16),
        in_specs=[vmem()] * 4,
        out_specs=vmem(),
        scratch_shapes=[
            pltpu.VMEM((items * ny + SUB, nx), F32),
            field,
            pltpu.VMEM((ny * depth + SUB, nx), F32),
        ],
        compiler_params=params,
        name="migrate",
    )(recv, band, blend, source)
    terms = lax.all_to_all(terms, ("freq", "half", "shot"), 0, 0, tiled=True)
    return jnp.sum(terms.astype(F32), axis=0).reshape(1, share, depth, nx)


def solution(mesh):
    return jax.shard_map(
        body,
        mesh=mesh,
        in_specs=(
            P(("group", "shot"), "half", "freq", None),
            P(("group", "shot"), "half", None),
            P(),
            P(),
            P(),
            P("group", "half", None),
            P(),
            P(),
        ),
        out_specs=P("half", "freq", "group", None),
        check_vma=False,
    )
```

```python
import functools
import math

import jax
import jax.numpy as jnp
from jax import lax
from jax.experimental import pallas as pl
from jax.experimental.pallas import tpu as pltpu
from jax.sharding import PartitionSpec as P

FPD = 3
LANES = 128
SUB = 8
ROW_PAD = 8
VMEM_BYTES = 40 * 1024 * 1024
BF16 = jnp.bfloat16
F32 = jnp.float32


def list_bins(plan_ref, counts_ref, bins_ref):
    groups, cap = plan_ref.shape
    start = jnp.int32(0)
    for holder in range(groups):
        for slot in range(cap):
            bins_ref[start + slot] = plan_ref[holder, slot]
        start = start + counts_ref[holder]


def lane_iota(shape):
    return lax.broadcasted_iota(jnp.int32, shape, len(shape) - 1)


def row_iota(shape):
    return lax.broadcasted_iota(jnp.int32, shape, 0)


def dft_rows(bins_ref, group, nt):
    shape = (SUB, nt)
    row = row_iota(shape)
    bin_id = jnp.zeros(shape, jnp.int32)
    for slot in range(FPD):
        bin_id = jnp.where(row // 2 == slot, bins_ref[group * FPD + slot], bin_id)
    phase = bin_id * lane_iota(shape)
    phase = lax.rem(phase, jnp.int32(nt)) if nt & (nt - 1) else phase & (nt - 1)
    quarter = nt // 4
    turn = (phase + quarter // 2) // quarter
    angle = (phase - turn * quarter).astype(F32) * (2.0 * math.pi / nt)
    turn = (turn + (row & 1)) & 3
    sq = angle * angle
    cos = 1.0 + sq * (-1.0 / 2 + sq * (1.0 / 24 + sq * (-1.0 / 720 + sq * (1.0 / 40320))))
    sin = angle * (1.0 + sq * (-1.0 / 6 + sq * (1.0 / 120 + sq * (-1.0 / 5040 + sq * (1.0 / 362880)))))
    value = jnp.where((turn & 1) == 1, sin, cos)
    value = jnp.where(((turn + 1) & 2) == 2, -value, value)
    return value * (1.0 / math.sqrt(nt))


def transform(dft, block):
    return lax.dot_general(dft, block, (((1,), (1,)), ((), ())), preferred_element_type=F32)


def put_spectra(groups, folded, out, put, tmp_ref):
    if not folded:
        put[...] = out.astype(BF16)
        return
    for group in range(groups):
        base = group * SUB * SUB
        for high in range(SUB):
            tmp_ref[pl.ds(base + high, SUB, stride=SUB), :] = out[
                group * SUB : (group + 1) * SUB, high * LANES : (high + 1) * LANES
            ]
        put[group] = tmp_ref[base : base + 2 * FPD * SUB].astype(BF16)


def prepare_kernel(
    groups, folded, plan_hbm, counts_hbm, wav_hbm, rec_hbm, dft_ref, own_ref, wave_ref, early_ref, last_ref,
    plan_ref, counts_ref, wav_ref, bins_ref, rec_ref, tmp_ref, sems,
):
    nt = dft_ref.shape[1]
    shots = rec_hbm.shape[0]
    small = [
        pltpu.make_async_copy(plan_hbm, plan_ref, sems.at[0]),
        pltpu.make_async_copy(counts_hbm, counts_ref, sems.at[1]),
        pltpu.make_async_copy(wav_hbm, wav_ref, sems.at[2]),
    ]
    records = [
        pltpu.make_async_copy(rec_hbm.at[shot], rec_ref.at[shot] if shot < shots - 1 else last_ref, sems.at[3 + shot])
        for shot in range(shots)
    ]
    for copy in small + records:
        copy.start()
    for copy in small:
        copy.wait()
    list_bins(plan_ref, counts_ref, bins_ref)
    for pair in range(0, groups, 2):
        both = [dft_rows(bins_ref, group, nt) for group in range(pair, min(pair + 2, groups))]
        dft_ref[pair * SUB : (pair + len(both)) * SUB] = jnp.concatenate(both, axis=0).astype(BF16)
    first = lax.axis_index("freq") * FPD
    lane = lane_iota((1, LANES))
    for plane in range(FPD):
        bin_id = bins_ref[first + plane]
        own_ref[plane : plane + 1] = jnp.full((1, LANES), bin_id, jnp.int32)
        wave_ref[plane : plane + 1] = jnp.where(lane < LANES // 2, wav_ref[0, bin_id], wav_ref[1, bin_id])
    for shot in range(shots - 1):
        records[shot].wait()
        put_spectra(groups, folded, transform(dft_ref[...], rec_ref[shot]), early_ref.at[shot], tmp_ref)
    records[shots - 1].wait()


def send_kernel(groups, folded, dft_ref, early_ref, last_ref, out_ref, tmp_ref):
    early = early_ref.shape[0]
    out = transform(dft_ref[...], last_ref[...])
    for shot in range(early):
        out_ref[shot] = early_ref[shot]
    put_spectra(groups, folded, out, out_ref.at[early], tmp_ref)


def make_bands(taps, nref, ny, picked_ref, band_ref):
    reach = taps // 2
    width = 2 * ny
    lane = lane_iota((taps, width))
    full_lane = lane_iota((ny, width))
    keep = jnp.abs((full_lane & (ny - 1)) - row_iota((ny, width))) <= reach
    sign = jnp.where((lane < ny // 2) | (lane >= ny + ny // 2), -1.0, 1.0)
    for ref in range(nref):
        base = jnp.zeros((taps, width), F32)
        for part in range(2):
            for tap in range(taps):
                value = picked_ref[pl.ds((ref * taps + tap) * taps * 2 + part, taps, stride=2), :]
                base = jnp.where(lane == (part * ny + reach - tap) % width, value, base)
        turned = pltpu.roll(base, ny, 1) * sign
        for col_tap in range(taps):
            for part, rows in enumerate((base, turned)):
                spread = jnp.broadcast_to(rows[col_tap : col_tap + 1], (ny, width))
                band = pltpu.roll(spread, 0, 1, stride=1, stride_axis=0)
                band = jnp.where(keep, band, 0.0).astype(BF16)
                at = col_tap * width + part * ny
                band_ref[at : at + ny, ref * width : (ref + 1) * width] = band


def set_field(field_ref, value):
    rows, width = value.shape
    field_ref[:ROW_PAD] = jnp.zeros((ROW_PAD, width), F32)
    field_ref[ROW_PAD : ROW_PAD + rows] = value
    field_ref[ROW_PAD + rows :] = jnp.zeros((ROW_PAD, width), F32)


def shifted(taps, field_ref):
    first = ROW_PAD - taps // 2
    rows = field_ref.shape[0] - 2 * ROW_PAD
    pieces = [field_ref[pl.ds(first + tap, rows), :].astype(BF16) for tap in range(taps)]
    return jnp.concatenate(pieces, axis=1)


def advance(left, band_ref, blend):
    width = blend.shape[1]
    both = jnp.dot(left, band_ref[...], preferred_element_type=F32)
    low, high = both[:, :width], both[:, width:]
    return (low + blend * (high - low)).astype(BF16).astype(F32)


def run_steps(taps, depth, field_ref, band_ref, blend_ref, prepare, use):
    rows = field_ref.shape[1] - 2 * ROW_PAD
    order = [(step, plane) for step in range(depth) for plane in range(FPD)]
    prepare(0)
    left = shifted(taps, field_ref.at[0])
    for at, (step, plane) in enumerate(order):
        follow = None
        if at + 1 < len(order):
            after = order[at + 1][1]
            if order[at + 1][0] == 0:
                prepare(after)
            follow = shifted(taps, field_ref.at[after])
        new = advance(left, band_ref.at[plane], blend_ref[step])
        if step + 1 < depth:
            field_ref[plane, ROW_PAD : ROW_PAD + rows] = new
        use(step, plane, new)
        left = follow


def source_kernel(taps, nref, depth, halves, own_ref, wave_ref, filt_ref, table_hbm, *refs):
    class_hbm, refs = refs[:halves], refs[halves:]
    pattern_hbm, refs = refs[:halves], refs[halves:]
    band_ref, blend_ref, source_ref, class_refs, pattern_refs, table_ref, picked_ref, grid_ref, tab_ref, field_ref, sems = refs
    copies = [pltpu.make_async_copy(table_hbm, table_ref, sems.at[0])]
    for turn in range(halves):
        copies.append(pltpu.make_async_copy(class_hbm[turn], class_refs.at[turn], sems.at[1 + 2 * turn]))
        copies.append(pltpu.make_async_copy(pattern_hbm[turn], pattern_refs.at[turn], sems.at[2 + 2 * turn]))
    for copy in copies:
        copy.start()
    mine = lax.axis_index("half")
    rows = class_hbm[0].shape[1]
    ny, nx = grid_ref.shape[1:]
    nbin = filt_ref.shape[1]
    for plane in range(FPD):
        hot = jnp.where(row_iota((nbin, LANES)) == own_ref[plane : plane + 1], 1.0, 0.0).astype(BF16)
        picked_ref[plane, : filt_ref.shape[0]] = jnp.dot(filt_ref[...], hot, preferred_element_type=F32)
    for plane in range(FPD - 1):
        make_bands(taps, nref, ny, picked_ref.at[plane], band_ref.at[plane])
    for copy in copies:
        copy.wait()
    for turn in range(halves):
        at = pl.ds(pl.multiple_of(lax.rem(mine + turn, halves) * rows, rows), rows)
        for step in range(depth):
            grid_ref[step, at, :] = class_refs[turn, step].astype(F32)
        grid_ref[depth, at, :] = pattern_refs[turn, mine].astype(F32)
    tab_ref[:, : table_ref.shape[1]] = jnp.broadcast_to(table_ref[...], (SUB, table_ref.shape[1]))
    for step in range(depth):
        pieces = []
        for row in range(0, ny, SUB):
            index = grid_ref[step, row : row + SUB].astype(jnp.int32)
            pieces.append(jnp.take_along_axis(tab_ref[...], index, axis=1))
        blend_ref[step] = jnp.concatenate(pieces + pieces, axis=0).T
    pattern = grid_ref[depth]
    pattern = jnp.concatenate([pattern, pattern], axis=0).T
    make_bands(taps, nref, ny, picked_ref.at[FPD - 1], band_ref.at[FPD - 1])

    def start(plane):
        set_field(field_ref.at[plane], (pattern * wave_ref[plane : plane + 1]).astype(BF16).astype(F32))

    def keep(step, plane, new):
        source_ref[step, plane] = new

    run_steps(taps, depth, field_ref, band_ref, blend_ref, start, keep)


def migrate_kernel(dims, recv_ref, band_ref, blend_ref, source_ref, out_ref, grid_ref, field_ref, image_ref):
    groups, halves, copies, xw, taps, scale, folded = dims
    depth, nx, width = blend_ref.shape
    ny = width // 2
    if folded:
        folds = LANES // xw
        half_rows = ny // halves
        lane = lane_iota((SUB, LANES))
        blocks = [recv_ref[block].astype(F32) for block in range(groups * halves)]
    else:
        grid_ref[: recv_ref.shape[0]] = recv_ref[...].astype(F32)
    steps = [None] * depth

    def gather(plane):
        if folded:
            for half in range(halves):
                for item in range(2 * plane, 2 * plane + 2):
                    for low in range(folds):
                        kept = None
                        for group in range(groups):
                            piece = blocks[half * groups + group][item * SUB : (item + 1) * SUB]
                            shift = ((group - low) * xw) % LANES
                            if shift:
                                piece = pltpu.roll(piece, shift, 1)
                            kept = piece if kept is None else jnp.where(lane // xw == group, piece, kept)
                        grid_ref[pl.ds(item * ny + half * half_rows + low, SUB, stride=folds), :] = kept
        set_field(field_ref.at[plane], grid_ref[plane * width : (plane + 1) * width].T)

    def correlate(step, plane, new):
        term = source_ref[step, plane] * new
        steps[step] = term if steps[step] is None else steps[step] + term
        if plane == FPD - 1:
            turned = steps[step].T
            image_ref[pl.ds(step, ny, stride=depth), :] = (turned[:ny] + turned[ny:]) * scale

    run_steps(taps, depth, field_ref, band_ref, blend_ref, gather, correlate)
    share = ny // (groups * halves) * depth
    for group in range(groups):
        for half in range(halves):
            start = (half * groups + group) * share
            piece = image_ref[start : start + share].astype(BF16)
            for copy in range(copies):
                out_ref[(group * halves + half) * copies + copy] = piece


def vmem():
    return pl.BlockSpec(memory_space=pltpu.VMEM)


def hbm():
    return pl.BlockSpec(memory_space=pltpu.HBM)


def pinned(*arrays):
    return [pltpu.with_memory_space_constraint(array, pltpu.HBM) for array in arrays]


def from_halves(block, halves):
    blocks = [block]
    for turn in range(1, halves):
        blocks.append(lax.ppermute(block, "half", [((to + turn) % halves, to) for to in range(halves)]))
    return blocks


def body(records, source_pattern, wavelet, filters, vel_table, vel_index, freq_plan, counts):
    groups = lax.axis_size("freq")
    halves = lax.axis_size("half")
    copies = lax.axis_size("shot")
    shots, rows, xw, nt = records.shape
    depth = vel_index.shape[0]
    nref, _, taps, _, nbin = filters.shape
    nx = xw * groups
    ny = rows * halves
    items = 2 * FPD
    cap = freq_plan.shape[1]
    cells = rows * xw
    folded = LANES % xw == 0 and cells == SUB * LANES
    bins = pltpu.SMEM((groups * FPD + cap,), jnp.int32)
    params = pltpu.CompilerParams(vmem_limit_bytes=VMEM_BYTES)


    if folded:
        send_shape = (shots, groups, items * SUB, LANES)
    else:
        send_shape = (shots, groups * SUB, cells)
    table = filters.transpose(0, 2, 3, 1, 4)
    classes = from_halves(vel_index, halves)
    tmp = pltpu.VMEM((groups * SUB * SUB + SUB, LANES), F32)
    dft, own, wave, early, last = pl.pallas_call(
        functools.partial(prepare_kernel, groups, folded),
        out_shape=[
            jax.ShapeDtypeStruct((groups * SUB, nt), BF16),
            jax.ShapeDtypeStruct((SUB, LANES), jnp.int32),
            jax.ShapeDtypeStruct((SUB, LANES), F32),
            jax.ShapeDtypeStruct((shots - 1,) + send_shape[1:], BF16),
            jax.ShapeDtypeStruct((cells, nt), BF16),
        ],
        in_specs=[hbm()] * 4,
        out_specs=[vmem()] * 5,
        scratch_shapes=[
            pltpu.SMEM(freq_plan.shape, jnp.int32),
            pltpu.SMEM(counts.shape, jnp.int32),
            pltpu.SMEM((2, nbin), F32),
            bins,
            pltpu.VMEM((shots - 1, cells, nt), BF16),
            tmp,
            pltpu.SemaphoreType.DMA((3 + shots,)),
        ],
        compiler_params=params,
        cost_estimate=pl.CostEstimate(flops=2 * 10**9, bytes_accessed=4 * 10**6, transcendentals=0),
        name="prepare",
    )(*pinned(freq_plan, counts, wavelet.T, records.reshape(shots, cells, nt)))
    own, source_pattern = lax.optimization_barrier((own, source_pattern))
    patterns = from_halves(source_pattern, halves)
    send = pl.pallas_call(
        functools.partial(send_kernel, groups, folded),
        out_shape=jax.ShapeDtypeStruct(send_shape, BF16),
        in_specs=[vmem()] * 3,
        out_specs=vmem(),
        scratch_shapes=[tmp],
        compiler_params=params,
        name="send_blocks",
    )(dft, early, last)
    if folded:
        send = send.reshape(groups * halves, items * SUB, LANES)
        recv = lax.all_to_all(send, ("half", "freq"), 0, 0, tiled=True)
    else:
        send = send.reshape(shots, groups, SUB, cells)[:, :, :items].swapaxes(0, 1)
        send = send.reshape(groups * halves, items, cells)
        recv = lax.all_to_all(send, ("freq", "half"), 0, 0, tiled=True)
        recv = recv.reshape(groups, halves, items, rows, xw).transpose(2, 1, 3, 0, 4).reshape(items * ny, nx)

    table = table.reshape(nref * taps * taps * 2, nbin)
    band_shape = (FPD, taps * 2 * ny, nref * 2 * ny)
    field = pltpu.VMEM((FPD, nx + 2 * ROW_PAD, 2 * ny), F32)
    band, blend, source = pl.pallas_call(
        functools.partial(source_kernel, taps, nref, depth, halves),
        out_shape=[
            jax.ShapeDtypeStruct(band_shape, BF16),
            jax.ShapeDtypeStruct((depth, nx, 2 * ny), F32),
            jax.ShapeDtypeStruct((depth, FPD, nx, 2 * ny), F32),
        ],
        in_specs=[vmem()] * 3 + [hbm()] * (2 + halves) + [pl.BlockSpec(memory_space=pl.ANY)] * (halves - 1),
        out_specs=[vmem()] * 3,
        scratch_shapes=[
            pltpu.VMEM((halves,) + vel_index.shape, jnp.int32),
            pltpu.VMEM((halves,) + source_pattern.shape, BF16),
            pltpu.VMEM((1,) + vel_table.shape, F32),
            pltpu.VMEM((FPD, (table.shape[0] + 2 * taps + SUB) // SUB * SUB + 2 * SUB, LANES), F32),
            pltpu.VMEM((depth + 1, ny, nx), F32),
            pltpu.VMEM((SUB, LANES), F32),
            field,
            pltpu.SemaphoreType.DMA((1 + 2 * halves,)),
        ],
        compiler_params=params,
        cost_estimate=pl.CostEstimate(flops=4 * 10**9, bytes_accessed=10**7, transcendentals=0),
        name="source_fields",
    )(own, wave, table, *pinned(vel_table[None], *classes, patterns[0]), *patterns[1:])

    scale = 1.0 / math.sqrt(FPD * groups * shots * copies)
    share = ny // (groups * halves)
    terms = pl.pallas_call(
        functools.partial(migrate_kernel, (groups, halves, copies, xw, taps, scale, folded)),
        out_shape=jax.ShapeDtypeStruct((groups * halves * copies, share * depth, nx), BF16),
        in_specs=[vmem()] * 4,
        out_specs=vmem(),
        scratch_shapes=[
            pltpu.VMEM((items * ny + SUB, nx), F32),
            field,
            pltpu.VMEM((ny * depth + SUB, nx), F32),
        ],
        compiler_params=params,
        name="migrate",
    )(recv, band, blend, source)
    terms = lax.all_to_all(terms, ("freq", "half", "shot"), 0, 0, tiled=True)
    return jnp.sum(terms.astype(F32), axis=0).reshape(1, share, depth, nx)


def solution(mesh):
    return jax.shard_map(
        body,
        mesh=mesh,
        in_specs=(
            P(("group", "shot"), "half", "freq", None),
            P(("group", "shot"), "half", None),
            P(),
            P(),
            P(),
            P("group", "half", None),
            P(),
            P(),
        ),
        out_specs=P("half", "freq", "group", None),
        check_vma=False,
    )
```

```python
import functools
import math

import jax
import jax.numpy as jnp
from jax import lax
from jax.experimental import pallas as pl
from jax.experimental.pallas import tpu as pltpu
from jax.sharding import PartitionSpec as P

FPD = 3
LANES = 128
SUB = 8
ROW_PAD = 8
VMEM_BYTES = 40 * 1024 * 1024
BF16 = jnp.bfloat16
F32 = jnp.float32


def list_bins(plan_ref, counts_ref, bins_ref):
    groups, cap = plan_ref.shape
    start = jnp.int32(0)
    for holder in range(groups):
        for slot in range(cap):
            bins_ref[start + slot] = plan_ref[holder, slot]
        start = start + counts_ref[holder]


def lane_iota(shape):
    return lax.broadcasted_iota(jnp.int32, shape, len(shape) - 1)


def row_iota(shape):
    return lax.broadcasted_iota(jnp.int32, shape, 0)


def dft_rows(bins_ref, group, nt):
    shape = (SUB, nt)
    row = row_iota(shape)
    bin_id = jnp.zeros(shape, jnp.int32)
    for slot in range(FPD):
        bin_id = jnp.where(row // 2 == slot, bins_ref[group * FPD + slot], bin_id)
    phase = bin_id * lane_iota(shape)
    phase = lax.rem(phase, jnp.int32(nt)) if nt & (nt - 1) else phase & (nt - 1)
    quarter = nt // 4
    turn = (phase + quarter // 2) // quarter
    angle = (phase - turn * quarter).astype(F32) * (2.0 * math.pi / nt)
    turn = (turn + (row & 1)) & 3
    sq = angle * angle
    cos = 1.0 + sq * (-1.0 / 2 + sq * (1.0 / 24 + sq * (-1.0 / 720 + sq * (1.0 / 40320))))
    sin = angle * (1.0 + sq * (-1.0 / 6 + sq * (1.0 / 120 + sq * (-1.0 / 5040 + sq * (1.0 / 362880)))))
    value = jnp.where((turn & 1) == 1, sin, cos)
    value = jnp.where(((turn + 1) & 2) == 2, -value, value)
    return value * (1.0 / math.sqrt(nt))


def transform(dft, block):
    return lax.dot_general(dft, block, (((1,), (1,)), ((), ())), preferred_element_type=F32)


def prepare_kernel(
    groups, plan_hbm, counts_hbm, wav_hbm, class_hbm, pattern_hbm, dft_ref, own_ref, wave_ref, shared_ref,
    plan_ref, counts_ref, wav_ref, class_ref, bins_ref, sems,
):
    nt = dft_ref.shape[1]
    depth, shots = class_hbm.shape[0], pattern_hbm.shape[0]
    later = [
        pltpu.make_async_copy(class_hbm, class_ref, sems.at[3]),
        pltpu.make_async_copy(pattern_hbm, shared_ref.at[pl.ds(depth, shots)], sems.at[4]),
    ]
    small = [
        pltpu.make_async_copy(plan_hbm, plan_ref, sems.at[0]),
        pltpu.make_async_copy(counts_hbm, counts_ref, sems.at[1]),
        pltpu.make_async_copy(wav_hbm, wav_ref, sems.at[2]),
    ]
    for copy in small + later:
        copy.start()
    for copy in small:
        copy.wait()
    list_bins(plan_ref, counts_ref, bins_ref)
    for pair in range(0, groups, 2):
        both = [dft_rows(bins_ref, group, nt) for group in range(pair, min(pair + 2, groups))]
        dft_ref[pair * SUB : (pair + len(both)) * SUB] = jnp.concatenate(both, axis=0).astype(BF16)
    first = lax.axis_index("freq") * FPD
    lane = lane_iota((1, LANES))
    for plane in range(FPD):
        bin_id = bins_ref[first + plane]
        own_ref[plane : plane + 1] = jnp.full((1, LANES), bin_id, jnp.int32)
        wave_ref[plane : plane + 1] = jnp.where(lane < LANES // 2, wav_ref[0, bin_id], wav_ref[1, bin_id])
    for copy in later:
        copy.wait()
    shared_ref[:depth] = class_ref[...].astype(BF16)


def send_kernel(groups, folded, dft_ref, rec_ref, out_ref, tmp_ref):
    shots, cells, _ = rec_ref.shape
    dft = dft_ref[...]
    for shot in range(shots):
        out = transform(dft, rec_ref[shot])
        if not folded:
            out_ref[shot] = out.astype(BF16)
            continue
        for group in range(groups):
            base = (group * shots + shot) * SUB * SUB
            for high in range(SUB):
                tmp_ref[pl.ds(base + high, SUB, stride=SUB), :] = out[
                    group * SUB : (group + 1) * SUB, high * LANES : (high + 1) * LANES
                ]
            out_ref[shot, group] = tmp_ref[base : base + 2 * FPD * SUB].astype(BF16)


def make_bands(taps, nref, ny, picked_ref, band_ref):
    reach = taps // 2
    width = 2 * ny
    lane = lane_iota((taps, width))
    full_lane = lane_iota((ny, width))
    keep = jnp.abs((full_lane & (ny - 1)) - row_iota((ny, width))) <= reach
    sign = jnp.where((lane < ny // 2) | (lane >= ny + ny // 2), -1.0, 1.0)
    for ref in range(nref):
        base = jnp.zeros((taps, width), F32)
        for part in range(2):
            for tap in range(taps):
                value = picked_ref[pl.ds((ref * taps + tap) * taps * 2 + part, taps, stride=2), :]
                base = jnp.where(lane == (part * ny + reach - tap) % width, value, base)
        turned = pltpu.roll(base, ny, 1) * sign
        for col_tap in range(taps):
            for part, rows in enumerate((base, turned)):
                spread = jnp.broadcast_to(rows[col_tap : col_tap + 1], (ny, width))
                band = pltpu.roll(spread, 0, 1, stride=1, stride_axis=0)
                band = jnp.where(keep, band, 0.0).astype(BF16)
                at = col_tap * width + part * ny
                band_ref[at : at + ny, ref * width : (ref + 1) * width] = band


def set_field(field_ref, value):
    rows, width = value.shape
    field_ref[:ROW_PAD] = jnp.zeros((ROW_PAD, width), F32)
    field_ref[ROW_PAD : ROW_PAD + rows] = value
    field_ref[ROW_PAD + rows :] = jnp.zeros((ROW_PAD, width), F32)


def shifted(taps, field_ref):
    first = ROW_PAD - taps // 2
    rows = field_ref.shape[0] - 2 * ROW_PAD
    pieces = [field_ref[pl.ds(first + tap, rows), :].astype(BF16) for tap in range(taps)]
    return jnp.concatenate(pieces, axis=1)


def advance(left, band_ref, blend):
    width = blend.shape[1]
    both = jnp.dot(left, band_ref[...], preferred_element_type=F32)
    low, high = both[:, :width], both[:, width:]
    return (low + blend * (high - low)).astype(BF16).astype(F32)


def run_steps(taps, depth, field_ref, band_ref, blend_ref, prepare, use):
    rows = field_ref.shape[1] - 2 * ROW_PAD
    order = [(step, plane) for step in range(depth) for plane in range(FPD)]
    prepare(0)
    left = shifted(taps, field_ref.at[0])
    for at, (step, plane) in enumerate(order):
        follow = None
        if at + 1 < len(order):
            after = order[at + 1][1]
            if order[at + 1][0] == 0:
                prepare(after)
            follow = shifted(taps, field_ref.at[after])
        new = advance(left, band_ref.at[plane], blend_ref[step])
        if step + 1 < depth:
            field_ref[plane, ROW_PAD : ROW_PAD + rows] = new
        use(step, plane, new)
        left = follow


def source_kernel(taps, nref, depth, halves, own_ref, wave_ref, filt_ref, table_hbm, class_hbm, pattern_hbm, *refs):
    others_hbm, refs = refs[: halves - 1], refs[halves - 1 :]
    (band_ref, blend_ref, source_ref, table_ref, class_ref, pattern_ref, others_ref,
     picked_ref, grid_ref, tab_ref, field_ref, sems) = refs
    copies = [
        pltpu.make_async_copy(table_hbm, table_ref, sems.at[0]),
        pltpu.make_async_copy(class_hbm, class_ref, sems.at[1]),
        pltpu.make_async_copy(pattern_hbm, pattern_ref, sems.at[2]),
    ]
    for turn in range(halves - 1):
        copies.append(pltpu.make_async_copy(others_hbm[turn], others_ref.at[turn], sems.at[3 + turn]))
    for copy in copies:
        copy.start()
    mine = lax.axis_index("half")
    rows = class_ref.shape[1]
    ny, nx = grid_ref.shape[1:]
    nbin = filt_ref.shape[1]
    for plane in range(FPD):
        hot = jnp.where(row_iota((nbin, LANES)) == own_ref[plane : plane + 1], 1.0, 0.0).astype(BF16)
        picked_ref[plane, : filt_ref.shape[0]] = jnp.dot(filt_ref[...], hot, preferred_element_type=F32)
    for plane in range(FPD - 1):
        make_bands(taps, nref, ny, picked_ref.at[plane], band_ref.at[plane])
    for copy in copies:
        copy.wait()
    for turn in range(halves):
        at = pl.ds(pl.multiple_of(lax.rem(mine + turn, halves) * rows, rows), rows)
        for step in range(depth):
            one = others_ref[turn - 1, step] if turn else class_ref[step]
            grid_ref[step, at, :] = one.astype(F32)
        one = others_ref[turn - 1, depth + mine] if turn else pattern_ref[mine]
        grid_ref[depth, at, :] = one.astype(F32)
    tab_ref[:, : table_ref.shape[1]] = jnp.broadcast_to(table_ref[...], (SUB, table_ref.shape[1]))
    for step in range(depth):
        pieces = []
        for row in range(0, ny, SUB):
            index = grid_ref[step, row : row + SUB].astype(jnp.int32)
            pieces.append(jnp.take_along_axis(tab_ref[...], index, axis=1))
        blend_ref[step] = jnp.concatenate(pieces + pieces, axis=0).T
    pattern = grid_ref[depth]
    pattern = jnp.concatenate([pattern, pattern], axis=0).T
    make_bands(taps, nref, ny, picked_ref.at[FPD - 1], band_ref.at[FPD - 1])

    def start(plane):
        set_field(field_ref.at[plane], (pattern * wave_ref[plane : plane + 1]).astype(BF16).astype(F32))

    def keep(step, plane, new):
        source_ref[step, plane] = new

    run_steps(taps, depth, field_ref, band_ref, blend_ref, start, keep)


def migrate_kernel(dims, recv_ref, band_ref, blend_ref, source_ref, out_ref, grid_ref, field_ref, image_ref):
    groups, halves, copies, xw, taps, scale, folded = dims
    depth, nx, width = blend_ref.shape
    ny = width // 2
    if folded:
        folds = LANES // xw
        half_rows = ny // halves
        lane = lane_iota((SUB, LANES))
        blocks = [recv_ref[block].astype(F32) for block in range(groups * halves)]
    else:
        grid_ref[: recv_ref.shape[0]] = recv_ref[...].astype(F32)
    steps = [None] * depth

    def gather(plane):
        if folded:
            for half in range(halves):
                for item in range(2 * plane, 2 * plane + 2):
                    for low in range(folds):
                        kept = None
                        for group in range(groups):
                            piece = blocks[half * groups + group][item * SUB : (item + 1) * SUB]
                            shift = ((group - low) * xw) % LANES
                            if shift:
                                piece = pltpu.roll(piece, shift, 1)
                            kept = piece if kept is None else jnp.where(lane // xw == group, piece, kept)
                        grid_ref[pl.ds(item * ny + half * half_rows + low, SUB, stride=folds), :] = kept
        set_field(field_ref.at[plane], grid_ref[plane * width : (plane + 1) * width].T)

    def correlate(step, plane, new):
        term = source_ref[step, plane] * new
        steps[step] = term if steps[step] is None else steps[step] + term
        if plane == FPD - 1:
            turned = steps[step].T
            image_ref[pl.ds(step, ny, stride=depth), :] = (turned[:ny] + turned[ny:]) * scale

    run_steps(taps, depth, field_ref, band_ref, blend_ref, gather, correlate)
    share = ny // (groups * halves) * depth
    for group in range(groups):
        for half in range(halves):
            start = (half * groups + group) * share
            piece = image_ref[start : start + share].astype(BF16)
            for copy in range(copies):
                out_ref[(group * halves + half) * copies + copy] = piece


def vmem():
    return pl.BlockSpec(memory_space=pltpu.VMEM)


def hbm():
    return pl.BlockSpec(memory_space=pltpu.HBM)


def pinned(*arrays):
    return [pltpu.with_memory_space_constraint(array, pltpu.HBM) for array in arrays]


def from_halves(block, halves):
    blocks = [block]
    for turn in range(1, halves):
        blocks.append(lax.ppermute(block, "half", [((to + turn) % halves, to) for to in range(halves)]))
    return blocks


def body(records, source_pattern, wavelet, filters, vel_table, vel_index, freq_plan, counts):
    groups = lax.axis_size("freq")
    halves = lax.axis_size("half")
    copies = lax.axis_size("shot")
    shots, rows, xw, nt = records.shape
    depth = vel_index.shape[0]
    nref, _, taps, _, nbin = filters.shape
    nx = xw * groups
    ny = rows * halves
    items = 2 * FPD
    cap = freq_plan.shape[1]
    cells = rows * xw
    folded = LANES % xw == 0 and cells == SUB * LANES
    bins = pltpu.SMEM((groups * FPD + cap,), jnp.int32)
    params = pltpu.CompilerParams(vmem_limit_bytes=VMEM_BYTES)


    if folded:
        send_shape = (shots, groups, items * SUB, LANES)
    else:
        send_shape = (shots, groups * SUB, cells)
    table = filters.transpose(0, 2, 3, 1, 4)
    dft, own, wave, shared = pl.pallas_call(
        functools.partial(prepare_kernel, groups),
        out_shape=[
            jax.ShapeDtypeStruct((groups * SUB, nt), BF16),
            jax.ShapeDtypeStruct((SUB, LANES), jnp.int32),
            jax.ShapeDtypeStruct((SUB, LANES), F32),
            jax.ShapeDtypeStruct((depth + shots, rows, nx), BF16),
        ],
        in_specs=[hbm()] * 5,
        out_specs=[vmem()] * 4,
        scratch_shapes=[
            pltpu.SMEM(freq_plan.shape, jnp.int32),
            pltpu.SMEM(counts.shape, jnp.int32),
            pltpu.SMEM((2, nbin), F32),
            pltpu.VMEM(vel_index.shape, jnp.int32),
            bins,
            pltpu.SemaphoreType.DMA((5,)),
        ],
        compiler_params=params,
        cost_estimate=pl.CostEstimate(flops=3 * 10**9, bytes_accessed=4 * 10**6, transcendentals=0),
        name="prepare",
    )(*pinned(freq_plan, counts, wavelet.T, vel_index, source_pattern))
    others = from_halves(shared, halves)[1:]
    send = pl.pallas_call(
        functools.partial(send_kernel, groups, folded),
        out_shape=jax.ShapeDtypeStruct(send_shape, BF16),
        in_specs=[vmem()] * 2,
        out_specs=vmem(),
        scratch_shapes=[pltpu.VMEM((groups * shots * SUB * SUB + SUB, LANES), F32)],
        compiler_params=params,
        name="send_blocks",
    )(dft, records.reshape(shots, cells, nt))
    if folded:
        send = send.reshape(groups * halves, items * SUB, LANES)
        recv = lax.all_to_all(send, ("half", "freq"), 0, 0, tiled=True)
    else:
        send = send.reshape(shots, groups, SUB, cells)[:, :, :items].swapaxes(0, 1)
        send = send.reshape(groups * halves, items, cells)
        recv = lax.all_to_all(send, ("freq", "half"), 0, 0, tiled=True)
        recv = recv.reshape(groups, halves, items, rows, xw).transpose(2, 1, 3, 0, 4).reshape(items * ny, nx)

    table = table.reshape(nref * taps * taps * 2, nbin)
    band_shape = (FPD, taps * 2 * ny, nref * 2 * ny)
    field = pltpu.VMEM((FPD, nx + 2 * ROW_PAD, 2 * ny), F32)
    band, blend, source = pl.pallas_call(
        functools.partial(source_kernel, taps, nref, depth, halves),
        out_shape=[
            jax.ShapeDtypeStruct(band_shape, BF16),
            jax.ShapeDtypeStruct((depth, nx, 2 * ny), F32),
            jax.ShapeDtypeStruct((depth, FPD, nx, 2 * ny), F32),
        ],
        in_specs=[vmem()] * 3 + [hbm()] * 2 + [pl.BlockSpec(memory_space=pl.ANY)] + [hbm()] * (halves - 1),
        out_specs=[vmem()] * 3,
        scratch_shapes=[
            pltpu.VMEM((1,) + vel_table.shape, F32),
            pltpu.VMEM(vel_index.shape, jnp.int32),
            pltpu.VMEM(source_pattern.shape, BF16),
            pltpu.VMEM((halves - 1,) + shared.shape, BF16),
            pltpu.VMEM((FPD, (table.shape[0] + 2 * taps + SUB) // SUB * SUB + 2 * SUB, LANES), F32),
            pltpu.VMEM((depth + 1, ny, nx), F32),
            pltpu.VMEM((SUB, LANES), F32),
            field,
            pltpu.SemaphoreType.DMA((2 + halves,)),
        ],
        compiler_params=params,
        cost_estimate=pl.CostEstimate(flops=4 * 10**9, bytes_accessed=10**7, transcendentals=0),
        name="source_fields",
    )(own, wave, table, *pinned(vel_table[None], vel_index), source_pattern, *pinned(*others))

    scale = 1.0 / math.sqrt(FPD * groups * shots * copies)
    share = ny // (groups * halves)
    terms = pl.pallas_call(
        functools.partial(migrate_kernel, (groups, halves, copies, xw, taps, scale, folded)),
        out_shape=jax.ShapeDtypeStruct((groups * halves * copies, share * depth, nx), BF16),
        in_specs=[vmem()] * 4,
        out_specs=vmem(),
        scratch_shapes=[
            pltpu.VMEM((items * ny + SUB, nx), F32),
            field,
            pltpu.VMEM((ny * depth + SUB, nx), F32),
        ],
        compiler_params=params,
        name="migrate",
    )(recv, band, blend, source)
    terms = lax.all_to_all(terms, ("freq", "half", "shot"), 0, 0, tiled=True)
    return jnp.sum(terms.astype(F32), axis=0).reshape(1, share, depth, nx)


def solution(mesh):
    return jax.shard_map(
        body,
        mesh=mesh,
        in_specs=(
            P(("group", "shot"), "half", "freq", None),
            P(("group", "shot"), "half", None),
            P(),
            P(),
            P(),
            P("group", "half", None),
            P(),
            P(),
        ),
        out_specs=P("half", "freq", "group", None),
        check_vma=False,
    )
```

```python
import functools
import math

import jax
import jax.numpy as jnp
from jax import lax
from jax.experimental import pallas as pl
from jax.experimental.pallas import tpu as pltpu
from jax.sharding import PartitionSpec as P

FPD = 3
LANES = 128
SUB = 8
ROW_PAD = 8
VMEM_BYTES = 40 * 1024 * 1024
BF16 = jnp.bfloat16
F32 = jnp.float32


def list_bins(plan_ref, counts_ref, bins_ref):
    groups, cap = plan_ref.shape
    start = jnp.int32(0)
    for holder in range(groups):
        for slot in range(cap):
            bins_ref[start + slot] = plan_ref[holder, slot]
        start = start + counts_ref[holder]


def lane_iota(shape):
    return lax.broadcasted_iota(jnp.int32, shape, len(shape) - 1)


def row_iota(shape):
    return lax.broadcasted_iota(jnp.int32, shape, 0)


def dft_rows(bins_ref, group, nt):
    shape = (SUB, nt)
    row = row_iota(shape)
    bin_id = jnp.zeros(shape, jnp.int32)
    for slot in range(FPD):
        bin_id = jnp.where(row // 2 == slot, bins_ref[group * FPD + slot], bin_id)
    phase = bin_id * lane_iota(shape)
    phase = lax.rem(phase, jnp.int32(nt)) if nt & (nt - 1) else phase & (nt - 1)
    quarter = nt // 4
    turn = (phase + quarter // 2) // quarter
    angle = (phase - turn * quarter).astype(F32) * (2.0 * math.pi / nt)
    turn = (turn + (row & 1)) & 3
    sq = angle * angle
    cos = 1.0 + sq * (-1.0 / 2 + sq * (1.0 / 24 + sq * (-1.0 / 720 + sq * (1.0 / 40320))))
    sin = angle * (1.0 + sq * (-1.0 / 6 + sq * (1.0 / 120 + sq * (-1.0 / 5040 + sq * (1.0 / 362880)))))
    value = jnp.where((turn & 1) == 1, sin, cos)
    value = jnp.where(((turn + 1) & 2) == 2, -value, value)
    return value * (1.0 / math.sqrt(nt))


def transform(dft, block):
    return lax.dot_general(dft, block, (((1,), (1,)), ((), ())), preferred_element_type=F32)


def prepare_kernel(
    groups, plan_hbm, counts_hbm, wav_hbm, dft_ref, own_ref, wave_ref,
    plan_ref, counts_ref, wav_ref, bins_ref, sems,
):
    nt = dft_ref.shape[1]
    small = [
        pltpu.make_async_copy(plan_hbm, plan_ref, sems.at[0]),
        pltpu.make_async_copy(counts_hbm, counts_ref, sems.at[1]),
        pltpu.make_async_copy(wav_hbm, wav_ref, sems.at[2]),
    ]
    for copy in small:
        copy.start()
    for copy in small:
        copy.wait()
    list_bins(plan_ref, counts_ref, bins_ref)
    for pair in range(0, groups, 2):
        both = [dft_rows(bins_ref, group, nt) for group in range(pair, min(pair + 2, groups))]
        dft_ref[pair * SUB : (pair + len(both)) * SUB] = jnp.concatenate(both, axis=0).astype(BF16)
    first = lax.axis_index("freq") * FPD
    lane = lane_iota((1, LANES))
    for plane in range(FPD):
        bin_id = bins_ref[first + plane]
        own_ref[plane : plane + 1] = jnp.full((1, LANES), bin_id, jnp.int32)
        wave_ref[plane : plane + 1] = jnp.where(lane < LANES // 2, wav_ref[0, bin_id], wav_ref[1, bin_id])


def send_kernel(groups, folded, dft_ref, rec_ref, out_ref, tmp_ref):
    shots, cells, _ = rec_ref.shape
    dft = dft_ref[...]
    for shot in range(shots):
        out = transform(dft, rec_ref[shot])
        if not folded:
            out_ref[shot] = out.astype(BF16)
            continue
        for group in range(groups):
            base = (group * shots + shot) * SUB * SUB
            for high in range(SUB):
                tmp_ref[pl.ds(base + high, SUB, stride=SUB), :] = out[
                    group * SUB : (group + 1) * SUB, high * LANES : (high + 1) * LANES
                ]
            out_ref[shot, group] = tmp_ref[base : base + 2 * FPD * SUB].astype(BF16)


def make_bands(taps, nref, ny, picked_ref, band_ref):
    reach = taps // 2
    width = 2 * ny
    lane = lane_iota((taps, width))
    full_lane = lane_iota((ny, width))
    keep = jnp.abs((full_lane & (ny - 1)) - row_iota((ny, width))) <= reach
    sign = jnp.where((lane < ny // 2) | (lane >= ny + ny // 2), -1.0, 1.0)
    for ref in range(nref):
        base = jnp.zeros((taps, width), F32)
        for part in range(2):
            for tap in range(taps):
                value = picked_ref[pl.ds((ref * taps + tap) * taps * 2 + part, taps, stride=2), :]
                base = jnp.where(lane == (part * ny + reach - tap) % width, value, base)
        turned = pltpu.roll(base, ny, 1) * sign
        for col_tap in range(taps):
            for part, rows in enumerate((base, turned)):
                spread = jnp.broadcast_to(rows[col_tap : col_tap + 1], (ny, width))
                band = pltpu.roll(spread, 0, 1, stride=1, stride_axis=0)
                band = jnp.where(keep, band, 0.0).astype(BF16)
                at = col_tap * width + part * ny
                band_ref[at : at + ny, ref * width : (ref + 1) * width] = band


def set_field(field_ref, value):
    rows, width = value.shape
    field_ref[:ROW_PAD] = jnp.zeros((ROW_PAD, width), F32)
    field_ref[ROW_PAD : ROW_PAD + rows] = value
    field_ref[ROW_PAD + rows :] = jnp.zeros((ROW_PAD, width), F32)


def shifted(taps, field_ref):
    first = ROW_PAD - taps // 2
    rows = field_ref.shape[0] - 2 * ROW_PAD
    pieces = [field_ref[pl.ds(first + tap, rows), :].astype(BF16) for tap in range(taps)]
    return jnp.concatenate(pieces, axis=1)


def advance(left, band_ref, blend):
    width = blend.shape[1]
    both = jnp.dot(left, band_ref[...], preferred_element_type=F32)
    low, high = both[:, :width], both[:, width:]
    return (low + blend * (high - low)).astype(BF16).astype(F32)


def run_steps(taps, depth, field_ref, band_ref, blend_ref, prepare, use):
    rows = field_ref.shape[1] - 2 * ROW_PAD
    order = [(step, plane) for step in range(depth) for plane in range(FPD)]
    for plane in range(FPD):
        prepare(plane)
    left = shifted(taps, field_ref.at[0])
    for at, (step, plane) in enumerate(order):
        follow = None
        if at + 1 < len(order):
            after = order[at + 1][1]
            follow = shifted(taps, field_ref.at[after])
        new = advance(left, band_ref.at[plane], blend_ref[step])
        if step + 1 < depth:
            field_ref[plane, ROW_PAD : ROW_PAD + rows] = new
        use(step, plane, new)
        left = follow


def source_kernel(taps, nref, depth, halves, own_ref, wave_ref, filt_ref, table_hbm, *refs):
    class_hbm, refs = refs[:halves], refs[halves:]
    pattern_hbm, refs = refs[:halves], refs[halves:]
    band_ref, blend_ref, source_ref, class_refs, pattern_refs, table_ref, picked_ref, grid_ref, tab_ref, field_ref, sems = refs
    copies = [pltpu.make_async_copy(table_hbm, table_ref, sems.at[0])]
    for turn in range(halves):
        copies.append(pltpu.make_async_copy(class_hbm[turn], class_refs.at[turn], sems.at[1 + 2 * turn]))
        copies.append(pltpu.make_async_copy(pattern_hbm[turn], pattern_refs.at[turn], sems.at[2 + 2 * turn]))
    for copy in copies:
        copy.start()
    mine = lax.axis_index("half")
    rows = class_hbm[0].shape[1]
    ny, nx = grid_ref.shape[1:]
    nbin = filt_ref.shape[1]
    for plane in range(FPD):
        hot = jnp.where(row_iota((nbin, LANES)) == own_ref[plane : plane + 1], 1.0, 0.0).astype(BF16)
        picked_ref[plane, : filt_ref.shape[0]] = jnp.dot(filt_ref[...], hot, preferred_element_type=F32)
    for plane in range(FPD - 1):
        make_bands(taps, nref, ny, picked_ref.at[plane], band_ref.at[plane])
    for copy in copies:
        copy.wait()
    for turn in range(halves):
        at = pl.ds(pl.multiple_of(lax.rem(mine + turn, halves) * rows, rows), rows)
        for step in range(depth):
            grid_ref[step, at, :] = class_refs[turn, step].astype(F32)
        grid_ref[depth, at, :] = pattern_refs[turn, mine].astype(F32)
    tab_ref[:, : table_ref.shape[1]] = jnp.broadcast_to(table_ref[...], (SUB, table_ref.shape[1]))
    for step in range(depth):
        pieces = []
        for row in range(0, ny, SUB):
            index = grid_ref[step, row : row + SUB].astype(jnp.int32)
            pieces.append(jnp.take_along_axis(tab_ref[...], index, axis=1))
        blend_ref[step] = jnp.concatenate(pieces + pieces, axis=0).T
    pattern = grid_ref[depth]
    pattern = jnp.concatenate([pattern, pattern], axis=0).T
    make_bands(taps, nref, ny, picked_ref.at[FPD - 1], band_ref.at[FPD - 1])

    def start(plane):
        set_field(field_ref.at[plane], (pattern * wave_ref[plane : plane + 1]).astype(BF16).astype(F32))

    def keep(step, plane, new):
        source_ref[step, plane] = new

    run_steps(taps, depth, field_ref, band_ref, blend_ref, start, keep)


def migrate_kernel(dims, recv_ref, band_ref, blend_ref, source_ref, out_ref, grid_ref, field_ref, image_ref):
    groups, halves, copies, xw, taps, scale, folded = dims
    depth, nx, width = blend_ref.shape
    ny = width // 2
    if folded:
        folds = LANES // xw
        half_rows = ny // halves
        lane = lane_iota((SUB, LANES))
        blocks = [recv_ref[block].astype(F32) for block in range(groups * halves)]
    else:
        grid_ref[: recv_ref.shape[0]] = recv_ref[...].astype(F32)
    steps = [None] * depth

    def gather(plane):
        if folded:
            for half in range(halves):
                for item in range(2 * plane, 2 * plane + 2):
                    for low in range(folds):
                        kept = None
                        for group in range(groups):
                            piece = blocks[half * groups + group][item * SUB : (item + 1) * SUB]
                            shift = ((group - low) * xw) % LANES
                            if shift:
                                piece = pltpu.roll(piece, shift, 1)
                            kept = piece if kept is None else jnp.where(lane // xw == group, piece, kept)
                        grid_ref[pl.ds(item * ny + half * half_rows + low, SUB, stride=folds), :] = kept
        set_field(field_ref.at[plane], grid_ref[plane * width : (plane + 1) * width].T)

    def correlate(step, plane, new):
        term = source_ref[step, plane] * new
        steps[step] = term if steps[step] is None else steps[step] + term
        if plane == FPD - 1:
            turned = steps[step].T
            image_ref[pl.ds(step, ny, stride=depth), :] = (turned[:ny] + turned[ny:]) * scale

    run_steps(taps, depth, field_ref, band_ref, blend_ref, gather, correlate)
    share = ny // (groups * halves) * depth
    for group in range(groups):
        for half in range(halves):
            start = (half * groups + group) * share
            piece = image_ref[start : start + share].astype(BF16)
            for copy in range(copies):
                out_ref[(group * halves + half) * copies + copy] = piece


def vmem():
    return pl.BlockSpec(memory_space=pltpu.VMEM)


def hbm():
    return pl.BlockSpec(memory_space=pltpu.HBM)


def pinned(*arrays):
    return [pltpu.with_memory_space_constraint(array, pltpu.HBM) for array in arrays]


def from_halves(block, halves):
    blocks = [block]
    for turn in range(1, halves):
        blocks.append(lax.ppermute(block, "half", [((to + turn) % halves, to) for to in range(halves)]))
    return blocks


def body(records, source_pattern, wavelet, filters, vel_table, vel_index, freq_plan, counts):
    groups = lax.axis_size("freq")
    halves = lax.axis_size("half")
    copies = lax.axis_size("shot")
    shots, rows, xw, nt = records.shape
    depth = vel_index.shape[0]
    nref, _, taps, _, nbin = filters.shape
    nx = xw * groups
    ny = rows * halves
    items = 2 * FPD
    cap = freq_plan.shape[1]
    cells = rows * xw
    folded = LANES % xw == 0 and cells == SUB * LANES
    bins = pltpu.SMEM((groups * FPD + cap,), jnp.int32)
    params = pltpu.CompilerParams(vmem_limit_bytes=VMEM_BYTES)


    if folded:
        send_shape = (shots, groups, items * SUB, LANES)
    else:
        send_shape = (shots, groups * SUB, cells)
    table = filters.transpose(0, 2, 3, 1, 4)
    dft, own, wave = pl.pallas_call(
        functools.partial(prepare_kernel, groups),
        out_shape=[
            jax.ShapeDtypeStruct((groups * SUB, nt), BF16),
            jax.ShapeDtypeStruct((SUB, LANES), jnp.int32),
            jax.ShapeDtypeStruct((SUB, LANES), F32),
        ],
        in_specs=[hbm()] * 3,
        out_specs=[vmem()] * 3,
        scratch_shapes=[
            pltpu.SMEM(freq_plan.shape, jnp.int32),
            pltpu.SMEM(counts.shape, jnp.int32),
            pltpu.SMEM((2, nbin), F32),
            bins,
            pltpu.SemaphoreType.DMA((3,)),
        ],
        compiler_params=params,
        cost_estimate=pl.CostEstimate(flops=3 * 10**9, bytes_accessed=4 * 10**6, transcendentals=0),
        name="prepare",
    )(*pinned(freq_plan, counts, wavelet.T))
    own, vel_index, source_pattern = lax.optimization_barrier((own, vel_index, source_pattern))
    classes = from_halves(vel_index, halves)
    patterns = from_halves(source_pattern, halves)
    send = pl.pallas_call(
        functools.partial(send_kernel, groups, folded),
        out_shape=jax.ShapeDtypeStruct(send_shape, BF16),
        in_specs=[vmem()] * 2,
        out_specs=vmem(),
        scratch_shapes=[pltpu.VMEM((groups * shots * SUB * SUB + SUB, LANES), F32)],
        compiler_params=params,
        name="send_blocks",
    )(dft, records.reshape(shots, cells, nt))
    if folded:
        send = send.reshape(groups * halves, items * SUB, LANES)
        recv = lax.all_to_all(send, ("half", "freq"), 0, 0, tiled=True)
    else:
        send = send.reshape(shots, groups, SUB, cells)[:, :, :items].swapaxes(0, 1)
        send = send.reshape(groups * halves, items, cells)
        recv = lax.all_to_all(send, ("freq", "half"), 0, 0, tiled=True)
        recv = recv.reshape(groups, halves, items, rows, xw).transpose(2, 1, 3, 0, 4).reshape(items * ny, nx)

    table = table.reshape(nref * taps * taps * 2, nbin)
    band_shape = (FPD, taps * 2 * ny, nref * 2 * ny)
    field = pltpu.VMEM((FPD, nx + 2 * ROW_PAD, 2 * ny), F32)
    band, blend, source = pl.pallas_call(
        functools.partial(source_kernel, taps, nref, depth, halves),
        out_shape=[
            jax.ShapeDtypeStruct(band_shape, BF16),
            jax.ShapeDtypeStruct((depth, nx, 2 * ny), F32),
            jax.ShapeDtypeStruct((depth, FPD, nx, 2 * ny), F32),
        ],
        in_specs=[vmem()] * 3 + [hbm()] * (2 + halves) + [pl.BlockSpec(memory_space=pl.ANY)] * (halves - 1),
        out_specs=[vmem()] * 3,
        scratch_shapes=[
            pltpu.VMEM((halves,) + vel_index.shape, jnp.int32),
            pltpu.VMEM((halves,) + source_pattern.shape, BF16),
            pltpu.VMEM((1,) + vel_table.shape, F32),
            pltpu.VMEM((FPD, (table.shape[0] + 2 * taps + SUB) // SUB * SUB + 2 * SUB, LANES), F32),
            pltpu.VMEM((depth + 1, ny, nx), F32),
            pltpu.VMEM((SUB, LANES), F32),
            field,
            pltpu.SemaphoreType.DMA((1 + 2 * halves,)),
        ],
        compiler_params=params,
        cost_estimate=pl.CostEstimate(flops=4 * 10**9, bytes_accessed=10**7, transcendentals=0),
        name="source_fields",
    )(own, wave, table, *pinned(vel_table[None], *classes, patterns[0]), *patterns[1:])

    scale = 1.0 / math.sqrt(FPD * groups * shots * copies)
    share = ny // (groups * halves)
    terms = pl.pallas_call(
        functools.partial(migrate_kernel, (groups, halves, copies, xw, taps, scale, folded)),
        out_shape=jax.ShapeDtypeStruct((groups * halves * copies, share * depth, nx), BF16),
        in_specs=[vmem()] * 4,
        out_specs=vmem(),
        scratch_shapes=[
            pltpu.VMEM((items * ny + SUB, nx), F32),
            field,
            pltpu.VMEM((ny * depth + SUB, nx), F32),
        ],
        compiler_params=params,
        name="migrate",
    )(recv, band, blend, source)
    terms = lax.all_to_all(terms, ("freq", "half", "shot"), 0, 0, tiled=True)
    return jnp.sum(terms.astype(F32), axis=0).reshape(1, share, depth, nx)


def solution(mesh):
    return jax.shard_map(
        body,
        mesh=mesh,
        in_specs=(
            P(("group", "shot"), "half", "freq", None),
            P(("group", "shot"), "half", None),
            P(),
            P(),
            P(),
            P("group", "half", None),
            P(),
            P(),
        ),
        out_specs=P("half", "freq", "group", None),
        check_vma=False,
    )
```

```python
import functools
import math

import jax
import jax.numpy as jnp
from jax import lax
from jax.experimental import pallas as pl
from jax.experimental.pallas import tpu as pltpu
from jax.sharding import PartitionSpec as P

FPD = 3
LANES = 128
SUB = 8
ROW_PAD = 8
VMEM_BYTES = 40 * 1024 * 1024
BF16 = jnp.bfloat16
F32 = jnp.float32


def list_bins(plan_ref, counts_ref, bins_ref):
    groups, cap = plan_ref.shape
    start = jnp.int32(0)
    for holder in range(groups):
        for slot in range(cap):
            bins_ref[start + slot] = plan_ref[holder, slot]
        start = start + counts_ref[holder]


def lane_iota(shape):
    return lax.broadcasted_iota(jnp.int32, shape, len(shape) - 1)


def row_iota(shape):
    return lax.broadcasted_iota(jnp.int32, shape, 0)


def dft_rows(bins_ref, group, nt):
    shape = (SUB, nt)
    row = row_iota(shape)
    bin_id = jnp.zeros(shape, jnp.int32)
    for slot in range(FPD):
        bin_id = jnp.where(row // 2 == slot, bins_ref[group * FPD + slot], bin_id)
    phase = bin_id * lane_iota(shape)
    phase = lax.rem(phase, jnp.int32(nt)) if nt & (nt - 1) else phase & (nt - 1)
    quarter = nt // 4
    turn = (phase + quarter // 2) // quarter
    angle = (phase - turn * quarter).astype(F32) * (2.0 * math.pi / nt)
    turn = (turn + (row & 1)) & 3
    sq = angle * angle
    cos = 1.0 + sq * (-1.0 / 2 + sq * (1.0 / 24 + sq * (-1.0 / 720 + sq * (1.0 / 40320))))
    sin = angle * (1.0 + sq * (-1.0 / 6 + sq * (1.0 / 120 + sq * (-1.0 / 5040 + sq * (1.0 / 362880)))))
    value = jnp.where((turn & 1) == 1, sin, cos)
    value = jnp.where(((turn + 1) & 2) == 2, -value, value)
    return value * (1.0 / math.sqrt(nt))


def transform(dft, block):
    return lax.dot_general(dft, block, (((1,), (1,)), ((), ())), preferred_element_type=F32)


def put_spectra(groups, folded, out, put, tmp_ref):
    if not folded:
        put[...] = out.astype(BF16)
        return
    for group in range(groups):
        base = group * SUB * SUB
        for high in range(SUB):
            tmp_ref[pl.ds(base + high, SUB, stride=SUB), :] = out[
                group * SUB : (group + 1) * SUB, high * LANES : (high + 1) * LANES
            ]
        put[group] = tmp_ref[base : base + 2 * FPD * SUB].astype(BF16)


def prepare_kernel(
    groups, folded, plan_hbm, counts_hbm, wav_hbm, class_hbm, pattern_hbm, rec_hbm,
    dft_ref, own_ref, wave_ref, shared_ref, early_ref, last_ref,
    plan_ref, counts_ref, wav_ref, class_ref, bins_ref, rec_ref, tmp_ref, sems,
):
    nt = dft_ref.shape[1]
    depth, shots = class_hbm.shape[0], pattern_hbm.shape[0]
    later = [
        pltpu.make_async_copy(class_hbm, class_ref, sems.at[3]),
        pltpu.make_async_copy(pattern_hbm, shared_ref.at[pl.ds(depth, shots)], sems.at[4]),
    ]
    small = [
        pltpu.make_async_copy(plan_hbm, plan_ref, sems.at[0]),
        pltpu.make_async_copy(counts_hbm, counts_ref, sems.at[1]),
        pltpu.make_async_copy(wav_hbm, wav_ref, sems.at[2]),
    ]
    early = [
        pltpu.make_async_copy(rec_hbm.at[shot], rec_ref.at[shot], sems.at[5 + shot]) for shot in range(shots - 1)
    ]
    last = pltpu.make_async_copy(rec_hbm.at[shots - 1], last_ref, sems.at[4 + shots])
    for copy in small + early + later + [last]:
        copy.start()
    for copy in small:
        copy.wait()
    list_bins(plan_ref, counts_ref, bins_ref)
    for pair in range(0, groups, 2):
        both = [dft_rows(bins_ref, group, nt) for group in range(pair, min(pair + 2, groups))]
        dft_ref[pair * SUB : (pair + len(both)) * SUB] = jnp.concatenate(both, axis=0).astype(BF16)
    first = lax.axis_index("freq") * FPD
    lane = lane_iota((1, LANES))
    for plane in range(FPD):
        bin_id = bins_ref[first + plane]
        own_ref[plane : plane + 1] = jnp.full((1, LANES), bin_id, jnp.int32)
        wave_ref[plane : plane + 1] = jnp.where(lane < LANES // 2, wav_ref[0, bin_id], wav_ref[1, bin_id])
    for copy in later:
        copy.wait()
    shared_ref[:depth] = class_ref[...].astype(BF16)
    for shot, copy in enumerate(early):
        copy.wait()
        put_spectra(groups, folded, transform(dft_ref[...], rec_ref[shot]), early_ref.at[shot], tmp_ref)
    last.wait()


def send_kernel(groups, folded, dft_ref, early_ref, last_ref, out_ref, tmp_ref):
    early = early_ref.shape[0]
    out = transform(dft_ref[...], last_ref[...])
    for shot in range(early):
        out_ref[shot] = early_ref[shot]
    put_spectra(groups, folded, out, out_ref.at[early], tmp_ref)


def make_bands(taps, nref, ny, picked_ref, band_ref):
    reach = taps // 2
    width = 2 * ny
    lane = lane_iota((taps, width))
    full_lane = lane_iota((ny, width))
    keep = jnp.abs((full_lane & (ny - 1)) - row_iota((ny, width))) <= reach
    sign = jnp.where((lane < ny // 2) | (lane >= ny + ny // 2), -1.0, 1.0)
    for ref in range(nref):
        base = jnp.zeros((taps, width), F32)
        for part in range(2):
            for tap in range(taps):
                value = picked_ref[pl.ds((ref * taps + tap) * taps * 2 + part, taps, stride=2), :]
                base = jnp.where(lane == (part * ny + reach - tap) % width, value, base)
        turned = pltpu.roll(base, ny, 1) * sign
        for col_tap in range(taps):
            for part, rows in enumerate((base, turned)):
                spread = jnp.broadcast_to(rows[col_tap : col_tap + 1], (ny, width))
                band = pltpu.roll(spread, 0, 1, stride=1, stride_axis=0)
                band = jnp.where(keep, band, 0.0).astype(BF16)
                at = col_tap * width + part * ny
                band_ref[at : at + ny, ref * width : (ref + 1) * width] = band


def set_field(field_ref, value):
    rows, width = value.shape
    field_ref[:ROW_PAD] = jnp.zeros((ROW_PAD, width), F32)
    field_ref[ROW_PAD : ROW_PAD + rows] = value
    field_ref[ROW_PAD + rows :] = jnp.zeros((ROW_PAD, width), F32)


def shifted(taps, field_ref):
    first = ROW_PAD - taps // 2
    rows = field_ref.shape[0] - 2 * ROW_PAD
    pieces = [field_ref[pl.ds(first + tap, rows), :].astype(BF16) for tap in range(taps)]
    return jnp.concatenate(pieces, axis=1)


def advance(left, band_ref, blend):
    width = blend.shape[1]
    both = jnp.dot(left, band_ref[...], preferred_element_type=F32)
    low, high = both[:, :width], both[:, width:]
    return (low + blend * (high - low)).astype(BF16).astype(F32)


def run_steps(taps, depth, field_ref, band_ref, blend_ref, prepare, use):
    rows = field_ref.shape[1] - 2 * ROW_PAD
    order = [(step, plane) for step in range(depth) for plane in range(FPD)]
    for plane in range(FPD):
        prepare(plane)
    left = shifted(taps, field_ref.at[0])
    for at, (step, plane) in enumerate(order):
        follow = None
        if at + 1 < len(order):
            after = order[at + 1][1]
            follow = shifted(taps, field_ref.at[after])
        new = advance(left, band_ref.at[plane], blend_ref[step])
        if step + 1 < depth:
            field_ref[plane, ROW_PAD : ROW_PAD + rows] = new
        use(step, plane, new)
        left = follow


def source_kernel(taps, nref, depth, halves, own_ref, wave_ref, filt_ref, table_hbm, class_hbm, pattern_hbm, *refs):
    others_hbm, refs = refs[: halves - 1], refs[halves - 1 :]
    (band_ref, blend_ref, source_ref, table_ref, class_ref, pattern_ref, others_ref,
     picked_ref, grid_ref, tab_ref, field_ref, sems) = refs
    copies = [
        pltpu.make_async_copy(table_hbm, table_ref, sems.at[0]),
        pltpu.make_async_copy(class_hbm, class_ref, sems.at[1]),
        pltpu.make_async_copy(pattern_hbm, pattern_ref, sems.at[2]),
    ]
    for turn in range(halves - 1):
        copies.append(pltpu.make_async_copy(others_hbm[turn], others_ref.at[turn], sems.at[3 + turn]))
    for copy in copies:
        copy.start()
    mine = lax.axis_index("half")
    rows = class_ref.shape[1]
    ny, nx = grid_ref.shape[1:]
    nbin = filt_ref.shape[1]
    for plane in range(FPD):
        hot = jnp.where(row_iota((nbin, LANES)) == own_ref[plane : plane + 1], 1.0, 0.0).astype(BF16)
        picked_ref[plane, : filt_ref.shape[0]] = jnp.dot(filt_ref[...], hot, preferred_element_type=F32)
    for plane in range(FPD - 1):
        make_bands(taps, nref, ny, picked_ref.at[plane], band_ref.at[plane])
    for copy in copies:
        copy.wait()
    for turn in range(halves):
        at = pl.ds(pl.multiple_of(lax.rem(mine + turn, halves) * rows, rows), rows)
        for step in range(depth):
            one = others_ref[turn - 1, step] if turn else class_ref[step]
            grid_ref[step, at, :] = one.astype(F32)
        one = others_ref[turn - 1, depth + mine] if turn else pattern_ref[mine]
        grid_ref[depth, at, :] = one.astype(F32)
    tab_ref[:, : table_ref.shape[1]] = jnp.broadcast_to(table_ref[...], (SUB, table_ref.shape[1]))
    for step in range(depth):
        pieces = []
        for row in range(0, ny, SUB):
            index = grid_ref[step, row : row + SUB].astype(jnp.int32)
            pieces.append(jnp.take_along_axis(tab_ref[...], index, axis=1))
        blend_ref[step] = jnp.concatenate(pieces + pieces, axis=0).T
    pattern = grid_ref[depth]
    pattern = jnp.concatenate([pattern, pattern], axis=0).T
    make_bands(taps, nref, ny, picked_ref.at[FPD - 1], band_ref.at[FPD - 1])

    def start(plane):
        set_field(field_ref.at[plane], (pattern * wave_ref[plane : plane + 1]).astype(BF16).astype(F32))

    def keep(step, plane, new):
        source_ref[step, plane] = new

    run_steps(taps, depth, field_ref, band_ref, blend_ref, start, keep)


def migrate_kernel(dims, recv_ref, band_ref, blend_ref, source_ref, out_ref, grid_ref, field_ref, image_ref):
    groups, halves, copies, xw, taps, scale, folded = dims
    depth, nx, width = blend_ref.shape
    ny = width // 2
    if folded:
        folds = LANES // xw
        half_rows = ny // halves
        lane = lane_iota((SUB, LANES))
        blocks = [recv_ref[block].astype(F32) for block in range(groups * halves)]
    else:
        grid_ref[: recv_ref.shape[0]] = recv_ref[...].astype(F32)
    steps = [None] * depth

    def gather(plane):
        if folded:
            for half in range(halves):
                for item in range(2 * plane, 2 * plane + 2):
                    for low in range(folds):
                        kept = None
                        for group in range(groups):
                            piece = blocks[half * groups + group][item * SUB : (item + 1) * SUB]
                            shift = ((group - low) * xw) % LANES
                            if shift:
                                piece = pltpu.roll(piece, shift, 1)
                            kept = piece if kept is None else jnp.where(lane // xw == group, piece, kept)
                        grid_ref[pl.ds(item * ny + half * half_rows + low, SUB, stride=folds), :] = kept
        set_field(field_ref.at[plane], grid_ref[plane * width : (plane + 1) * width].T)

    def correlate(step, plane, new):
        term = source_ref[step, plane] * new
        steps[step] = term if steps[step] is None else steps[step] + term
        if plane == FPD - 1:
            turned = steps[step].T
            image_ref[pl.ds(step, ny, stride=depth), :] = (turned[:ny] + turned[ny:]) * scale

    run_steps(taps, depth, field_ref, band_ref, blend_ref, gather, correlate)
    share = ny // (groups * halves) * depth
    for group in range(groups):
        for half in range(halves):
            start = (half * groups + group) * share
            piece = image_ref[start : start + share].astype(BF16)
            for copy in range(copies):
                out_ref[(group * halves + half) * copies + copy] = piece


def vmem():
    return pl.BlockSpec(memory_space=pltpu.VMEM)


def hbm():
    return pl.BlockSpec(memory_space=pltpu.HBM)


def pinned(*arrays):
    return [pltpu.with_memory_space_constraint(array, pltpu.HBM) for array in arrays]


def from_halves(block, halves):
    blocks = [block]
    for turn in range(1, halves):
        blocks.append(lax.ppermute(block, "half", [((to + turn) % halves, to) for to in range(halves)]))
    return blocks


def body(records, source_pattern, wavelet, filters, vel_table, vel_index, freq_plan, counts):
    groups = lax.axis_size("freq")
    halves = lax.axis_size("half")
    copies = lax.axis_size("shot")
    shots, rows, xw, nt = records.shape
    depth = vel_index.shape[0]
    nref, _, taps, _, nbin = filters.shape
    nx = xw * groups
    ny = rows * halves
    items = 2 * FPD
    cap = freq_plan.shape[1]
    cells = rows * xw
    folded = LANES % xw == 0 and cells == SUB * LANES
    bins = pltpu.SMEM((groups * FPD + cap,), jnp.int32)
    params = pltpu.CompilerParams(vmem_limit_bytes=VMEM_BYTES)


    if folded:
        send_shape = (shots, groups, items * SUB, LANES)
    else:
        send_shape = (shots, groups * SUB, cells)
    table = filters.transpose(0, 2, 3, 1, 4)
    flat = records.reshape(shots, cells, nt)
    tmp = pltpu.VMEM((groups * SUB * SUB + SUB, LANES), F32)
    dft, own, wave, shared, early, last = pl.pallas_call(
        functools.partial(prepare_kernel, groups, folded),
        out_shape=[
            jax.ShapeDtypeStruct((groups * SUB, nt), BF16),
            jax.ShapeDtypeStruct((SUB, LANES), jnp.int32),
            jax.ShapeDtypeStruct((SUB, LANES), F32),
            jax.ShapeDtypeStruct((depth + shots, rows, nx), BF16),
            jax.ShapeDtypeStruct((shots - 1,) + send_shape[1:], BF16),
            jax.ShapeDtypeStruct((cells, nt), BF16),
        ],
        in_specs=[hbm()] * 6,
        out_specs=[vmem()] * 6,
        scratch_shapes=[
            pltpu.SMEM(freq_plan.shape, jnp.int32),
            pltpu.SMEM(counts.shape, jnp.int32),
            pltpu.SMEM((2, nbin), F32),
            pltpu.VMEM(vel_index.shape, jnp.int32),
            bins,
            pltpu.VMEM((shots - 1, cells, nt), BF16),
            tmp,
            pltpu.SemaphoreType.DMA((5 + shots,)),
        ],
        compiler_params=params,
        cost_estimate=pl.CostEstimate(flops=3 * 10**9, bytes_accessed=4 * 10**6, transcendentals=0),
        name="prepare",
    )(*pinned(freq_plan, counts, wavelet.T, vel_index, source_pattern, flat))
    others = from_halves(shared, halves)[1:]
    send = pl.pallas_call(
        functools.partial(send_kernel, groups, folded),
        out_shape=jax.ShapeDtypeStruct(send_shape, BF16),
        in_specs=[vmem()] * 3,
        out_specs=vmem(),
        scratch_shapes=[tmp],
        compiler_params=params,
        name="send_blocks",
    )(dft, early, last)
    if folded:
        send = send.reshape(groups * halves, items * SUB, LANES)
        recv = lax.all_to_all(send, ("half", "freq"), 0, 0, tiled=True)
    else:
        send = send.reshape(shots, groups, SUB, cells)[:, :, :items].swapaxes(0, 1)
        send = send.reshape(groups * halves, items, cells)
        recv = lax.all_to_all(send, ("freq", "half"), 0, 0, tiled=True)
        recv = recv.reshape(groups, halves, items, rows, xw).transpose(2, 1, 3, 0, 4).reshape(items * ny, nx)

    table = table.reshape(nref * taps * taps * 2, nbin)
    band_shape = (FPD, taps * 2 * ny, nref * 2 * ny)
    field = pltpu.VMEM((FPD, nx + 2 * ROW_PAD, 2 * ny), F32)
    band, blend, source = pl.pallas_call(
        functools.partial(source_kernel, taps, nref, depth, halves),
        out_shape=[
            jax.ShapeDtypeStruct(band_shape, BF16),
            jax.ShapeDtypeStruct((depth, nx, 2 * ny), F32),
            jax.ShapeDtypeStruct((depth, FPD, nx, 2 * ny), F32),
        ],
        in_specs=[vmem()] * 3 + [hbm()] * 2 + [pl.BlockSpec(memory_space=pl.ANY)] + [hbm()] * (halves - 1),
        out_specs=[vmem()] * 3,
        scratch_shapes=[
            pltpu.VMEM((1,) + vel_table.shape, F32),
            pltpu.VMEM(vel_index.shape, jnp.int32),
            pltpu.VMEM(source_pattern.shape, BF16),
            pltpu.VMEM((halves - 1,) + shared.shape, BF16),
            pltpu.VMEM((FPD, (table.shape[0] + 2 * taps + SUB) // SUB * SUB + 2 * SUB, LANES), F32),
            pltpu.VMEM((depth + 1, ny, nx), F32),
            pltpu.VMEM((SUB, LANES), F32),
            field,
            pltpu.SemaphoreType.DMA((2 + halves,)),
        ],
        compiler_params=params,
        cost_estimate=pl.CostEstimate(flops=4 * 10**9, bytes_accessed=10**7, transcendentals=0),
        name="source_fields",
    )(own, wave, table, *pinned(vel_table[None], vel_index), source_pattern, *pinned(*others))

    scale = 1.0 / math.sqrt(FPD * groups * shots * copies)
    share = ny // (groups * halves)
    terms = pl.pallas_call(
        functools.partial(migrate_kernel, (groups, halves, copies, xw, taps, scale, folded)),
        out_shape=jax.ShapeDtypeStruct((groups * halves * copies, share * depth, nx), BF16),
        in_specs=[vmem()] * 4,
        out_specs=vmem(),
        scratch_shapes=[
            pltpu.VMEM((items * ny + SUB, nx), F32),
            field,
            pltpu.VMEM((ny * depth + SUB, nx), F32),
        ],
        compiler_params=params,
        name="migrate",
    )(recv, band, blend, source)
    terms = lax.all_to_all(terms, ("freq", "half", "shot"), 0, 0, tiled=True)
    return jnp.sum(terms.astype(F32), axis=0).reshape(1, share, depth, nx)


def solution(mesh):
    return jax.shard_map(
        body,
        mesh=mesh,
        in_specs=(
            P(("group", "shot"), "half", "freq", None),
            P(("group", "shot"), "half", None),
            P(),
            P(),
            P(),
            P("group", "half", None),
            P(),
            P(),
        ),
        out_specs=P("half", "freq", "group", None),
        check_vma=False,
    )
```

```python
import functools
import math

import jax
import jax.numpy as jnp
from jax import lax
from jax.experimental import pallas as pl
from jax.experimental.pallas import tpu as pltpu
from jax.sharding import PartitionSpec as P

FPD = 3
LANES = 128
SUB = 8
ROW_PAD = 8
VMEM_BYTES = 40 * 1024 * 1024
BF16 = jnp.bfloat16
F32 = jnp.float32


def list_bins(plan_ref, counts_ref, bins_ref):
    groups, cap = plan_ref.shape
    start = jnp.int32(0)
    for holder in range(groups):
        for slot in range(cap):
            bins_ref[start + slot] = plan_ref[holder, slot]
        start = start + counts_ref[holder]


def lane_iota(shape):
    return lax.broadcasted_iota(jnp.int32, shape, len(shape) - 1)


def row_iota(shape):
    return lax.broadcasted_iota(jnp.int32, shape, 0)


def dft_rows(bins_ref, group, nt):
    shape = (SUB, nt)
    row = row_iota(shape)
    bin_id = jnp.zeros(shape, jnp.int32)
    for slot in range(FPD):
        bin_id = jnp.where(row // 2 == slot, bins_ref[group * FPD + slot], bin_id)
    phase = bin_id * lane_iota(shape)
    phase = lax.rem(phase, jnp.int32(nt)) if nt & (nt - 1) else phase & (nt - 1)
    quarter = nt // 4
    turn = (phase + quarter // 2) // quarter
    angle = (phase - turn * quarter).astype(F32) * (2.0 * math.pi / nt)
    turn = (turn + (row & 1)) & 3
    sq = angle * angle
    cos = 1.0 + sq * (-1.0 / 2 + sq * (1.0 / 24 + sq * (-1.0 / 720 + sq * (1.0 / 40320))))
    sin = angle * (1.0 + sq * (-1.0 / 6 + sq * (1.0 / 120 + sq * (-1.0 / 5040 + sq * (1.0 / 362880)))))
    value = jnp.where((turn & 1) == 1, sin, cos)
    value = jnp.where(((turn + 1) & 2) == 2, -value, value)
    return value * (1.0 / math.sqrt(nt))


def transform(dft, block):
    return lax.dot_general(dft, block, (((1,), (1,)), ((), ())), preferred_element_type=F32)


def prepare_kernel(
    groups, plan_hbm, counts_hbm, wav_hbm, class_hbm, pattern_hbm, dft_ref, own_ref, wave_ref, shared_ref,
    plan_ref, counts_ref, wav_ref, class_ref, bins_ref, sems,
):
    nt = dft_ref.shape[1]
    depth, shots = class_hbm.shape[0], pattern_hbm.shape[0]
    later = [
        pltpu.make_async_copy(class_hbm, class_ref, sems.at[3]),
        pltpu.make_async_copy(pattern_hbm, shared_ref.at[pl.ds(depth, shots)], sems.at[4]),
    ]
    small = [
        pltpu.make_async_copy(plan_hbm, plan_ref, sems.at[0]),
        pltpu.make_async_copy(counts_hbm, counts_ref, sems.at[1]),
        pltpu.make_async_copy(wav_hbm, wav_ref, sems.at[2]),
    ]
    for copy in small + later:
        copy.start()
    for copy in small:
        copy.wait()
    list_bins(plan_ref, counts_ref, bins_ref)
    for pair in range(0, groups, 2):
        both = [dft_rows(bins_ref, group, nt) for group in range(pair, min(pair + 2, groups))]
        dft_ref[pair * SUB : (pair + len(both)) * SUB] = jnp.concatenate(both, axis=0).astype(BF16)
    first = lax.axis_index("freq") * FPD
    lane = lane_iota((1, LANES))
    for plane in range(FPD):
        bin_id = bins_ref[first + plane]
        own_ref[plane : plane + 1] = jnp.full((1, LANES), bin_id, jnp.int32)
        wave_ref[plane : plane + 1] = jnp.where(lane < LANES // 2, wav_ref[0, bin_id], wav_ref[1, bin_id])
    for copy in later:
        copy.wait()
    shared_ref[:depth] = class_ref[...].astype(BF16)


def send_kernel(groups, folded, dft_ref, rec_ref, out_ref, tmp_ref):
    shots, cells, _ = rec_ref.shape
    dft = dft_ref[...]
    for shot in range(shots):
        out = transform(dft, rec_ref[shot])
        if not folded:
            out_ref[shot] = out.astype(BF16)
            continue
        for group in range(groups):
            base = (group * shots + shot) * SUB * SUB
            for high in range(SUB):
                tmp_ref[pl.ds(base + high, SUB, stride=SUB), :] = out[
                    group * SUB : (group + 1) * SUB, high * LANES : (high + 1) * LANES
                ]
            out_ref[shot, group] = tmp_ref[base : base + 2 * FPD * SUB].astype(BF16)


def make_bands(taps, nref, ny, picked_ref, band_ref):
    reach = taps // 2
    width = 2 * ny
    lane = lane_iota((taps, width))
    full_lane = lane_iota((ny, width))
    keep = jnp.abs((full_lane & (ny - 1)) - row_iota((ny, width))) <= reach
    sign = jnp.where((lane < ny // 2) | (lane >= ny + ny // 2), -1.0, 1.0)
    for ref in range(nref):
        base = jnp.zeros((taps, width), F32)
        for part in range(2):
            for tap in range(taps):
                value = picked_ref[pl.ds((ref * taps + tap) * taps * 2 + part, taps, stride=2), :]
                base = jnp.where(lane == (part * ny + reach - tap) % width, value, base)
        turned = pltpu.roll(base, ny, 1) * sign
        for col_tap in range(taps):
            for part, rows in enumerate((base, turned)):
                spread = jnp.broadcast_to(rows[col_tap : col_tap + 1], (ny, width))
                band = pltpu.roll(spread, 0, 1, stride=1, stride_axis=0)
                band = jnp.where(keep, band, 0.0).astype(BF16)
                at = col_tap * width + part * ny
                band_ref[at : at + ny, ref * width : (ref + 1) * width] = band


def set_field(field_ref, value):
    rows, width = value.shape
    field_ref[:ROW_PAD] = jnp.zeros((ROW_PAD, width), F32)
    field_ref[ROW_PAD : ROW_PAD + rows] = value
    field_ref[ROW_PAD + rows :] = jnp.zeros((ROW_PAD, width), F32)


def shifted(taps, field_ref):
    first = ROW_PAD - taps // 2
    rows = field_ref.shape[0] - 2 * ROW_PAD
    pieces = [field_ref[pl.ds(first + tap, rows), :].astype(BF16) for tap in range(taps)]
    return jnp.concatenate(pieces, axis=1)


def advance(left, band_ref, blend):
    width = blend.shape[1]
    both = jnp.dot(left, band_ref[...], preferred_element_type=F32)
    low, high = both[:, :width], both[:, width:]
    return (low + blend * (high - low)).astype(BF16).astype(F32)


def run_steps(taps, depth, field_ref, band_ref, blend_ref, prepare, use):
    rows = field_ref.shape[1] - 2 * ROW_PAD
    order = [(step, plane) for step in range(depth) for plane in range(FPD)]
    for plane in range(FPD):
        prepare(plane)
    left = shifted(taps, field_ref.at[0])
    for at, (step, plane) in enumerate(order):
        follow = None
        if at + 1 < len(order):
            after = order[at + 1][1]
            follow = shifted(taps, field_ref.at[after])
        new = advance(left, band_ref.at[plane], blend_ref[step])
        if step + 1 < depth:
            field_ref[plane, ROW_PAD : ROW_PAD + rows] = new
        use(step, plane, new)
        left = follow


def source_kernel(taps, nref, depth, halves, own_ref, wave_ref, filt_ref, table_hbm, class_hbm, pattern_hbm, *refs):
    others_hbm, refs = refs[: halves - 1], refs[halves - 1 :]
    (band_ref, blend_ref, source_ref, table_ref, class_ref, pattern_ref, others_ref,
     picked_ref, grid_ref, tab_ref, field_ref, sems) = refs
    copies = [
        pltpu.make_async_copy(table_hbm, table_ref, sems.at[0]),
        pltpu.make_async_copy(class_hbm, class_ref, sems.at[1]),
        pltpu.make_async_copy(pattern_hbm, pattern_ref, sems.at[2]),
    ]
    for turn in range(halves - 1):
        copies.append(pltpu.make_async_copy(others_hbm[turn], others_ref.at[turn], sems.at[3 + turn]))
    for copy in copies:
        copy.start()
    mine = lax.axis_index("half")
    rows = class_ref.shape[1]
    ny, nx = grid_ref.shape[1:]
    nbin = filt_ref.shape[1]
    for plane in range(FPD):
        hot = jnp.where(row_iota((nbin, LANES)) == own_ref[plane : plane + 1], 1.0, 0.0).astype(BF16)
        picked_ref[plane, : filt_ref.shape[0]] = jnp.dot(filt_ref[...], hot, preferred_element_type=F32)
    for plane in range(FPD - 1):
        make_bands(taps, nref, ny, picked_ref.at[plane], band_ref.at[plane])
    for copy in copies:
        copy.wait()
    for turn in range(halves):
        at = pl.ds(pl.multiple_of(lax.rem(mine + turn, halves) * rows, rows), rows)
        for step in range(depth):
            one = others_ref[turn - 1, step] if turn else class_ref[step]
            grid_ref[step, at, :] = one.astype(F32)
        one = others_ref[turn - 1, depth + mine] if turn else pattern_ref[mine]
        grid_ref[depth, at, :] = one.astype(F32)
    tab_ref[:, : table_ref.shape[1]] = jnp.broadcast_to(table_ref[...], (SUB, table_ref.shape[1]))
    for step in range(depth):
        pieces = []
        for row in range(0, ny, SUB):
            index = grid_ref[step, row : row + SUB].astype(jnp.int32)
            pieces.append(jnp.take_along_axis(tab_ref[...], index, axis=1))
        blend_ref[step] = jnp.concatenate(pieces + pieces, axis=0).T
    pattern = grid_ref[depth]
    pattern = jnp.concatenate([pattern, pattern], axis=0).T
    make_bands(taps, nref, ny, picked_ref.at[FPD - 1], band_ref.at[FPD - 1])

    def start(plane):
        set_field(field_ref.at[plane], (pattern * wave_ref[plane : plane + 1]).astype(BF16).astype(F32))

    def keep(step, plane, new):
        source_ref[step, plane] = new

    run_steps(taps, depth, field_ref, band_ref, blend_ref, start, keep)


def migrate_kernel(dims, recv_ref, band_ref, blend_ref, source_ref, out_ref, grid_ref, field_ref, image_ref):
    groups, halves, copies, xw, taps, scale, folded = dims
    depth, nx, width = blend_ref.shape
    ny = width // 2
    if folded:
        folds = LANES // xw
        half_rows = ny // halves
        lane = lane_iota((SUB, LANES))
        blocks = [recv_ref[block].astype(F32) for block in range(groups * halves)]
    else:
        grid_ref[: recv_ref.shape[0]] = recv_ref[...].astype(F32)
    steps = [None] * depth

    def gather(plane):
        if folded:
            for half in range(halves):
                for item in range(2 * plane, 2 * plane + 2):
                    for low in range(folds):
                        kept = None
                        for group in range(groups):
                            piece = blocks[half * groups + group][item * SUB : (item + 1) * SUB]
                            shift = ((group - low) * xw) % LANES
                            if shift:
                                piece = pltpu.roll(piece, shift, 1)
                            kept = piece if kept is None else jnp.where(lane // xw == group, piece, kept)
                        grid_ref[pl.ds(item * ny + half * half_rows + low, SUB, stride=folds), :] = kept
        set_field(field_ref.at[plane], grid_ref[plane * width : (plane + 1) * width].T)

    def correlate(step, plane, new):
        term = source_ref[step, plane] * new
        steps[step] = term if steps[step] is None else steps[step] + term
        if plane == FPD - 1:
            turned = steps[step].T
            image_ref[pl.ds(step, ny, stride=depth), :] = (turned[:ny] + turned[ny:]) * scale

    run_steps(taps, depth, field_ref, band_ref, blend_ref, gather, correlate)
    share = ny // (groups * halves) * depth
    for group in range(groups):
        for half in range(halves):
            start = (half * groups + group) * share
            piece = image_ref[start : start + share].astype(BF16)
            for copy in range(copies):
                out_ref[(group * halves + half) * copies + copy] = piece


def vmem():
    return pl.BlockSpec(memory_space=pltpu.VMEM)


def hbm():
    return pl.BlockSpec(memory_space=pltpu.HBM)


def pinned(*arrays):
    return [pltpu.with_memory_space_constraint(array, pltpu.HBM) for array in arrays]


def from_halves(block, halves):
    blocks = [block]
    for turn in range(1, halves):
        blocks.append(lax.ppermute(block, "half", [((to + turn) % halves, to) for to in range(halves)]))
    return blocks


def body(records, source_pattern, wavelet, filters, vel_table, vel_index, freq_plan, counts):
    groups = lax.axis_size("freq")
    halves = lax.axis_size("half")
    copies = lax.axis_size("shot")
    shots, rows, xw, nt = records.shape
    depth = vel_index.shape[0]
    nref, _, taps, _, nbin = filters.shape
    nx = xw * groups
    ny = rows * halves
    items = 2 * FPD
    cap = freq_plan.shape[1]
    cells = rows * xw
    folded = LANES % xw == 0 and cells == SUB * LANES
    bins = pltpu.SMEM((groups * FPD + cap,), jnp.int32)
    params = pltpu.CompilerParams(vmem_limit_bytes=VMEM_BYTES)


    if folded:
        send_shape = (shots, groups, items * SUB, LANES)
    else:
        send_shape = (shots, groups * SUB, cells)
    table = filters.transpose(0, 2, 3, 1, 4)
    dft, own, wave, shared = pl.pallas_call(
        functools.partial(prepare_kernel, groups),
        out_shape=[
            jax.ShapeDtypeStruct((groups * SUB, nt), BF16),
            jax.ShapeDtypeStruct((SUB, LANES), jnp.int32),
            jax.ShapeDtypeStruct((SUB, LANES), F32),
            jax.ShapeDtypeStruct((depth + shots, rows, nx), BF16),
        ],
        in_specs=[hbm()] * 5,
        out_specs=[vmem()] * 4,
        scratch_shapes=[
            pltpu.SMEM(freq_plan.shape, jnp.int32),
            pltpu.SMEM(counts.shape, jnp.int32),
            pltpu.SMEM((2, nbin), F32),
            pltpu.VMEM(vel_index.shape, jnp.int32),
            bins,
            pltpu.SemaphoreType.DMA((5,)),
        ],
        compiler_params=params,
        cost_estimate=pl.CostEstimate(flops=3 * 10**9, bytes_accessed=4 * 10**6, transcendentals=0),
        name="prepare",
    )(*pinned(freq_plan, counts, wavelet.T, vel_index, source_pattern))
    others = from_halves(shared, halves)[1:]
    send = pl.pallas_call(
        functools.partial(send_kernel, groups, folded),
        out_shape=jax.ShapeDtypeStruct(send_shape, BF16),
        in_specs=[vmem()] * 2,
        out_specs=vmem(),
        scratch_shapes=[pltpu.VMEM((groups * shots * SUB * SUB + SUB, LANES), F32)],
        compiler_params=params,
        name="send_blocks",
    )(dft, records.reshape(shots, cells, nt))
    if folded:
        send = send.reshape(groups * halves, items * SUB, LANES)
        recv = lax.all_to_all(send, ("half", "freq"), 0, 0, tiled=True)
    else:
        send = send.reshape(shots, groups, SUB, cells)[:, :, :items].swapaxes(0, 1)
        send = send.reshape(groups * halves, items, cells)
        recv = lax.all_to_all(send, ("freq", "half"), 0, 0, tiled=True)
        recv = recv.reshape(groups, halves, items, rows, xw).transpose(2, 1, 3, 0, 4).reshape(items * ny, nx)

    table = table.reshape(nref * taps * taps * 2, nbin)
    band_shape = (FPD, taps * 2 * ny, nref * 2 * ny)
    field = pltpu.VMEM((FPD, nx + 2 * ROW_PAD, 2 * ny), F32)
    band, blend, source = pl.pallas_call(
        functools.partial(source_kernel, taps, nref, depth, halves),
        out_shape=[
            jax.ShapeDtypeStruct(band_shape, BF16),
            jax.ShapeDtypeStruct((depth, nx, 2 * ny), F32),
            jax.ShapeDtypeStruct((depth, FPD, nx, 2 * ny), F32),
        ],
        in_specs=[vmem()] * 3 + [hbm()] * 2 + [pl.BlockSpec(memory_space=pl.ANY)] + [hbm()] * (halves - 1),
        out_specs=[vmem()] * 3,
        scratch_shapes=[
            pltpu.VMEM((1,) + vel_table.shape, F32),
            pltpu.VMEM(vel_index.shape, jnp.int32),
            pltpu.VMEM(source_pattern.shape, BF16),
            pltpu.VMEM((halves - 1,) + shared.shape, BF16),
            pltpu.VMEM((FPD, (table.shape[0] + 2 * taps + SUB) // SUB * SUB + 2 * SUB, LANES), F32),
            pltpu.VMEM((depth + 1, ny, nx), F32),
            pltpu.VMEM((SUB, LANES), F32),
            field,
            pltpu.SemaphoreType.DMA((2 + halves,)),
        ],
        compiler_params=params,
        cost_estimate=pl.CostEstimate(flops=4 * 10**9, bytes_accessed=10**7, transcendentals=0),
        name="source_fields",
    )(own, wave, table, *pinned(vel_table[None], vel_index), source_pattern, *pinned(*others))

    scale = 1.0 / math.sqrt(FPD * groups * shots * copies)
    share = ny // (groups * halves)
    terms = pl.pallas_call(
        functools.partial(migrate_kernel, (groups, halves, copies, xw, taps, scale, folded)),
        out_shape=jax.ShapeDtypeStruct((groups * halves * copies, share * depth, nx), BF16),
        in_specs=[vmem()] * 4,
        out_specs=vmem(),
        scratch_shapes=[
            pltpu.VMEM((items * ny + SUB, nx), F32),
            field,
            pltpu.VMEM((ny * depth + SUB, nx), F32),
        ],
        compiler_params=params,
        name="migrate",
    )(recv, band, blend, source)
    terms = lax.all_to_all(terms, ("freq", "half", "shot"), 0, 0, tiled=True)
    return jnp.sum(terms.astype(F32), axis=0).reshape(1, share, depth, nx)


def solution(mesh):
    return jax.shard_map(
        body,
        mesh=mesh,
        in_specs=(
            P(("group", "shot"), "half", "freq", None),
            P(("group", "shot"), "half", None),
            P(),
            P(),
            P(),
            P("group", "half", None),
            P(),
            P(),
        ),
        out_specs=P("half", "freq", "group", None),
        check_vma=False,
    )
```
